128 devices in a mesh: seq: 8 (over y, core), tensor: 16 (over z, x).
Axes of the slice: x: 4, y: 4, z: 4, core: 2. Of those that a mesh axis runs over, the one named last changes fastest.
Arguments:
- hidden: bfloat16 [4096, 4096], P('seq', 'tensor'), may hold values from -40 to 40
- encoded: bfloat16 [64, 128, 4096], P('seq', None, 'tensor'), may hold values from -6 to 6
- w_query: bfloat16 [4096, 4096], P(None, 'tensor'), may hold values from -0.375 to 0.375
- w_key: bfloat16 [4096, 4096], P(None, 'tensor'), may hold values from -0.09375 to 0.09375
- w_value: bfloat16 [4096, 4096], P(None, 'tensor'), may hold values from -0.09375 to 0.09375
- w_out: bfloat16 [4096, 4096], P('tensor'), may hold values from -0.1875 to 0.1875
- send_rows: int32 [8, 16], P('seq'), may hold values from -1 to 7, as said below
- read_slot: int32 [64, 2], P('seq'), may hold values from 0 to 15, as said below
- grad_out: bfloat16 [4096, 4096], P('seq', 'tensor'), may hold values from -6 to 6
Outputs:
- out: bfloat16 [4096, 4096], P('seq', 'tensor')
- grad_hidden: bfloat16 [4096, 4096], P('seq', 'tensor')
- grad_encoded: bfloat16 [64, 128, 4096], P('seq', None, 'tensor')
The draws below stay inside these ranges and needn't reach their ends.
Inputs may be any that keep to these rules, and one draw needn't show every extreme that they name: `send_rows`: for every owner and reading device the live slots come first, one to 2 of them, naming distinct local rows; padded slots hold -1. Some pairs have 2 live slots and some have one. `read_slot`: every entry names a live slot of the reading device; every live slot of a reading device is named by some span of that device.
All inputs are finite; a program needn't handle non-finite values.
Results may differ from the reference program's by a relative error of at most 0.029.
The reference program's roundings to bfloat16 on the way count: a program that leaves them out, or rounds other values in their place, can miss the bound.
Values may be sent and summed in bfloat16 or wider, within the bound.
A program may use at most 128 MiB of HBM per device.

```python
import jax
import jax.numpy as jnp
from jax import lax

D = 4096
HEADS = 32
SPAN = 64
NEIGH = 2
RLEN = 128
SLOTS = 2
NB_DEV = 8
HEAD_DIM = 128
TOKENS = 4096
SPANS_DEV = 8
SPANS = 64
NB_TOTAL = 64
N_SEQ = 8
N_TENSOR = 16


def routing(key):
    count_key, perm_key = jax.random.split(jax.random.fold_in(key, 17), 2)
    owner_ids = jnp.arange(N_SEQ, dtype=jnp.int32)
    pair_counts = jax.random.randint(count_key, (N_SEQ, N_SEQ), 1, SLOTS + 1)
    full_pair = (owner_ids[:, None] + 1) % N_SEQ == owner_ids[None, :]
    single_pair = owner_ids[:, None] == owner_ids[None, :]
    pair_counts = jnp.where(single_pair, 1, jnp.where(full_pair, SLOTS, pair_counts))
    pair_keys = jax.random.split(perm_key, N_SEQ * N_SEQ)
    shuffled = jax.vmap(lambda inner: jax.random.permutation(inner, NB_DEV))(pair_keys)
    shuffled = shuffled.reshape(N_SEQ, N_SEQ, NB_DEV).astype(jnp.int32)
    last_row = NB_DEV - 1
    swapped = jnp.where(shuffled == last_row, shuffled[:, :, :1], shuffled)
    forced = swapped.at[:, :, 0].set(last_row)
    shuffled = jnp.where(full_pair[:, :, None], forced, shuffled)[:, :, :SLOTS]
    live_slots = jnp.arange(SLOTS, dtype=jnp.int32)[None, None, :] < pair_counts[:, :, None]
    send_table = jnp.where(live_slots, shuffled, -1).astype(jnp.int32)
    return (send_table, live_slots)


def draw_send_rows(key, part):
    send_table, live_slots = routing(key)
    return send_table.reshape(N_SEQ, N_SEQ * SLOTS)


def draw_read_slot(key, part):
    send_table, live_slots = routing(key)
    key = jax.random.fold_in(key, 7)
    read_count = SPANS_DEV * NEIGH

    def reader(reader_index, reader_key):
        live_mask = jnp.take(live_slots, reader_index, axis=1).reshape(N_SEQ * SLOTS)
        ranked = jnp.argsort(jnp.where(live_mask, 0, 1).astype(jnp.int32), stable=True).astype(jnp.int32)
        live_count = jnp.sum(live_mask.astype(jnp.int32))
        pick_key, mix_key = jax.random.split(reader_key)
        spare_pick = jax.random.randint(pick_key, (read_count,), 0, live_count)
        position = jnp.arange(read_count, dtype=jnp.int32)
        picked = jnp.where(position < live_count, position, spare_pick)
        chosen_slots = jax.random.permutation(mix_key, ranked[picked])
        return chosen_slots.reshape(SPANS_DEV, NEIGH)
    reader_keys = jax.random.split(key, N_SEQ)
    result = jax.vmap(reader)(jnp.arange(N_SEQ, dtype=jnp.int32), reader_keys)
    return result.reshape(N_SEQ * SPANS_DEV, NEIGH).astype(jnp.int32)


def draw_hidden(key, part):
    key = jax.random.fold_in(key, 3)
    base_key = jax.random.fold_in(key, 0)
    return jnp.clip(jax.random.normal(base_key, (TOKENS, D), jnp.float32), -6.0, 6.0).astype(jnp.bfloat16)


def block_scale(rng, dims, cuts, low, high):
    factor_of = 1.0
    for axis_at, blocks in cuts:
        heights = jax.random.uniform(jax.random.fold_in(jax.random.fold_in(rng, 6), axis_at), (blocks,), jnp.float32, low / len(cuts), high / len(cuts))
        factor_of = factor_of * jnp.repeat(jnp.exp(heights), dims[axis_at] // blocks).reshape((-1,) + (1,) * (len(dims) - 1 - axis_at))
    return factor_of


def bell_draw(key, shape, scale, limit, pieces=(), kind=jnp.bfloat16):
    loudness = block_scale(key, shape, pieces, -0.22, 0.18) if pieces else 1.0
    values = jax.random.normal(key, shape, jnp.float32) * scale * loudness
    return jnp.minimum(jnp.maximum(values, -limit), limit).astype(kind)


def setup_inputs(seed: int = 0) -> dict:
    splits = jax.random.split(jax.random.key(seed), 10)
    return {
        "hidden": draw_hidden(jax.random.fold_in(splits[9], 71), 0),
        "encoded": bell_draw(splits[1], (NB_TOTAL, RLEN, D), 1.0, 6.0, ((0, 8), (2, 16))),
        "w_query": bell_draw(splits[2], (D, D), (D // 16) ** -0.5, 0.375, ((1, 16),)),
        "w_key": bell_draw(splits[3], (D, D), D ** -0.5, 0.09375, ((1, 16),)),
        "w_value": bell_draw(splits[4], (D, D), D ** -0.5, 0.09375, ((1, 16),)),
        "w_out": bell_draw(splits[5], (D, D), (D // 4) ** -0.5, 0.1875, ((0, 16),)),
        "send_rows": draw_send_rows(jax.random.fold_in(splits[9], 71), 0),
        "read_slot": draw_read_slot(jax.random.fold_in(splits[9], 71), 0),
        "grad_out": bell_draw(splits[8], (TOKENS, D), 1.0, 6.0, ((0, 8), (1, 16))),
    }


def grouped_product(lefts, rights):
    width = lefts[0].shape[1] // N_TENSOR

    def step(total, group):
        term = jnp.zeros((lefts[0].shape[0], rights[0].shape[1]), jnp.float32)
        for left, right in zip(lefts, rights):
            part_left = lax.dynamic_slice_in_dim(left, group * width, width, 1)
            part_right = lax.dynamic_slice_in_dim(right, group * width, width, 0)
            term = term + jnp.dot(part_left, part_right, preferred_element_type=jnp.float32)
        rounded = lax.optimization_barrier(term.astype(jnp.bfloat16))
        return total + rounded.astype(jnp.float32), None

    start = jnp.zeros((lefts[0].shape[0], rights[0].shape[1]), jnp.float32)
    total, _ = lax.scan(step, start, jnp.arange(N_TENSOR, dtype=jnp.int32))
    return total.astype(jnp.bfloat16)


def reader_sums(read_grads, neighbour):
    grads = read_grads.reshape(N_SEQ, SPANS_DEV * NEIGH, RLEN, D)
    owners = neighbour.reshape(N_SEQ, SPANS_DEV * NEIGH)
    targets = jnp.arange(NB_TOTAL, dtype=jnp.int32)

    def step(total, pair):
        grad_rows, ids = pair
        onehot = (ids[None, :] == targets[:, None]).astype(jnp.float32)
        term = jnp.einsum("nr,rtd->ntd", onehot, grad_rows, precision=lax.Precision.HIGHEST)
        rounded = lax.optimization_barrier(term.astype(jnp.bfloat16))
        return total + rounded.astype(jnp.float32), None

    total, _ = lax.scan(step, jnp.zeros((NB_TOTAL, RLEN, D), jnp.float32), (grads, owners))
    return total.astype(jnp.bfloat16)


def reference(hidden, encoded, w_query, w_key, w_value, w_out, send_rows, read_slot, grad_out):
    scale = HEAD_DIM ** -0.5
    offset_rows = SPAN - 1
    queries = jnp.dot(hidden, w_query, preferred_element_type=jnp.float32).astype(jnp.bfloat16)
    flat_enc = encoded.reshape(NB_TOTAL * RLEN, D)
    keys = jnp.dot(flat_enc, w_key, preferred_element_type=jnp.float32).astype(jnp.bfloat16).reshape(NB_TOTAL, RLEN, D)
    values = jnp.dot(flat_enc, w_value, preferred_element_type=jnp.float32).astype(jnp.bfloat16).reshape(NB_TOTAL, RLEN, D)
    reader = (jnp.arange(SPANS, dtype=jnp.int32) // SPANS_DEV)[:, None]
    owner = read_slot // SLOTS
    within = read_slot % SLOTS
    table = send_rows.reshape(N_SEQ, N_SEQ, SLOTS)
    neighbour = (owner * NB_DEV + table[owner, reader, within]).astype(jnp.int32)
    span_keys = keys[neighbour].reshape(SPANS, NEIGH * RLEN, HEADS, HEAD_DIM).astype(jnp.float32)
    span_values = values[neighbour].reshape(SPANS, NEIGH * RLEN, HEADS, HEAD_DIM).astype(jnp.float32)
    tail = jnp.zeros((offset_rows, D), jnp.bfloat16)
    attached = jnp.concatenate([queries[offset_rows:], tail], 0).reshape(SPANS, SPAN, HEADS, HEAD_DIM).astype(jnp.float32)
    scores = jnp.einsum("cqhd,ckhd->chqk", attached, span_keys) * scale
    peak = jnp.max(scores, axis=-1, keepdims=True)
    weights = jnp.exp(scores - peak)
    probs = weights / jnp.sum(weights, axis=-1, keepdims=True)
    probs_low = probs.astype(jnp.bfloat16).astype(jnp.float32)
    context = jnp.einsum("chqk,ckhd->cqhd", probs_low, span_values).astype(jnp.bfloat16).reshape(TOKENS, D)
    attended = jnp.concatenate([tail, context[:TOKENS - offset_rows]], 0)
    out = grouped_product((attended,), (w_out,))
    grad_attended = jnp.dot(grad_out, w_out.T, preferred_element_type=jnp.float32).astype(jnp.bfloat16)
    grad_context = jnp.concatenate([grad_attended[offset_rows:], tail], 0).reshape(SPANS, SPAN, HEADS, HEAD_DIM).astype(jnp.float32)
    grad_probs = jnp.einsum("cqhd,ckhd->chqk", grad_context, span_values)
    grad_values_read = jnp.einsum("chqk,cqhd->ckhd", probs_low, grad_context)
    grad_scores = probs * (grad_probs - jnp.sum(grad_probs * probs, axis=-1, keepdims=True))
    grad_scaled = (grad_scores * scale).astype(jnp.bfloat16).astype(jnp.float32)
    grad_blocks = jnp.einsum("chqk,ckhd->cqhd", grad_scaled, span_keys).astype(jnp.bfloat16).reshape(TOKENS, D)
    grad_queries = jnp.concatenate([tail, grad_blocks[:TOKENS - offset_rows]], 0)
    grad_keys_read = jnp.einsum("chqk,cqhd->ckhd", grad_scaled, attached)
    grad_keys_total = reader_sums(grad_keys_read, neighbour)
    grad_values_total = reader_sums(grad_values_read, neighbour)
    grad_encoded = grouped_product(
        (grad_keys_total.reshape(NB_TOTAL * RLEN, D), grad_values_total.reshape(NB_TOTAL * RLEN, D)),
        (w_key.T, w_value.T)).reshape(NB_TOTAL, RLEN, D)
    grad_hidden = grouped_product((grad_queries,), (w_query.T,))
    return out, grad_hidden, grad_encoded
```

```python
import functools

import jax
import jax.numpy as jnp
from jax import lax
from jax.experimental import pallas as pl
from jax.experimental.pallas import tpu as pltpu
from jax.sharding import PartitionSpec as P

SPAN = 64
NEIGH = 2
RLEN = 128
HEAD_DIM = 128
NSEQ = 8
SIDE = 4
NT = SIDE * SIDE
W = 256
ROWS = 512
MESH = pl.DeviceIdType.MESH
ANY = pl.BlockSpec(memory_space=pl.ANY)
VM = pl.BlockSpec(memory_space=pltpu.VMEM)
SM = pl.BlockSpec(memory_space=pltpu.SMEM)
F32 = jnp.float32
BF16 = jnp.bfloat16
NT_DIMS = (((1,), (1,)), ((), ()))
TN_DIMS = (((0,), (0,)), ((), ()))


def wrap(value, count):
    return lax.rem(value + count, count)


class Grid:
    def __init__(self):
        self.seq = lax.axis_index("seq")
        tensor = lax.axis_index("tensor")
        self.z = lax.div(tensor, SIDE)
        self.x = lax.rem(tensor, SIDE)

    def first(self, order):
        return self.z if order == "zx" else self.x

    def second(self, order):
        return self.x if order == "zx" else self.z

    def block(self, order, b, a):
        return a * SIDE + b if order == "zx" else b * SIDE + a

    def along_first(self, order, step):
        a = wrap(self.first(order) + step, SIDE)
        return {"tensor": self.block(order, self.second(order), a)}

    def along_second(self, order, step):
        b = wrap(self.second(order) + step, SIDE)
        return {"tensor": self.block(order, b, self.first(order))}

    def along_seq(self, step):
        return {"seq": wrap(self.seq + step, NSEQ)}

    def barrier(self):
        sem = pltpu.get_barrier_semaphore()
        peers = [self.along_first("zx", 1), self.along_first("zx", -1)]
        peers += [self.along_second("zx", 1), self.along_second("zx", -1)]
        peers += [self.along_seq(k) for k in range(1, NSEQ)]
        for peer in peers:
            pl.semaphore_signal(sem, inc=1, device_id=peer, device_id_type=MESH)
        pl.semaphore_wait(sem, len(peers))


class Messages:
    def __init__(self, send, recv):
        self.send, self.recv, self.sent = send, recv, []

    def start(self, m, src, dst, peer):
        copy = pltpu.make_async_remote_copy(
            src_ref=src,
            dst_ref=dst,
            send_sem=self.send.at[m],
            recv_sem=self.recv.at[m],
            device_id=peer,
            device_id_type=MESH,
        )
        copy.start()
        self.sent.append(copy)

    def wait(self, m, dst):
        pltpu.make_async_copy(dst, dst, self.recv.at[m]).wait()

    def finish(self):
        for copy in self.sent:
            copy.wait_send()
        self.sent = []


class Gather:
    def __init__(self, grid, order, own, buf, send, recv):
        self.g, self.order, self.own, self.buf = grid, order, own, buf
        self.msg = Messages(send, recv)
        self.a, self.b = grid.first(order), grid.second(order)

    def slot(self, db, da):
        return self.buf.at[wrap(self.b + db, SIDE), wrap(self.a + da, SIDE)]

    def second(self, da, src=None):
        src = self.slot(0, da) if src is None else src
        for i, step in enumerate((1, -1)):
            peer = self.g.along_second(self.order, step)
            self.msg.start(4 + 2 * da + i, src, self.slot(0, da), peer)

    def start_first(self):
        for i, step in enumerate((1, -1)):
            peer = self.g.along_first(self.order, step)
            self.msg.start(i, self.own, self.slot(0, 0), peer)

    def start_second(self):
        self.second(0, self.own)

    def stage1(self):
        half = ROWS // 2
        low, high = pl.ds(0, half), pl.ds(half, half)
        self.msg.wait(0, self.slot(0, 3))
        part = self.slot(0, 3).at[low]
        self.msg.start(2, part, part, self.g.along_first(self.order, 1))
        self.second(3)
        self.msg.wait(1, self.slot(0, 1))
        part = self.slot(0, 1).at[high]
        self.msg.start(3, part, part, self.g.along_first(self.order, -1))
        self.second(1)

    def stage2(self):
        self.msg.wait(4, self.slot(3, 0))
        self.msg.start(12, self.slot(3, 0), self.slot(3, 0), self.g.along_second(self.order, 1))
        self.msg.wait(5, self.slot(1, 0))

    def stage3(self):
        half = ROWS // 2
        self.msg.wait(2, self.slot(0, 2).at[pl.ds(0, half)])
        self.msg.wait(3, self.slot(0, 2).at[pl.ds(half, half)])
        self.second(2)

    def stage4(self):
        self.msg.wait(4 + 6, self.slot(3, 3))
        self.msg.wait(5 + 6, self.slot(1, 3))
        self.msg.start(14, self.slot(1, 3), self.slot(1, 3), self.g.along_second(self.order, -1))
        self.msg.wait(4 + 2, self.slot(3, 1))
        self.msg.start(13, self.slot(3, 1), self.slot(3, 1), self.g.along_second(self.order, 1))
        self.msg.wait(5 + 2, self.slot(1, 1))

    def stage5(self):
        self.msg.wait(4 + 4, self.slot(3, 2))
        self.msg.wait(5 + 4, self.slot(1, 2))
        self.msg.start(15, self.slot(1, 2), self.slot(1, 2), self.g.along_second(self.order, -1))

    def stage6(self):
        for m, da in ((12, 0), (13, 1), (14, 3), (15, 2)):
            self.msg.wait(m, self.slot(2, da))

    def consume(self, db, use):
        b = wrap(self.b + db, SIDE)

        @pl.loop(0, SIDE)
        def _(a):
            use(self.buf.at[b, a], self.g.block(self.order, b, a))


def gather_kernel(
    enc_ref, hid_ref, gout_ref, wq_ref, wk_ref, wv_ref, wo_ref, rows_ref,
    q_ref, ga_ref, kv_ref,
    enc_lo, enc_hi, hid_all, gout_all, wq, wk, wv, wo, acc_k, acc_v, own_kv, stage, q_low, ga_low,
    send, recv, seq_send, seq_recv, edge_send, edge_recv, local,
):
    g = Grid()
    local_copies = [
        pltpu.make_async_copy(src, dst, local.at[i])
        for i, (src, dst) in enumerate(
            ((wk_ref, wk), (wv_ref, wv), (wq_ref, wq), (wo_ref, wo))
        )
    ]
    lo, hi = enc_ref.at[pl.ds(0, ROWS)], enc_ref.at[pl.ds(ROWS, ROWS)]
    streams = []
    for i, (order, own, buf) in enumerate(
        (("zx", lo, enc_lo), ("xz", hi, enc_hi), ("zx", hid_ref, hid_all), ("xz", gout_ref, gout_all))
    ):
        stream = Gather(g, order, own, buf, send.at[i], recv.at[i])
        streams.append(stream)
        local_copies.append(pltpu.make_async_copy(own, stream.slot(0, 0), local.at[4 + i]))
    enc, act = streams[:2], streams[2:]
    g.barrier()
    for s in enc:
        s.start_first()
    for s in enc:
        s.start_second()
    for copy in local_copies:
        copy.start()
    acc_k[...] = jnp.zeros_like(acc_k)
    acc_v[...] = jnp.zeros_like(acc_v)
    for s in enc:
        s.stage1()
    for s in enc:
        s.stage2()
    for s in enc:
        s.stage3()
    for s in act:
        s.start_first()
    for s in act:
        s.start_second()
    for copy in local_copies:
        copy.wait()

    def keys_values(i):
        def use(block, t):
            depth = pl.ds(pl.multiple_of(t * W, W), W)
            acc_k[i] += jnp.dot(block[...], wk[depth, :], preferred_element_type=F32)
            acc_v[i] += jnp.dot(block[...], wv[depth, :], preferred_element_type=F32)

        return use

    for i, s in enumerate(enc):
        s.consume(0, keys_values(i))
    for s in enc:
        s.stage4()
    for s in enc:
        s.stage5()
    for i, s in enumerate(enc):
        s.consume(3, keys_values(i))
        s.consume(1, keys_values(i))
    for s in act:
        s.stage1()
    for s in enc:
        s.stage6()
    for i, s in enumerate(enc):
        s.consume(2, keys_values(i))
    per_half = ROWS // RLEN
    for n in range(2 * per_half):
        rows = pl.ds((n % per_half) * RLEN, RLEN)
        own_kv[n, 0] = acc_k[n // per_half, rows, :].astype(BF16)
        own_kv[n, 1] = acc_v[n // per_half, rows, :].astype(BF16)

    @pl.loop(0, NSEQ)
    def _(r):
        for s in range(2):
            stage[r, s] = own_kv[jnp.maximum(rows_ref[0, 2 * r + s], 0)]

    seq_msg = Messages(seq_send, seq_recv)
    for k in range(1, NSEQ):
        peer = wrap(g.seq + k, NSEQ)
        seq_msg.start(k, stage.at[peer], kv_ref.at[g.seq], {"seq": peer})
    keep = pltpu.make_async_copy(stage.at[g.seq], kv_ref.at[g.seq], local.at[8])
    keep.start()

    acc_k[...] = jnp.zeros_like(acc_k)
    for s in act:
        s.stage2()
    for s in act:
        s.stage3()

    def queries(block, t):
        depth = pl.ds(pl.multiple_of(t * W, W), W)
        acc_k[0] += jnp.dot(block[...], wq[depth, :], preferred_element_type=F32)

    def grads(block, t):
        depth = pl.ds(pl.multiple_of(t * W, W), W)
        acc_k[1] += lax.dot_general(
            block[...], wo[:, depth], NT_DIMS, preferred_element_type=F32
        )

    uses = (queries, grads)
    for i, s in enumerate(act):
        s.consume(0, uses[i])
    for s in act:
        s.stage4()
    for s in act:
        s.stage5()
    for i, s in enumerate(act):
        s.consume(3, uses[i])
        s.consume(1, uses[i])
    for s in act:
        s.stage6()
    for i, s in enumerate(act):
        s.consume(2, uses[i])
    q_low[...] = acc_k[0].astype(BF16)
    ga_low[...] = acc_k[1].astype(BF16)
    edge = Messages(edge_send, edge_recv)
    head, tail, body = pl.ds(0, SPAN), pl.ds(ROWS, SPAN), pl.ds(0, ROWS)
    edge.start(0, q_low.at[head], q_ref.at[tail], g.along_seq(-1))
    edge.start(1, ga_low.at[head], ga_ref.at[tail], g.along_seq(-1))
    out_copies = [
        pltpu.make_async_copy(q_low, q_ref.at[body], local.at[0]),
        pltpu.make_async_copy(ga_low, ga_ref.at[body], local.at[1]),
    ]
    for copy in out_copies:
        copy.start()
    for s in streams:
        s.msg.finish()
    seq_msg.finish()
    edge.finish()
    for copy in out_copies:
        copy.wait()
    keep.wait()
    for k in range(1, NSEQ):
        seq_msg.wait(k, kv_ref.at[wrap(g.seq - k, NSEQ)])
    edge.wait(0, q_ref.at[tail])
    edge.wait(1, ga_ref.at[tail])


def attention_kernel(slot_ref, q_ref, ga_ref, kv_ref, att_ref, gq_ref, sums_ref, sums):
    spans = ROWS // SPAN
    scale = HEAD_DIM ** (-0.5)
    last = lax.axis_index("seq") == NSEQ - 1
    row = lax.broadcasted_iota(jnp.int32, (SPAN, 2 * SPAN), 0)
    col = lax.broadcasted_iota(jnp.int32, (SPAN, 2 * SPAN), 1)
    picked = col == row + (SPAN - 1)
    sums[...] = jnp.zeros_like(sums)

    @pl.loop(0, spans)
    def _(u):
        rows = pl.ds(pl.multiple_of(u * SPAN, SPAN), 2 * SPAN)
        inside = jnp.logical_or(col < SPAN, jnp.logical_not(last & (u == spans - 1)))
        shift = jnp.logical_and(picked, inside).astype(BF16)
        q_all = jnp.dot(shift, q_ref[rows, :], preferred_element_type=F32).astype(BF16)
        g_all = jnp.dot(shift, ga_ref[rows, :], preferred_element_type=F32).astype(BF16)
        slots = [slot_ref[u, j] for j in range(NEIGH)]
        for h in range(W // HEAD_DIM):
            cols = slice(h * HEAD_DIM, (h + 1) * HEAD_DIM)
            q, gr = q_all[:, cols], g_all[:, cols]
            k = jnp.concatenate([kv_ref[s, 0, :, cols] for s in slots], 0)
            v = jnp.concatenate([kv_ref[s, 1, :, cols] for s in slots], 0)
            scores = lax.dot_general(q, k, NT_DIMS, preferred_element_type=F32) * scale
            peak = jnp.max(scores, axis=-1, keepdims=True)
            weights = jnp.exp(scores - peak)
            probs = weights / jnp.sum(weights, axis=-1, keepdims=True)
            probs_low = probs.astype(BF16)
            context = jnp.dot(probs_low, v, preferred_element_type=F32)
            grad_probs = lax.dot_general(gr, v, NT_DIMS, preferred_element_type=F32)
            dot_sum = jnp.sum(grad_probs * probs, axis=-1, keepdims=True)
            grad_scores = (probs * (grad_probs - dot_sum) * scale).astype(BF16)
            grad_q = jnp.dot(grad_scores, k, preferred_element_type=F32)
            grad_k = lax.dot_general(grad_scores, q, TN_DIMS, preferred_element_type=F32)
            grad_v = lax.dot_general(probs_low, gr, TN_DIMS, preferred_element_type=F32)
            here = pl.ds(pl.multiple_of(u * SPAN, SPAN), SPAN)
            att_ref[here, cols] = context.astype(BF16)
            gq_ref[here, cols] = grad_q.astype(BF16)
            for j, s in enumerate(slots):
                part = slice(j * RLEN, (j + 1) * RLEN)
                sums[s, 0, :, cols] += grad_k[part]
                sums[s, 1, :, cols] += grad_v[part]

    @pl.loop(0, sums.shape[0])
    def _(s):
        sums_ref[s] = sums[s].astype(BF16)


class Scatter:
    def __init__(self, grid, order, parts, one, two, three, four, send, recv):
        self.g, self.order, self.parts = grid, order, parts
        self.one, self.two, self.three, self.four = one, two, three, four
        self.msg = Messages(send, recv)
        self.a, self.b = grid.first(order), grid.second(order)

    def part(self, db, da):
        return self.parts.at[wrap(self.b + db, SIDE), wrap(self.a + da, SIDE)]

    def fill(self, db, make):
        b = wrap(self.b + db, SIDE)

        @pl.loop(0, SIDE)
        def _(a):
            self.parts[b, a] = make(self.g.block(self.order, b, a)).astype(BF16)

    def far(self):
        minus, plus = self.g.along_second(self.order, -1), self.g.along_second(self.order, 1)
        self.msg.start(0, self.part(2, 2), self.one.at[0], minus)
        self.msg.start(1, self.part(2, 1), self.one.at[1], plus)
        self.msg.start(2, self.part(2, 0), self.one.at[2], minus)
        self.msg.start(3, self.part(2, 3), self.one.at[3], plus)

    def near_own(self):
        minus, plus = self.g.along_second(self.order, -1), self.g.along_second(self.order, 1)
        self.msg.start(4 + 2, self.part(1, 2), self.two.at[0, 2], plus)
        self.msg.start(8 + 1, self.part(3, 1), self.two.at[1, 1], minus)
        self.msg.start(8 + 3, self.part(3, 3), self.two.at[1, 3], minus)
        self.msg.start(4 + 0, self.part(1, 0), self.two.at[0, 0], plus)

    def add(self, ref, *others):
        total = ref[...].astype(F32)
        for other in others:
            total = total + other[...].astype(F32)
        ref[...] = total.astype(BF16)

    def near_summed(self):
        minus, plus = self.g.along_second(self.order, -1), self.g.along_second(self.order, 1)
        for m, db, da, base, side, peer in (
            (0, 3, 2, 8, 1, minus), (1, 1, 1, 4, 0, plus), (3, 1, 3, 4, 0, plus), (2, 3, 0, 8, 1, minus)
        ):
            self.msg.wait(m, self.one.at[m])
            self.add(self.part(db, da), self.one.at[m])
            self.msg.start(base + da, self.part(db, da), self.two.at[side, da], peer)

    def settle(self, da):
        self.msg.wait(4 + da, self.two.at[0, da])
        self.msg.wait(8 + da, self.two.at[1, da])
        self.add(self.part(0, da), self.two.at[0, da], self.two.at[1, da])

    def first_far(self):
        self.settle(2)
        half = ROWS // 2
        minus, plus = self.g.along_first(self.order, -1), self.g.along_first(self.order, 1)
        self.msg.start(12, self.part(0, 2).at[pl.ds(0, half)], self.three.at[0], minus)
        self.msg.start(13, self.part(0, 2).at[pl.ds(half, half)], self.three.at[1], plus)

    def first_near(self):
        half = ROWS // 2
        minus, plus = self.g.along_first(self.order, -1), self.g.along_first(self.order, 1)
        self.settle(1)
        self.msg.wait(13, self.three.at[1])
        self.add(self.part(0, 1).at[pl.ds(half, half)], self.three.at[1])
        self.msg.start(14, self.part(0, 1), self.four.at[0], plus)
        self.settle(3)
        self.msg.wait(12, self.three.at[0])
        self.add(self.part(0, 3).at[pl.ds(0, half)], self.three.at[0])
        self.msg.start(15, self.part(0, 3), self.four.at[1], minus)

    def end(self, out):
        self.settle(0)
        self.msg.wait(14, self.four.at[0])
        self.msg.wait(15, self.four.at[1])
        total = self.part(0, 0)[...].astype(F32) + self.four[0].astype(F32)
        out[...] = (total + self.four[1].astype(F32)).astype(BF16)


def scatter_kernel(
    att_ref, gq_ref, sums_ref, wq_ref, wk_ref, wv_ref, wo_ref, rows_ref,
    out_ref, gh_ref, ge_ref,
    parts, one, two, three, four, wq, wk, wv, wo, att, gq, att_tok, gq_tok, sums_in, gk, gv,
    send, recv, seq_send, seq_recv, edge_send, edge_recv, local,
):
    g = Grid()
    body, head, last = pl.ds(SPAN, ROWS), pl.ds(0, SPAN), pl.ds(ROWS - SPAN, SPAN)
    copies = [
        pltpu.make_async_copy(src, dst, local.at[i])
        for i, (src, dst) in enumerate(
            (
                (att_ref, att.at[body]), (gq_ref, gq.at[body]), (wo_ref, wo), (wq_ref, wq),
                (wk_ref, wk), (wv_ref, wv), (sums_ref.at[g.seq], sums_in.at[g.seq]),
            )
        )
    ]
    for copy in copies:
        copy.start()
    g.barrier()
    edge = Messages(edge_send, edge_recv)
    edge.start(0, att_ref.at[last], att.at[head], g.along_seq(1))
    edge.start(1, gq_ref.at[last], gq.at[head], g.along_seq(1))
    seq_msg = Messages(seq_send, seq_recv)
    for k in range(1, NSEQ):
        peer = wrap(g.seq + k, NSEQ)
        seq_msg.start(k, sums_ref.at[peer], sums_in.at[g.seq], {"seq": peer})
    for copy in copies:
        copy.wait()
    edge.wait(0, att.at[head])
    edge.wait(1, gq.at[head])

    @pl.when(g.seq == 0)
    def _():
        att[head, :] = jnp.zeros((SPAN, W), BF16)
        gq[head, :] = jnp.zeros((SPAN, W), BF16)

    row = lax.broadcasted_iota(jnp.int32, (SPAN, 2 * SPAN), 0)
    col = lax.broadcasted_iota(jnp.int32, (SPAN, 2 * SPAN), 1)
    shift = (col == row + 1).astype(BF16)

    @pl.loop(0, ROWS // SPAN)
    def _(u):
        rows = pl.ds(pl.multiple_of(u * SPAN, SPAN), 2 * SPAN)
        here = pl.ds(pl.multiple_of(u * SPAN, SPAN), SPAN)
        att_tok[here, :] = jnp.dot(shift, att[rows, :], preferred_element_type=F32).astype(BF16)
        gq_tok[here, :] = jnp.dot(shift, gq[rows, :], preferred_element_type=F32).astype(BF16)

    streams = [
        Scatter(
            g, "zx" if i % 2 == 0 else "xz", parts.at[i], one.at[i], two.at[i], three.at[i],
            four.at[i], send.at[i], recv.at[i],
        )
        for i in range(4)
    ]
    act, enc = streams[:2], streams[2:]

    def out_part(t):
        depth = pl.ds(pl.multiple_of(t * W, W), W)
        return jnp.dot(att_tok[...], wo[:, depth], preferred_element_type=F32)

    def hidden_part(t):
        depth = pl.ds(pl.multiple_of(t * W, W), W)
        return lax.dot_general(gq_tok[...], wq[depth, :], NT_DIMS, preferred_element_type=F32)

    def enc_part(i):
        def make(t):
            depth = pl.ds(pl.multiple_of(t * W, W), W)
            total = lax.dot_general(gk[i], wk[depth, :], NT_DIMS, preferred_element_type=F32)
            return total + lax.dot_general(
                gv[i], wv[depth, :], NT_DIMS, preferred_element_type=F32
            )

        return make

    def launch(pair, makes):
        for s, make in zip(pair, makes):
            s.fill(2, make)
            s.far()
        for s, make in zip(pair, makes):
            s.fill(1, make)
            s.fill(3, make)
            s.near_own()
        for s, make in zip(pair, makes):
            s.fill(0, make)

    launch(act, (out_part, hidden_part))
    for s in act:
        s.near_summed()

    for k in range(1, NSEQ):
        seq_msg.wait(k, sums_in.at[wrap(g.seq - k, NSEQ)])
    targets = [rows_ref[0, j] for j in range(2 * NSEQ)]

    @pl.loop(0, RLEN // 16)
    def _(c):
        tile = pl.ds(pl.multiple_of(c * 16, 16), 16)
        for kind, dest in ((0, gk), (1, gv)):
            for half in range(W // 128):
                cols = slice(half * 128, (half + 1) * 128)
                totals = [jnp.zeros((16, 128), F32) for _ in range(NSEQ)]
                for j in range(2 * NSEQ):
                    value = sums_in[j // 2, j % 2, kind, tile, cols].astype(F32)
                    for n in range(NSEQ):
                        totals[n] = totals[n] + jnp.where(targets[j] == n, value, 0.0)
                for n in range(NSEQ):
                    rows = pl.ds((n % 4) * RLEN + pl.multiple_of(c * 16, 16), 16)
                    dest[n // 4, rows, cols] = totals[n].astype(BF16)

    launch(enc, (enc_part(0), enc_part(1)))
    for s in act:
        s.first_far()
    for s in act:
        s.first_near()
    for s in enc:
        s.near_summed()
    act[0].end(out_ref)
    act[1].end(gh_ref)
    for s in enc:
        s.first_far()
    for s in enc:
        s.first_near()
    enc[0].end(ge_ref.at[pl.ds(0, ROWS)])
    enc[1].end(ge_ref.at[pl.ds(ROWS, ROWS)])
    for s in streams:
        s.msg.finish()
    seq_msg.finish()
    edge.finish()


def params(ident):
    return pltpu.CompilerParams(
        collective_id=ident, has_side_effects=True, vmem_limit_bytes=60 * 1024 * 1024
    )


def shape(*dims, dtype=BF16):
    return jax.ShapeDtypeStruct(dims, dtype)


def per_device(hidden, encoded, w_query, w_key, w_value, w_out, send_rows, read_slot, grad_out):
    dma = pltpu.SemaphoreType.DMA
    weight = pltpu.VMEM((NT * W, W), BF16)
    weight_out = pltpu.VMEM((W, NT * W), BF16)
    block = pltpu.VMEM((ROWS, W), BF16)
    everything = pltpu.VMEM((SIDE, SIDE, ROWS, W), BF16)
    q, ga, kv = pl.pallas_call(
        gather_kernel,
        name="gather_project",
        out_shape=(
            shape(ROWS + SPAN, W), shape(ROWS + SPAN, W), shape(NSEQ, 2, 2, RLEN, W),
        ),
        in_specs=[ANY] * 7 + [SM],
        out_specs=(ANY, ANY, ANY),
        scratch_shapes=[
            everything, everything, everything, everything,
            weight, weight, weight, weight_out,
            pltpu.VMEM((2, ROWS, W), F32), pltpu.VMEM((2, ROWS, W), F32),
            pltpu.VMEM((NSEQ, 2, RLEN, W), BF16), pltpu.VMEM((NSEQ, 2, 2, RLEN, W), BF16),
            block, block,
            dma((4, 16)), dma((4, 16)), dma((NSEQ,)), dma((NSEQ,)), dma((2,)), dma((2,)), dma((9,)),
        ],
        compiler_params=params(0),
    )(
        encoded.reshape(2 * ROWS, W), hidden, grad_out, w_query, w_key, w_value, w_out, send_rows,
    )
    att, gq, sums = pl.pallas_call(
        attention_kernel,
        name="attention",
        out_shape=(shape(ROWS, W), shape(ROWS, W), shape(2 * NSEQ, 2, RLEN, W)),
        in_specs=[SM, VM, VM, VM],
        out_specs=(VM, VM, VM),
        scratch_shapes=[pltpu.VMEM((2 * NSEQ, 2, RLEN, W), F32)],
        compiler_params=pltpu.CompilerParams(vmem_limit_bytes=60 * 1024 * 1024),
    )(read_slot, q, ga, kv.reshape(2 * NSEQ, 2, RLEN, W))
    out, gh, ge = pl.pallas_call(
        scatter_kernel,
        name="project_scatter",
        out_shape=(shape(ROWS, W), shape(ROWS, W), shape(2 * ROWS, W)),
        in_specs=[ANY] * 7 + [SM],
        out_specs=(VM, VM, VM),
        scratch_shapes=[
            pltpu.VMEM((4, SIDE, SIDE, ROWS, W), BF16),
            pltpu.VMEM((4, 4, ROWS, W), BF16),
            pltpu.VMEM((4, 2, 4, ROWS, W), BF16),
            pltpu.VMEM((4, 2, ROWS // 2, W), BF16),
            pltpu.VMEM((4, 2, ROWS, W), BF16),
            weight, weight, weight, weight_out,
            pltpu.VMEM((ROWS + SPAN, W), BF16), pltpu.VMEM((ROWS + SPAN, W), BF16),
            block, block,
            pltpu.VMEM((NSEQ, 2, 2, RLEN, W), BF16),
            pltpu.VMEM((2, ROWS, W), BF16), pltpu.VMEM((2, ROWS, W), BF16),
            dma((4, 16)), dma((4, 16)), dma((NSEQ,)), dma((NSEQ,)), dma((2,)), dma((2,)), dma((9,)),
        ],
        compiler_params=params(1),
    )(
        att, gq, sums.reshape(NSEQ, 2, 2, RLEN, W), w_query, w_key, w_value, w_out, send_rows,
    )
    return out, gh, ge.reshape(encoded.shape)


def solution(mesh):
    placed = (
        P("seq", "tensor"),
        P("seq", None, "tensor"),
        P(None, "tensor"),
        P(None, "tensor"),
        P(None, "tensor"),
        P("tensor", None),
        P("seq", None),
        P("seq", None),
        P("seq", "tensor"),
    )
    return jax.shard_map(
        per_device,
        mesh=mesh,
        in_specs=placed,
        out_specs=(P("seq", "tensor"), P("seq", "tensor"), P("seq", None, "tensor")),
        check_vma=False,
    )
```

```python
import functools

import jax
import jax.numpy as jnp
from jax import lax
from jax.experimental import pallas as pl
from jax.experimental.pallas import tpu as pltpu
from jax.sharding import PartitionSpec as P

SPAN = 64
NEIGH = 2
RLEN = 128
HEAD_DIM = 128
NSEQ = 8
SIDE = 4
NT = SIDE * SIDE
W = 256
ROWS = 512
Q = ROWS // SIDE
EQ = 2 * ROWS // SIDE
MESH = pl.DeviceIdType.MESH
ANY = pl.BlockSpec(memory_space=pl.ANY)
VM = pl.BlockSpec(memory_space=pltpu.VMEM)
SM = pl.BlockSpec(memory_space=pltpu.SMEM)
F32 = jnp.float32
BF16 = jnp.bfloat16
NT_DIMS = (((1,), (1,)), ((), ()))
TN_DIMS = (((0,), (0,)), ((), ()))


def wrap(value, count):
    return lax.rem(value + count, count)


class Grid:
    def __init__(self):
        self.seq = lax.axis_index("seq")
        tensor = lax.axis_index("tensor")
        self.z = lax.div(tensor, SIDE)
        self.x = lax.rem(tensor, SIDE)
        self.y = lax.div(self.seq, 2)
        self.core = lax.rem(self.seq, 2)

    def at(self, axis):
        return self.z if axis == "z" else self.x

    def along(self, axis, step):
        if axis == "z":
            return {"tensor": wrap(self.z + step, SIDE) * SIDE + self.x}
        if axis == "x":
            return {"tensor": self.z * SIDE + wrap(self.x + step, SIDE)}
        if axis == "y":
            return {"seq": wrap(self.y + step, SIDE) * 2 + self.core}
        if axis == "core":
            return {"seq": self.y * 2 + (1 - self.core)}
        return {"seq": wrap(self.seq + step, NSEQ)}

    def barrier(self):
        sem = pltpu.get_barrier_semaphore()
        peers = [self.along(axis, k) for axis in "zx" for k in range(1, SIDE)]
        peers += [self.along("seq", k) for k in range(1, NSEQ)]
        for peer in peers:
            pl.semaphore_signal(sem, inc=1, device_id=peer, device_id_type=MESH)
        pl.semaphore_wait(sem, len(peers))


class Messages:
    def __init__(self, send, recv):
        self.send, self.recv, self.sent, self.used = send, recv, [], 0

    def block(self, count):
        self.used += count
        return self.used - count

    def start(self, m, src, dst, peer):
        copy = pltpu.make_async_remote_copy(
            src_ref=src,
            dst_ref=dst,
            send_sem=self.send.at[m],
            recv_sem=self.recv.at[m],
            device_id=peer,
            device_id_type=MESH,
        )
        copy.start()
        self.sent.append(copy)

    def wait(self, m, dst):
        pltpu.make_async_copy(dst, dst, self.recv.at[m]).wait()

    def finish(self):
        for copy in self.sent:
            copy.wait_send()
        self.sent = []


class Gather:
    def __init__(self, grid, msg, cut, ring, own, buf):
        self.g, self.msg, self.cut, self.ring, self.own, self.buf = grid, msg, cut, ring, own, buf
        self.n = buf.shape[2]
        self.i, self.j = grid.at(cut), grid.at(ring)
        self.base = msg.block(15)

    def slot(self, dj, di):
        return self.buf.at[wrap(self.j + dj, SIDE), wrap(self.i + di, SIDE)]

    def quarter(self, di):
        start = wrap(self.i + di, SIDE) * self.n
        return self.own.at[pl.ds(pl.multiple_of(start, self.n), self.n)]

    def swap(self):
        for k in (1, 3, 2):
            peer = self.g.along(self.cut, k)
            self.msg.start(self.base + k - 1, self.quarter(k), self.slot(0, 0), peer)

    def spread(self, di):
        src = self.quarter(0) if di == 0 else self.slot(0, di)
        if di:
            self.msg.wait(self.base + SIDE - di - 1, src)
        for n, step in enumerate((1, -1)):
            self.msg.start(
                self.base + 3 + 2 * di + n, src, self.slot(0, di), self.g.along(self.ring, step)
            )

    def forward(self, di):
        ahead = di in (0, 1)
        self.msg.wait(self.base + 3 + 2 * di, self.slot(3, di))
        self.msg.wait(self.base + 4 + 2 * di, self.slot(1, di))
        block = self.slot(3 if ahead else 1, di)
        self.msg.start(
            self.base + 11 + di, block, block, self.g.along(self.ring, 1 if ahead else -1)
        )

    def settle(self):
        for di in range(SIDE):
            self.msg.wait(self.base + 11 + di, self.slot(2, di))


class Weight:
    def __init__(self, grid, msg, cut, own, full, shared, wide):
        self.g, self.msg, self.cut, self.own, self.full = grid, msg, cut, own, full
        self.shared, self.wide = shared, wide
        self.i = grid.at(cut)
        self.base = msg.block(17)
        self.half = NT * W // 2
        self.n = self.half // SIDE if shared else self.half

    def cutout(self, ref, start, size):
        rows = pl.ds(pl.multiple_of(start, W), size)
        return ref.at[:, rows] if self.wide else ref.at[rows]

    def region(self, core):
        return core * self.half, self.half

    def chunk(self, dy=0):
        if not self.shared:
            return self.region(self.g.core)
        return self.g.core * self.half + wrap(self.g.y + dy, SIDE) * self.n, self.n

    def piece(self, e, where, part=None):
        start, size = where
        if part is not None:
            size = size // 2
            start = start + part * size
        return self.cutout(self.full.at[wrap(self.i + e, SIDE)], start, size)

    def start(self):
        mine = self.cutout(self.own, *self.chunk())
        for n, step in enumerate((1, -1)):
            self.msg.start(
                self.base + n, mine, self.piece(0, self.chunk()), self.g.along(self.cut, step)
            )

    def share(self, e):
        if self.shared:
            first = {3: 4, 1: 6, 2: 8}[e]
            block = self.piece(e, self.chunk())
            for n, step in enumerate((1, -1)):
                self.msg.start(self.base + first + n, block, block, self.g.along("y", step))
        else:
            self.swap_cores(e)

    def swap_cores(self, e):
        block = self.piece(e, self.region(self.g.core))
        self.msg.start(self.base + 14 + {3: 0, 1: 1, 2: 2}[e], block, block, self.g.along("core", 1))

    def near(self):
        here = self.chunk()
        self.msg.wait(self.base, self.piece(3, here))
        part = self.piece(3, here, 0)
        self.msg.start(self.base + 2, part, part, self.g.along(self.cut, 1))
        self.msg.wait(self.base + 1, self.piece(1, here))
        part = self.piece(1, here, 1)
        self.msg.start(self.base + 3, part, part, self.g.along(self.cut, -1))
        self.share(3)
        self.share(1)

    def far(self):
        here = self.chunk()
        self.msg.wait(self.base + 2, self.piece(2, here, 0))
        self.msg.wait(self.base + 3, self.piece(2, here, 1))
        self.share(2)

    def shared_near(self):
        up, down = self.chunk(-1), self.chunk(1)
        for e, first in ((3, 4), (1, 6)):
            self.msg.wait(self.base + first, self.piece(e, up))
            self.msg.wait(self.base + first + 1, self.piece(e, down))
        block = self.piece(3, up)
        self.msg.start(self.base + 10, block, block, self.g.along("y", 1))
        block = self.piece(1, down)
        self.msg.start(self.base + 11, block, block, self.g.along("y", -1))

    def shared_far(self):
        up, down = self.chunk(-1), self.chunk(1)
        self.msg.wait(self.base + 8, self.piece(2, up))
        self.msg.wait(self.base + 9, self.piece(2, down))
        block = self.piece(2, up, 0)
        self.msg.start(self.base + 12, block, block, self.g.along("y", 1))
        block = self.piece(2, down, 1)
        self.msg.start(self.base + 13, block, block, self.g.along("y", -1))

    def shared_end(self):
        across = self.chunk(2)
        self.msg.wait(self.base + 10, self.piece(3, across))
        self.swap_cores(3)
        self.msg.wait(self.base + 11, self.piece(1, across))
        self.swap_cores(1)
        self.msg.wait(self.base + 12, self.piece(2, across, 0))
        self.msg.wait(self.base + 13, self.piece(2, across, 1))
        self.swap_cores(2)

    def ready(self, e):
        if e:
            m = self.base + 14 + {3: 0, 1: 1, 2: 2}[e]
            self.msg.wait(m, self.piece(e, self.region(1 - self.g.core)))


def lanes(blocks):
    return jnp.concatenate(blocks, 1)


def gather_kernel(
    enc_ref, hid_ref, gout_ref, wq_ref, wk_ref, wv_ref, wo_ref, rows_ref,
    q_ref, ga_ref, kv_ref, wq_out, wk_out, wv_out, wo_out,
    enc_all, hid_all, gout_all, wq, wk, wv, wo, kv_send, q_send, ga_send, own_k, own_v, stage, q_low, ga_low,
    send, recv, local,
):
    g = Grid()
    msg = Messages(send, recv)
    used = [0]

    def copy(src, dst):
        used[0] += 1
        return pltpu.make_async_copy(src, dst, local.at[used[0] - 1])

    enc = Gather(g, msg, "x", "z", enc_ref, enc_all)
    hid = Gather(g, msg, "z", "x", hid_ref, hid_all)
    gout = Gather(g, msg, "z", "x", gout_ref, gout_all)
    w_key = Weight(g, msg, "x", wk_ref, wk, True, False)
    w_value = Weight(g, msg, "x", wv_ref, wv, False, False)
    w_query = Weight(g, msg, "z", wq_ref, wq, True, False)
    w_out = Weight(g, msg, "z", wo_ref, wo, False, True)
    loads = [copy(s.quarter(0), s.slot(0, 0)) for s in (enc, hid, gout)]
    loads += [copy(w.own, w.full.at[w.i]) for w in (w_key, w_value, w_query, w_out)]
    g.barrier()
    enc.swap()
    hid.swap()
    gout.swap()
    w_key.start()
    enc.spread(0)
    w_query.start()
    w_value.start()
    for load in loads:
        load.start()
    for di in (3, 1, 2):
        enc.spread(di)
    w_out.start()
    for di in (0, 3, 1):
        enc.forward(di)
    w_key.near()
    w_key.far()
    enc.forward(2)
    w_query.near()
    w_query.far()
    for s in (hid, gout):
        for di in (0, 3, 1, 2):
            s.spread(di)
    w_key.shared_near()
    w_key.shared_far()
    enc.settle()
    w_value.near()
    w_key.shared_end()
    w_query.shared_near()
    w_query.shared_far()
    for load in loads:
        load.wait()

    keep = []
    out_base = msg.block(12)

    def columns(s, w, e):
        w.ready(e)
        at = wrap(w.i + e, SIDE)
        total = None
        for n in range(SIDE):
            if s.ring == "z":
                left = lanes([s.buf[n, k] for k in range(SIDE)])
            else:
                left = lanes([s.buf[k, n] for k in range(SIDE)])
            depth = pl.ds(n * SIDE * W, SIDE * W)
            if w.wide:
                term = lax.dot_general(
                    left, w.full[at, :, depth], NT_DIMS, preferred_element_type=F32
                )
            else:
                term = jnp.dot(left, w.full[at, depth, :], preferred_element_type=F32)
            total = term if total is None else total + term
        return total.astype(BF16)

    def project(s, w, e, kind, dst, sender):
        value = columns(s, w, e)
        shaped = value.reshape(sender.shape[1:])
        if e == 0:
            dst[...] = shaped
        else:
            sender[e] = shaped
            msg.start(out_base + 3 * kind + e - 1, sender.at[e], dst, g.along(s.cut, e))

    def arrived(s, kind, dst_of):
        for e in range(1, SIDE):
            msg.wait(out_base + 3 * kind + e - 1, dst_of(wrap(s.i - e, SIDE)))

    per = SPAN * 4 // RLEN

    def kv_rows(kind):
        return lambda i: (own_k, own_v)[kind].at[pl.ds(i * per, per)]

    for e in (0, 3, 1, 2):
        project(enc, w_key, e, 0, kv_rows(0)(g.x), kv_send.at[0])
    w_value.far()
    w_out.near()
    for e in (0, 3, 1, 2):
        project(enc, w_value, e, 1, kv_rows(1)(g.x), kv_send.at[1])

    seq_base = msg.block(2 * NSEQ)

    def exchange(kind):
        arrived(enc, kind, kv_rows(kind))

        @pl.loop(0, NSEQ)
        def _(r):
            for s in range(2):
                stage[kind, r, s] = (own_k, own_v)[kind][jnp.maximum(rows_ref[0, 2 * r + s], 0)]

        for k in range(1, NSEQ):
            peer = wrap(g.seq + k, NSEQ)
            msg.start(
                seq_base + NSEQ * kind + k, stage.at[kind, peer], kv_ref.at[kind, g.seq], {"seq": peer}
            )
        own = copy(stage.at[kind, g.seq], kv_ref.at[kind, g.seq])
        own.start()
        keep.append(own)

    exchange(0)
    exchange(1)
    w_query.shared_end()
    w_out.far()
    for s in (hid, gout):
        for di in (0, 3, 1, 2):
            s.forward(di)
    for s in (hid, gout):
        s.settle()

    def rows_of(ref):
        return lambda i: ref.at[pl.ds(pl.multiple_of(i * Q, Q), Q)]

    for e in (0, 3, 1, 2):
        project(hid, w_query, e, 2, rows_of(q_low)(g.z), q_send)
    for e in (0, 3, 1, 2):
        project(gout, w_out, e, 3, rows_of(ga_low)(g.z), ga_send)
    weights_out = [
        copy(w.full, out)
        for w, out in ((w_key, wk_out), (w_value, wv_out), (w_query, wq_out), (w_out, wo_out))
    ]
    for c in weights_out:
        c.start()
    edge = msg.block(2)
    head, tail, body = pl.ds(0, SPAN), pl.ds(ROWS, SPAN), pl.ds(0, ROWS)
    for kind, (s, low, ref) in enumerate(((hid, q_low, q_ref), (gout, ga_low, ga_ref))):
        arrived(s, 2 + kind, rows_of(low))
        msg.start(edge + kind, low.at[head], ref.at[tail], g.along("seq", -1))
        own = copy(low, ref.at[body])
        own.start()
        keep.append(own)
    for kind in range(2):
        for k in range(1, NSEQ):
            msg.wait(seq_base + NSEQ * kind + k, kv_ref.at[kind, wrap(g.seq - k, NSEQ)])
    msg.wait(edge, q_ref.at[tail])
    msg.wait(edge + 1, ga_ref.at[tail])
    msg.finish()
    for c in keep + weights_out:
        c.wait()


def attention_kernel(slot_ref, q_ref, ga_ref, kv_ref, att_ref, gq_ref, sums_ref, sums):
    spans = ROWS // SPAN
    scale = HEAD_DIM ** (-0.5)
    last = lax.axis_index("seq") == NSEQ - 1
    row = lax.broadcasted_iota(jnp.int32, (SPAN, 2 * SPAN), 0)
    col = lax.broadcasted_iota(jnp.int32, (SPAN, 2 * SPAN), 1)
    picked = col == row + (SPAN - 1)
    sums[...] = jnp.zeros_like(sums)

    @pl.loop(0, spans)
    def _(u):
        rows = pl.ds(pl.multiple_of(u * SPAN, SPAN), 2 * SPAN)
        inside = jnp.logical_or(col < SPAN, jnp.logical_not(last & (u == spans - 1)))
        shift = jnp.logical_and(picked, inside).astype(BF16)
        q_all = jnp.dot(shift, q_ref[rows, :], preferred_element_type=F32).astype(BF16)
        g_all = jnp.dot(shift, ga_ref[rows, :], preferred_element_type=F32).astype(BF16)
        slots = [slot_ref[u, j] for j in range(NEIGH)]
        for h in range(W // HEAD_DIM):
            cols = slice(h * HEAD_DIM, (h + 1) * HEAD_DIM)
            q, gr = q_all[:, cols], g_all[:, cols]
            k = jnp.concatenate([kv_ref[0, s, :, cols] for s in slots], 0)
            v = jnp.concatenate([kv_ref[1, s, :, cols] for s in slots], 0)
            scores = lax.dot_general(q, k, NT_DIMS, preferred_element_type=F32) * scale
            peak = jnp.max(scores, axis=-1, keepdims=True)
            weights = jnp.exp(scores - peak)
            probs = weights / jnp.sum(weights, axis=-1, keepdims=True)
            probs_low = probs.astype(BF16)
            context = jnp.dot(probs_low, v, preferred_element_type=F32)
            grad_probs = lax.dot_general(gr, v, NT_DIMS, preferred_element_type=F32)
            dot_sum = jnp.sum(grad_probs * probs, axis=-1, keepdims=True)
            grad_scores = (probs * (grad_probs - dot_sum) * scale).astype(BF16)
            grad_q = jnp.dot(grad_scores, k, preferred_element_type=F32)
            grad_k = lax.dot_general(grad_scores, q, TN_DIMS, preferred_element_type=F32)
            grad_v = lax.dot_general(probs_low, gr, TN_DIMS, preferred_element_type=F32)
            here = pl.ds(pl.multiple_of(u * SPAN, SPAN), SPAN)
            att_ref[here, cols] = context.astype(BF16)
            gq_ref[here, cols] = grad_q.astype(BF16)
            for j, s in enumerate(slots):
                part = slice(j * RLEN, (j + 1) * RLEN)
                sums[s, 0, :, cols] += grad_k[part]
                sums[s, 1, :, cols] += grad_v[part]

    @pl.loop(0, sums.shape[0])
    def _(s):
        sums_ref[s] = sums[s].astype(BF16)


class Scatter:
    def __init__(self, grid, msg, cut, ring, own, got, parts, one, two):
        self.g, self.msg, self.cut, self.ring = grid, msg, cut, ring
        self.own, self.got, self.parts, self.one, self.two = own, got, parts, one, two
        self.i, self.j = grid.at(cut), grid.at(ring)
        self.base = msg.block(12)

    def swap(self):
        for k in (1, 3, 2):
            peer = wrap(self.i + k, SIDE)
            self.msg.start(
                self.base + k - 1, self.own.at[peer], self.got.at[self.i], self.g.along(self.cut, k)
            )
        self.got[self.i] = self.own[self.i]

    def swapped(self):
        for k in (1, 3, 2):
            self.msg.wait(self.base + k - 1, self.got.at[wrap(self.i - k, SIDE)])

    def part(self, dj, where=None):
        block = self.parts.at[wrap(self.j + dj, SIDE)]
        return block if where is None else block.at[pl.ds(2 * where, 2)]

    def fill(self, dj, make):
        j = wrap(self.j + dj, SIDE)

        @pl.loop(0, SIDE)
        def _(i):
            t = j * SIDE + i if self.ring == "z" else i * SIDE + j
            self.parts[j, i] = make(t).astype(BF16)

    def far(self):
        self.msg.start(self.base + 3, self.part(2, 0), self.one.at[0], self.g.along(self.ring, -1))
        self.msg.start(self.base + 4, self.part(2, 1), self.one.at[1], self.g.along(self.ring, 1))

    def to_plus(self, where):
        self.msg.start(
            self.base + 5 + where, self.part(1, where), self.two.at[0, pl.ds(2 * where, 2)],
            self.g.along(self.ring, 1),
        )

    def to_minus(self, where):
        self.msg.start(
            self.base + 7 + where, self.part(3, where), self.two.at[1, pl.ds(2 * where, 2)],
            self.g.along(self.ring, -1),
        )

    def add(self, ref, *others):
        total = ref[...].astype(F32)
        for other in others:
            total = total + other[...].astype(F32)
        ref[...] = total.astype(BF16)

    def near(self):
        self.msg.wait(self.base + 3, self.one.at[0])
        self.add(self.part(3, 0), self.one.at[0])
        self.to_minus(0)
        self.msg.wait(self.base + 4, self.one.at[1])
        self.add(self.part(1, 1), self.one.at[1])
        self.to_plus(1)

    def end(self, out):
        n = self.parts.shape[2]
        for where in (1, 0):
            half = pl.ds(2 * where, 2)
            self.msg.wait(self.base + 5 + where, self.two.at[0, half])
            self.msg.wait(self.base + 7 + where, self.two.at[1, half])
            self.add(self.part(0, where), self.two.at[0, half], self.two.at[1, half])

        def rows(i):
            return out.at[pl.ds(pl.multiple_of(i * n, n), n)]

        for k in (1, 3, 2):
            self.msg.start(
                self.base + 8 + k, self.part(0).at[wrap(self.i + k, SIDE)], rows(self.i),
                self.g.along(self.cut, k),
            )
        rows(self.i)[...] = self.part(0)[self.i]
        return rows

    def back(self, rows):
        for k in range(1, SIDE):
            self.msg.wait(self.base + 8 + k, rows(wrap(self.i - k, SIDE)))


def scatter_kernel(
    att_ref, gq_ref, sums_ref, wq_ref, wk_ref, wv_ref, wo_ref, rows_ref,
    out_ref, gh_ref, ge_ref,
    parts, parts_enc, one, one_enc, two, two_enc, wq, wk, wv, wo, att, gq, tok, got, sums_in, gkv, gkv_got,
    send, recv, local,
):
    g = Grid()
    msg = Messages(send, recv)
    body, head, last = pl.ds(SPAN, ROWS), pl.ds(0, SPAN), pl.ds(ROWS - SPAN, SPAN)
    copies = [
        pltpu.make_async_copy(src, dst, local.at[i])
        for i, (src, dst) in enumerate(
            (
                (att_ref, att.at[body]), (gq_ref, gq.at[body]), (sums_ref.at[g.seq], sums_in.at[g.seq]),
                (wo_ref, wo), (wq_ref, wq), (wk_ref, wk), (wv_ref, wv),
            )
        )
    ]
    for c in copies:
        c.start()
    g.barrier()
    edge, seq_base = msg.block(2), msg.block(NSEQ)
    msg.start(edge, att_ref.at[last], att.at[head], g.along("seq", 1))
    msg.start(edge + 1, gq_ref.at[last], gq.at[head], g.along("seq", 1))
    for k in range(1, NSEQ):
        peer = wrap(g.seq + k, NSEQ)
        msg.start(seq_base + k, sums_ref.at[peer], sums_in.at[g.seq], {"seq": peer})
    streams = [
        Scatter(g, msg, "z", "x", tok.at[i], got.at[i], parts.at[i], one.at[i], two.at[i])
        for i in range(2)
    ]
    enc = Scatter(g, msg, "x", "z", gkv, gkv_got, parts_enc, one_enc, two_enc)
    copies[0].wait()
    copies[1].wait()
    msg.wait(edge, att.at[head])
    msg.wait(edge + 1, gq.at[head])

    @pl.when(g.seq == 0)
    def _():
        att[head, :] = jnp.zeros((SPAN, W), BF16)
        gq[head, :] = jnp.zeros((SPAN, W), BF16)

    row = lax.broadcasted_iota(jnp.int32, (Q, Q + SPAN), 0)
    col = lax.broadcasted_iota(jnp.int32, (Q, Q + SPAN), 1)
    shift = (col == row + 1).astype(BF16)
    for kind, src in ((0, att), (1, gq)):
        for n in range(SIDE):
            moved = jnp.dot(shift, src[n * Q : (n + 1) * Q + SPAN, :], preferred_element_type=F32)
            tok[kind, n] = moved.astype(BF16)
        streams[kind].swap()

    def out_part(t):
        depth = pl.ds(pl.multiple_of(t * W, W), W)
        return sum(
            jnp.dot(got[0, i], wo[i, :, depth], preferred_element_type=F32) for i in range(SIDE)
        )

    def hidden_part(t):
        depth = pl.ds(pl.multiple_of(t * W, W), W)
        return sum(
            lax.dot_general(got[1, i], wq[i, depth, :], NT_DIMS, preferred_element_type=F32)
            for i in range(SIDE)
        )

    def enc_part(t):
        depth = pl.ds(pl.multiple_of(t * W, W), W)
        total = None
        for kind, w in ((0, wk), (1, wv)):
            for i in range(SIDE):
                term = lax.dot_general(
                    gkv_got[i, kind], w[i, depth, :], NT_DIMS, preferred_element_type=F32
                )
                total = term if total is None else total + term
        return total

    def launch(s, make):
        s.swapped()
        s.fill(2, make)
        s.far()
        s.fill(1, make)
        s.to_plus(0)
        s.fill(3, make)
        s.to_minus(1)
        s.fill(0, make)

    copies[3].wait()
    launch(streams[0], out_part)
    copies[4].wait()
    launch(streams[1], hidden_part)
    for s in streams:
        s.near()
    copies[2].wait()
    for k in range(1, NSEQ):
        msg.wait(seq_base + k, sums_in.at[wrap(g.seq - k, NSEQ)])
    targets = [rows_ref[0, j] for j in range(2 * NSEQ)]
    per = EQ // RLEN

    @pl.loop(0, RLEN // 16)
    def _(c):
        tile = pl.ds(pl.multiple_of(c * 16, 16), 16)
        for kind in range(2):
            for half in range(W // 128):
                cols = slice(half * 128, (half + 1) * 128)
                totals = [jnp.zeros((16, 128), F32) for _ in range(NSEQ)]
                for j in range(2 * NSEQ):
                    value = sums_in[j // 2, j % 2, kind, tile, cols].astype(F32)
                    for n in range(NSEQ):
                        totals[n] = totals[n] + jnp.where(targets[j] == n, value, 0.0)
                for n in range(NSEQ):
                    rows = pl.ds((n % per) * RLEN + pl.multiple_of(c * 16, 16), 16)
                    gkv[n // per, kind, rows, cols] = totals[n].astype(BF16)

    enc.swap()
    ends = [s.end(out) for s, out in zip(streams, (out_ref, gh_ref))]
    copies[5].wait()
    copies[6].wait()
    launch(enc, enc_part)
    enc.near()
    end = enc.end(ge_ref)
    for s, rows in zip(streams, ends):
        s.back(rows)
    enc.back(end)
    msg.finish()


def params(ident):
    return pltpu.CompilerParams(
        collective_id=ident, has_side_effects=True, vmem_limit_bytes=60 * 1024 * 1024
    )


def shape(*dims, dtype=BF16):
    return jax.ShapeDtypeStruct(dims, dtype)


def per_device(hidden, encoded, w_query, w_key, w_value, w_out, send_rows, read_slot, grad_out):
    dma = pltpu.SemaphoreType.DMA
    weight = pltpu.VMEM((SIDE, NT * W, W), BF16)
    weight_out = pltpu.VMEM((SIDE, W, NT * W), BF16)
    block = pltpu.VMEM((ROWS, W), BF16)
    quarters = pltpu.VMEM((SIDE, Q, W), BF16)
    tall = shape(SIDE, NT * W, W)
    q, ga, kv, wq, wk, wv, wo = pl.pallas_call(
        gather_kernel,
        name="gather_project",
        out_shape=(
            shape(ROWS + SPAN, W), shape(ROWS + SPAN, W), shape(2, NSEQ, 2, RLEN, W),
            tall, tall, tall, shape(SIDE, W, NT * W),
        ),
        in_specs=[ANY] * 7 + [SM],
        out_specs=(ANY,) * 7,
        scratch_shapes=[
            pltpu.VMEM((SIDE, SIDE, EQ, W), BF16),
            pltpu.VMEM((SIDE, SIDE, Q, W), BF16), pltpu.VMEM((SIDE, SIDE, Q, W), BF16),
            weight, weight, weight, weight_out,
            pltpu.VMEM((2, SIDE, EQ // RLEN, RLEN, W), BF16), quarters, quarters,
            pltpu.VMEM((NSEQ, RLEN, W), BF16), pltpu.VMEM((NSEQ, RLEN, W), BF16),
            pltpu.VMEM((2, NSEQ, 2, RLEN, W), BF16),
            block, block,
            dma((144,)), dma((144,)), dma((16,)),
        ],
        compiler_params=params(0),
    )(
        encoded.reshape(2 * ROWS, W), hidden, grad_out, w_query, w_key, w_value, w_out, send_rows,
    )
    att, gq, sums = pl.pallas_call(
        attention_kernel,
        name="attention",
        out_shape=(shape(ROWS, W), shape(ROWS, W), shape(2 * NSEQ, 2, RLEN, W)),
        in_specs=[SM, VM, VM, VM],
        out_specs=(VM, VM, VM),
        scratch_shapes=[pltpu.VMEM((2 * NSEQ, 2, RLEN, W), F32)],
        compiler_params=pltpu.CompilerParams(vmem_limit_bytes=60 * 1024 * 1024),
    )(read_slot, q, ga, kv.reshape(2, 2 * NSEQ, RLEN, W))
    out, gh, ge = pl.pallas_call(
        scatter_kernel,
        name="project_scatter",
        out_shape=(shape(ROWS, W), shape(ROWS, W), shape(2 * ROWS, W)),
        in_specs=[ANY] * 7 + [SM],
        out_specs=(VM, VM, VM),
        scratch_shapes=[
            pltpu.VMEM((2, SIDE, SIDE, Q, W), BF16), pltpu.VMEM((SIDE, SIDE, EQ, W), BF16),
            pltpu.VMEM((2, 2, 2, Q, W), BF16), pltpu.VMEM((2, 2, EQ, W), BF16),
            pltpu.VMEM((2, 2, SIDE, Q, W), BF16), pltpu.VMEM((2, SIDE, EQ, W), BF16),
            weight, weight, weight, weight_out,
            pltpu.VMEM((ROWS + SPAN, W), BF16), pltpu.VMEM((ROWS + SPAN, W), BF16),
            pltpu.VMEM((2, SIDE, Q, W), BF16), pltpu.VMEM((2, SIDE, Q, W), BF16),
            pltpu.VMEM((NSEQ, 2, 2, RLEN, W), BF16),
            pltpu.VMEM((SIDE, 2, EQ, W), BF16), pltpu.VMEM((SIDE, 2, EQ, W), BF16),
            dma((48,)), dma((48,)), dma((8,)),
        ],
        compiler_params=params(1),
    )(
        att, gq, sums.reshape(NSEQ, 2, 2, RLEN, W), wq, wk, wv, wo, send_rows,
    )
    return out, gh, ge.reshape(encoded.shape)


def solution(mesh):
    placed = (
        P("seq", "tensor"),
        P("seq", None, "tensor"),
        P(None, "tensor"),
        P(None, "tensor"),
        P(None, "tensor"),
        P("tensor", None),
        P("seq", None),
        P("seq", None),
        P("seq", "tensor"),
    )
    return jax.shard_map(
        per_device,
        mesh=mesh,
        in_specs=placed,
        out_specs=(P("seq", "tensor"), P("seq", "tensor"), P("seq", None, "tensor")),
        check_vma=False,
    )
```

```python
import functools

import jax
import jax.numpy as jnp
from jax import lax
from jax.experimental import pallas as pl
from jax.experimental.pallas import tpu as pltpu
from jax.sharding import PartitionSpec as P

SPAN = 64
NEIGH = 2
RLEN = 128
HEAD_DIM = 128
NSEQ = 8
SIDE = 4
NT = SIDE * SIDE
W = 256
ROWS = 512
Q = ROWS // SIDE
EQ = 2 * ROWS // SIDE
MESH = pl.DeviceIdType.MESH
ANY = pl.BlockSpec(memory_space=pl.ANY)
VM = pl.BlockSpec(memory_space=pltpu.VMEM)
SM = pl.BlockSpec(memory_space=pltpu.SMEM)
F32 = jnp.float32
BF16 = jnp.bfloat16
NT_DIMS = (((1,), (1,)), ((), ()))
TN_DIMS = (((0,), (0,)), ((), ()))
SPANS = ROWS // SPAN
SLOTS = 2 * NSEQ
HEADS = W // HEAD_DIM
HALF = RLEN // 2
NONE = SPANS * NEIGH
OFFSETS = (0, 3, 1, 2)
SHARES = {"K": (256,), "V": (256,), "Q": (), "O": (256,)}
ALONE = 256
UNROLL = 2


ORDER = (
    0, 46, 92, 149, 195, 211, 227, 199, 200, 197, 198, 175, 115, 196, 167, 174, 136, 168, 100, 150, 32, 78,
    48, 47, 79, 72, 291, 207, 65, 85, 33, 204, 71, 205, 206, 119, 203, 155, 177, 36, 34, 202, 154, 76, 83,
    140, 176, 201, 74, 81, 80, 152, 49, 151, 94, 50, 51, 54, 53, 1, 64, 86, 232, 52, 178, 171, 179, 82, 172,
    104, 160, 169, 114, 58, 57, 180, 188, 19, 84, 231, 215, 55, 56, 216, 2, 143, 89, 87, 18, 69, 67, 37, 35,
    26, 62, 210, 164, 135, 208, 73, 209, 156, 153, 157, 122, 129, 60, 128, 98, 75, 61, 88, 59, 3, 66, 25, 5,
    6, 90, 239, 68, 223, 40, 39, 161, 63, 38, 93, 101, 190, 121, 11, 159, 158, 192, 77, 118, 147, 165, 21, 4,
    7, 8, 23, 28, 91, 30, 163, 142, 170, 117, 70, 139, 107, 137, 261, 22, 20, 126, 258, 263, 264, 42, 133, 15,
    214, 12, 259, 27, 131, 124, 108, 213, 10, 243, 41, 262, 9, 260, 29, 162, 182, 96, 103, 24, 105, 44, 43,
    132, 173, 244, 245, 16, 181, 116, 212, 97, 102, 14, 13, 95, 31, 45, 166, 246, 247, 221, 189, 222, 265,
    270, 267, 268, 269, 272, 17, 271, 266, 138, 228, 219, 220, 130, 145, 109, 123, 226, 229, 146, 125, 248,
    111, 249, 225, 120, 144, 218, 217, 230, 106, 99, 112, 110, 250, 224, 255, 184, 186, 251, 141, 256, 235,
    236, 253, 252, 257, 254, 233, 234, 134, 276, 127, 277, 274, 275, 273, 183, 185, 191, 193, 148, 238, 237,
    241, 113, 240, 278, 279, 242, 187, 194, 280, 283, 287, 285, 282, 284, 286, 281, 293, 288, 292, 324, 289,
    325, 327, 329, 326, 290, 294, 306, 328, 308, 302, 295, 305, 309, 348, 333, 331, 338, 332, 342, 317, 330,
    349, 353, 334, 350, 352, 335, 319, 316, 310, 351, 303, 313, 298, 323, 301, 320, 321, 318, 307, 304, 314,
    296, 322, 355, 362, 354, 359, 358, 356, 366, 357, 337, 341, 336, 339, 311, 300, 360, 363, 361, 365, 343,
    297, 315, 312, 340, 397, 400, 401, 399, 398, 347, 346, 345, 344, 299, 364, 367, 368, 372, 370, 369, 371,
    373, 376, 377, 375, 374, 402, 407, 406, 404, 414, 403, 410, 405, 378, 383, 409, 413, 382, 380, 408, 411,
    381, 379, 386, 390, 384, 387, 385, 389, 415, 412, 416, 418, 420, 417, 419, 388, 391, 392, 395, 396, 393,
    394,
)
MESSAGES = 342


def wrap(value, count):
    return lax.rem(value + count, count)


class Grid:
    def __init__(self):
        self.seq = lax.axis_index("seq")
        tensor = lax.axis_index("tensor")
        self.z = lax.div(tensor, SIDE)
        self.x = lax.rem(tensor, SIDE)
        self.y = lax.div(self.seq, 2)
        self.core = lax.rem(self.seq, 2)

    def at(self, axis):
        return self.z if axis == "z" else self.x

    def along(self, axis, step):
        if axis == "z":
            return {"tensor": wrap(self.z + step, SIDE) * SIDE + self.x}
        if axis == "x":
            return {"tensor": self.z * SIDE + wrap(self.x + step, SIDE)}
        if axis == "y":
            return {"seq": wrap(self.y + step, SIDE) * 2 + self.core}
        if axis == "core":
            return {"seq": self.y * 2 + (1 - self.core)}
        return {"seq": wrap(self.seq + step, NSEQ)}

    def barrier(self):
        sem = pltpu.get_barrier_semaphore()
        peers = [self.along(axis, k) for axis in "zx" for k in range(1, SIDE)]
        peers += [self.along("seq", k) for k in range(1, NSEQ)]
        for peer in peers:
            pl.semaphore_signal(sem, inc=1, device_id=peer, device_id_type=MESH)
        pl.semaphore_wait(sem, len(peers))


class Plan:
    def __init__(self, send, recv, local):
        self.send, self.recv, self.local = send, recv, local
        self.actions, self.copies, self.landed, self.left = {}, {}, set(), set()
        self.messages = self.locals = 0

    def message(self, name, src, dst, peer, land, after=()):
        self.actions[name] = ("message", (src, dst, peer, land, self.messages), after, ())
        self.messages += 1

    def step(self, name, work, after=(), sent=()):
        self.actions[name] = ("step", work, after, sent)

    def load(self, name, src, dst):
        self.actions[name] = ("load", (src, dst, self.locals), (), ())
        self.locals += 1

    def need(self, name):
        if name in self.landed:
            return
        kind, data, _, _ = self.actions[name]
        assert name in self.copies, name
        if kind == "message":
            land = data[3]
            pltpu.make_async_copy(land, land, self.recv.at[data[4]]).wait()
        else:
            self.copies[name].wait()
        self.landed.add(name)

    def leave(self, name):
        if name not in self.left:
            self.copies[name].wait_send()
            self.left.add(name)

    def run(self, name):
        kind, data, after, sent = self.actions[name]
        for other in after:
            self.need(other)
        for other in sent:
            self.leave(other)
        if kind == "message":
            src, dst, peer, _, number = data
            copy = pltpu.make_async_remote_copy(
                src_ref=src,
                dst_ref=dst,
                send_sem=self.send.at[number],
                recv_sem=self.recv.at[number],
                device_id=peer,
                device_id_type=MESH,
            )
            copy.start()
            self.copies[name] = copy
        elif kind == "load":
            src, dst, number = data
            copy = pltpu.make_async_copy(src, dst, self.local.at[number])
            copy.start()
            self.copies[name] = copy
        else:
            data()
            self.landed.add(name)

    def finish(self):
        for name, (kind, _, _, _) in self.actions.items():
            if kind != "step":
                self.need(name)
            if kind == "message":
                self.leave(name)


def signs():
    return (("+", 1), ("-", -1))


def add_gather(plan, g, n, cut, ring, own, buf):
    rows = buf.shape[2]
    i, j = g.at(cut), g.at(ring)

    def slot(dj, di):
        return buf.at[wrap(j + dj, SIDE), wrap(i + di, SIDE)]

    def quarter(di):
        return own.at[pl.ds(pl.multiple_of(wrap(i + di, SIDE) * rows, rows), rows)]

    plan.load((n, "l"), quarter(0), slot(0, 0))
    for k in (1, 3, 2):
        plan.message((n, "x", k), quarter(k), slot(0, 0), g.along(cut, k), slot(0, SIDE - k))
    for d in OFFSETS:
        src, after = (slot(0, d), ((n, "x", SIDE - d),)) if d else (quarter(0), ())
        for sign, step in signs():
            plan.message(
                (n, "s", d, sign), src, slot(0, d), g.along(ring, step), slot(-step + SIDE, d), after
            )
    for d in OFFSETS:
        sign, step = ("+", 1) if d in (0, 1) else ("-", -1)
        block = slot(SIDE - step, d)
        plan.message((n, "f", d), block, block, g.along(ring, step), slot(2, d), ((n, "s", d, sign),))
    names = [(n, "l")] + [(n, "x", k) for k in (1, 2, 3)] + [(n, "f", d) for d in OFFSETS]
    return names + [(n, "s", d, sign) for d in OFFSETS for sign in "+-"]


def add_weight(plan, g, n, cut, own, full, wide):
    i = g.at(cut)
    needs = {e: [] for e in OFFSETS}
    plan.load((n, "l"), own, full.at[i])
    needs[0].append((n, "l"))

    def cutout(ref, start, size):
        rows = pl.ds(pl.multiple_of(start, 128), size)
        return ref.at[:, rows] if wide else ref.at[rows]

    def add_piece(p, begin, size, shared):
        half = SIDE * size if shared else size
        other = begin + (1 - g.core) * half
        region = begin + g.core * half

        def chunk(dy):
            return region + wrap(g.y + dy, SIDE) * size if shared else region

        def at(e, start, length=size):
            return cutout(full.at[wrap(i + e, SIDE)], start, length)

        def ends(sign):
            return 0 if sign == "+" else size // 2

        here = chunk(0)
        for sign, step in signs():
            plan.message(
                (p, "n", sign), cutout(own, here, size), at(0, here), g.along(cut, step),
                at(SIDE - step, here),
            )
        for sign, step in signs():
            part = at(SIDE - step, here + ends(sign), size // 2)
            plan.message(
                (p, "h", sign), part, part, g.along(cut, step), at(2, here + ends(sign), size // 2),
                ((p, "n", sign),),
            )
        have = {3: [(p, "n", "+")], 1: [(p, "n", "-")], 2: [(p, "h", "+"), (p, "h", "-")]}
        if shared:
            for e in (3, 1, 2):
                for sign, step in signs():
                    plan.message(
                        (p, "y", e, sign), at(e, here), at(e, here), g.along("y", step),
                        at(e, chunk(SIDE - step)), tuple(have[e]),
                    )
            for e, sign, step, length in ((3, "+", 1, size), (1, "-", -1, size), (2, "+", 1, size // 2), (2, "-", -1, size // 2)):
                off = ends(sign) if e == 2 else 0
                part = at(e, chunk(SIDE - step) + off, length)
                plan.message(
                    (p, "z", e, sign), part, part, g.along("y", step), at(e, chunk(2) + off, length),
                    ((p, "y", e, sign),),
                )
            for e, last in ((3, "+"), (1, "-"), (2, "+-")):
                have[e] += [(p, "y", e, "+"), (p, "y", e, "-")] + [(p, "z", e, sign) for sign in last]
        for e in (3, 1, 2):
            block = at(e, region, half)
            plan.message(
                (p, "c", e), block, block, g.along("core", 1), at(e, other, half), tuple(have[e])
            )
            needs[e] += have[e] + [(p, "c", e)]

    begin = 0
    for count, size in enumerate(SHARES[n]):
        add_piece((n, count), begin, size, True)
        begin += 2 * SIDE * size
    while begin < NT * W:
        add_piece((n, begin // (2 * ALONE) + 8), begin, ALONE, False)
        begin += 2 * ALONE
    return needs


def lanes(blocks):
    return jnp.concatenate(blocks, 1)


def add_project(plan, g, n, cut, ring, buf, have, full, needs, wide, dst, sender):
    i = g.at(cut)

    def columns(e):
        at = wrap(i + e, SIDE)
        total = None
        for m in range(SIDE):
            if ring == "z":
                left = lanes([buf[m, k] for k in range(SIDE)])
            else:
                left = lanes([buf[k, m] for k in range(SIDE)])
            depth = pl.ds(m * SIDE * W, SIDE * W)
            if wide:
                term = lax.dot_general(left, full[at, :, depth], NT_DIMS, preferred_element_type=F32)
            else:
                term = jnp.dot(left, full[at, depth, :], preferred_element_type=F32)
            total = term if total is None else total + term
        return total.astype(BF16)

    def make(e):
        def work():
            if e:
                sender[e] = columns(e).reshape(sender.shape[1:])
            else:
                dst(i)[...] = columns(e).reshape(sender.shape[1:])

        return work

    for e in OFFSETS:
        plan.step((n, "p", e), make(e), tuple(have + needs[e]))
        if e:
            plan.message(
                (n, "o", e), sender.at[e], dst(i), g.along(cut, e), dst(wrap(i - e, SIDE)),
                ((n, "p", e),),
            )
    return [(n, "p", 0)] + [(n, "o", e) for e in (1, 2, 3)]


def add_scatter(plan, g, n, cut, ring, own, own_step, got, parts, one, two, make, out, old=(), final=None):
    i, j = g.at(cut), g.at(ring)

    def keep():
        got[i] = own[i]

    plan.step((n, "k"), keep, (own_step,))
    for k in (1, 3, 2):
        peer = wrap(i + k, SIDE)
        plan.message(
            (n, "x", k), own.at[peer], got.at[i], g.along(cut, k), got.at[wrap(i - k, SIDE)],
            (own_step,),
        )
    swapped = ((n, "k"), (n, "x", 1), (n, "x", 2), (n, "x", 3))

    def part(dj, where=None):
        block = parts.at[wrap(j + dj, SIDE)]
        return block if where is None else block.at[pl.ds(2 * where, 2)]

    def fill(dj):
        def work():
            row = wrap(j + dj, SIDE)

            @pl.loop(0, SIDE)
            def _(k):
                t = row * SIDE + k if ring == "z" else k * SIDE + row
                parts[row, k] = make(t).astype(BF16)

        return work

    def add(ref, *others):
        total = ref[...].astype(F32)
        for other in others:
            total = total + other[...].astype(F32)
        ref[...] = total.astype(BF16)

    for dj in (2, 1, 3, 0):
        plan.step((n, "f", dj), fill(dj), swapped, old)
    plan.message((n, "n", 0), part(2, 0), one.at[0], g.along(ring, -1), one.at[0], ((n, "f", 2),))
    plan.message((n, "n", 1), part(2, 1), one.at[1], g.along(ring, 1), one.at[1], ((n, "f", 2),))
    plan.step((n, "r", 0), lambda: add(part(3, 0), one.at[0]), ((n, "f", 3), (n, "n", 0)))
    plan.step((n, "r", 1), lambda: add(part(1, 1), one.at[1]), ((n, "f", 1), (n, "n", 1)))
    for where in range(2):
        half = pl.ds(2 * where, 2)
        up, down = two.at[0, half], two.at[1, half]
        plan.message(
            (n, "u", where), part(1, where), up, g.along(ring, 1), up, ((n, "r", 1) if where else (n, "f", 1),)
        )
        plan.message(
            (n, "d", where), part(3, where), down, g.along(ring, -1), down, ((n, "f", 3) if where else (n, "r", 0),)
        )
        plan.step(
            (n, "t", where),
            functools.partial(add, part(0, where), up, down),
            ((n, "f", 0), (n, "u", where), (n, "d", where)),
        )
    totals = ((n, "t", 0), (n, "t", 1))
    ready = parts.at[j]
    if final is not None:
        ready = final

        def turn():
            for k in range(SIDE):
                final[k] = parts[j, k].astype(F32).T.astype(BF16).reshape(final.shape[1:])

        plan.step((n, "v"), turn, totals)
        totals = ((n, "v"),)
    for k in (1, 3, 2):
        plan.message(
            (n, "b", k), ready.at[wrap(i + k, SIDE)], out(i), g.along(cut, k),
            out(wrap(i - k, SIDE)), totals,
        )

    def own_rows():
        out(i)[...] = ready[i]

    plan.step((n, "b", 0), own_rows, totals)


def register(
    plan, g,
    enc_ref, hid_ref, gout_ref, wq_ref, wk_ref, wv_ref, wo_ref, rows_ref, slot_ref,
    out_ref, gh_ref, ge_ref,
    enc_all, hid_all, gout_all, wq, wk, wv, wo, kv_send, q_send, ga_send, own_k, own_v, stage_k, stage_v,
    k_in, v_in, q_ext, ga_ext, q_span, ga_span, probs, att, gq, tok_a, tok_c, got_a, got_c, reads,
    slot_out, slot_in, gkv, gkv_t, gkv_got, parts_c, parts_enc, one_a, two_a, one_c, two_c, one_enc, two_enc,
    final_c, final_enc, chain,
):
    scale = HEAD_DIM ** (-0.5)
    all_weights = {}
    for n, cut, own, full in (("K", "x", wk_ref, wk), ("V", "x", wv_ref, wv), ("Q", "z", wq_ref, wq), ("O", "z", wo_ref, wo)):
        all_weights[n] = add_weight(plan, g, n, cut, own, full, n == "O")
    enc = add_gather(plan, g, "E", "x", "z", enc_ref, enc_all)
    hid = add_gather(plan, g, "H", "z", "x", hid_ref, hid_all)
    gout = add_gather(plan, g, "G", "z", "x", gout_ref, gout_all)

    per = EQ // RLEN
    for n, full, own, stage, sender, land in (
        ("K", wk, own_k, stage_k, kv_send.at[0], k_in), ("V", wv, own_v, stage_v, kv_send.at[1], v_in)
    ):
        def rows(i, own=own):
            return own.at[pl.ds(i * per, per)]

        made = add_project(
            plan, g, n, "x", "z", enc_all, enc, full, all_weights[n], False, rows, sender
        )

        def pick(own=own, stage=stage, land=land):
            @pl.loop(0, NSEQ)
            def _(r):
                for s in range(2):
                    stage[r, s] = own[jnp.maximum(rows_ref[0, 2 * r + s], 0)]

            land[g.seq] = stage[g.seq]

        plan.step((n, "x"), pick, tuple(made))
        for k in range(1, NSEQ):
            plan.message(
                (n, "a", k), stage.at[wrap(g.seq + k, NSEQ)], land.at[g.seq], g.along("seq", k),
                land.at[wrap(g.seq - k, NSEQ)], ((n, "x"),),
            )

    head, tail = pl.ds(0, SPAN), pl.ds(ROWS, SPAN)
    row = col = None

    def shift_rows(by, limit=None):
        row = lax.broadcasted_iota(jnp.int32, (Q, Q + SPAN), 0)
        col = lax.broadcasted_iota(jnp.int32, (Q, Q + SPAN), 1)
        picked = col == row + by
        if limit is not None:
            picked = jnp.logical_and(picked, col < limit)
        return picked.astype(BF16)

    for n, buf, have, full, ext, span, sender in (
        ("Q", hid_all, hid, wq, q_ext, q_span, q_send), ("O", gout_all, gout, wo, ga_ext, ga_span, ga_send)
    ):
        def rows(i, ext=ext):
            return ext.at[pl.ds(pl.multiple_of(i * Q, Q), Q)]

        made = add_project(
            plan, g, n, "z", "x", buf, have, full, all_weights[n], n == "O", rows, sender
        )
        plan.message(
            (n, "e"), ext.at[head], ext.at[tail], g.along("seq", NSEQ - 1), ext.at[tail], tuple(made)
        )

        def align(ext=ext, span=span):
            for m in range(SIDE):
                limit = None
                if m == SIDE - 1:
                    limit = jnp.where(g.seq == NSEQ - 1, Q, Q + SPAN)
                moved = jnp.dot(
                    shift_rows(SPAN - 1, limit), ext[m * Q : (m + 1) * Q + SPAN, :],
                    preferred_element_type=F32,
                )
                span[m * Q : (m + 1) * Q, :] = moved.astype(BF16)

        plan.step((n, "t"), align, tuple(made) + ((n, "e"),))

    def tables():
        for kind in range(2):
            reads[kind, NONE] = jnp.zeros((RLEN, HEAD_DIM), F32)
        ids = [slot_ref[p // NEIGH, p % NEIGH] for p in range(NONE)]
        targets = [rows_ref[0, j] for j in range(NONE)]
        for line, values in ((0, ids), (2, targets)):
            for p in range(NONE):
                before, latest = jnp.int32(NONE), jnp.int32(NONE)
                for q in range(NONE):
                    if q < p:
                        before = jnp.where(values[q] == values[p], q, before)
                    latest = jnp.where(values[q] == p, q, latest)
                chain[line, p] = before
                chain[line + 1, p] = latest

    plan.step(("T", "t"), tables)

    def read(ref, u, cols):
        picked = []
        for j in range(NEIGH):
            s = slot_ref[u, j]
            picked.append(ref[lax.div(s, 2), lax.rem(s, 2), :, cols])
        return jnp.concatenate(picked, 0)

    def forward(h):
        cols = slice(h * HEAD_DIM, (h + 1) * HEAD_DIM)

        def work():
            @pl.loop(0, SPANS, unroll=UNROLL)
            def _(u):
                here = pl.ds(pl.multiple_of(u * SPAN, SPAN), SPAN)
                k, v = read(k_in, u, cols), read(v_in, u, cols)
                scores = lax.dot_general(
                    q_span[here, cols], k, NT_DIMS, preferred_element_type=F32
                ) * scale
                peak = jnp.max(scores, axis=-1, keepdims=True)
                weights = jnp.exp(scores - peak)
                prob = weights / jnp.sum(weights, axis=-1, keepdims=True)
                probs[h, u] = prob
                context = jnp.dot(prob.astype(BF16), v, preferred_element_type=F32)
                att[pl.ds(pl.multiple_of(u * SPAN, SPAN) + SPAN, SPAN), cols] = context.astype(BF16)

        return work

    def backward(h):
        cols = slice(h * HEAD_DIM, (h + 1) * HEAD_DIM)

        def work():
            @pl.loop(0, SPANS, unroll=UNROLL)
            def _(u):
                here = pl.ds(pl.multiple_of(u * SPAN, SPAN), SPAN)
                k, v = read(k_in, u, cols), read(v_in, u, cols)
                prob = probs[h, u]
                q, gr = q_span[here, cols], ga_span[here, cols]
                grad_probs = lax.dot_general(gr, v, NT_DIMS, preferred_element_type=F32)
                dot_sum = jnp.sum(grad_probs * prob, axis=-1, keepdims=True)
                grad_scores = (prob * (grad_probs - dot_sum) * scale).astype(BF16)
                grad_q = jnp.dot(grad_scores, k, preferred_element_type=F32)
                gq[pl.ds(pl.multiple_of(u * SPAN, SPAN) + SPAN, SPAN), cols] = grad_q.astype(BF16)
                grad_k = lax.dot_general(grad_scores, q, TN_DIMS, preferred_element_type=F32)
                grad_v = lax.dot_general(
                    prob.astype(BF16), gr, TN_DIMS, preferred_element_type=F32
                )
                for j in range(NEIGH):
                    part = slice(j * RLEN, (j + 1) * RLEN)
                    p = NEIGH * u + j
                    before = chain[0, p]
                    reads[0, p] = grad_k[part] + reads[0, before]
                    reads[1, p] = grad_v[part] + reads[1, before]

            @pl.loop(0, SLOTS)
            def _(s):
                latest = chain[1, s]
                for r in range(2):
                    for kind in range(2):
                        slot_out[h, r, lax.div(s, 2), lax.rem(s, 2), kind] = reads[
                            kind, latest, r * HALF : (r + 1) * HALF, :
                        ].astype(BF16)

            for r in range(2):
                slot_in[h, r, g.seq] = slot_out[h, r, g.seq]

        return work

    landed = tuple((n, "a", k) for n in "KV" for k in range(1, NSEQ)) + (("K", "x"), ("V", "x"))
    for h in range(HEADS):
        plan.step(("F", h), forward(h), landed + (("Q", "t"),))
    for h in range(HEADS):
        plan.step(("B", h), backward(h), (("F", h), ("O", "t"), ("T", "t")))
        for r in range(2):
            for k in range(1, NSEQ):
                plan.message(
                    ("S", h, r, "a", k), slot_out.at[h, r, wrap(g.seq + k, NSEQ)], slot_in.at[h, r, g.seq],
                    g.along("seq", k), slot_in.at[h, r, wrap(g.seq - k, NSEQ)], (("B", h),),
                )

    last = pl.ds(ROWS, SPAN)

    def out_part(t):
        depth = pl.ds(pl.multiple_of(t * W, W), W)
        return sum(
            jnp.dot(got_a[k], wo[k, :, depth], preferred_element_type=F32) for k in range(SIDE)
        )

    def hidden_part(t):
        depth = pl.ds(pl.multiple_of(t * W, W), W)
        return sum(
            jnp.dot(wq[k, depth, :], got_c[k], preferred_element_type=F32)
            for k in range(SIDE)
        )

    gone = [("H", "f", d) for d in OFFSETS]
    gone += [("H", "s", d, sign) for d in (1, 2, 3) for sign in "+-"]
    for n, src, made, make, tok, got, parts, one, two, result, old, final in (
        ("A", att, (("F", 0), ("F", 1)), out_part, tok_a, got_a, hid_all, one_a, two_a, out_ref, tuple(gone), None),
        ("C", gq, (("B", 0), ("B", 1)), hidden_part, tok_c, got_c, parts_c, one_c, two_c, gh_ref, (), final_c),
    ):
        plan.message((n, "e"), src.at[last], src.at[head], g.along("seq", 1), src.at[head], made)

        def align(src=src, tok=tok, final=final):
            @pl.when(g.seq == 0)
            def _():
                src[head, :] = jnp.zeros((SPAN, W), BF16)

            for m in range(SIDE):
                moved = jnp.dot(
                    shift_rows(1), src[m * Q : (m + 1) * Q + SPAN, :], preferred_element_type=F32
                )
                tok[m] = (moved if final is None else moved.T).astype(BF16)

        plan.step((n, "t"), align, made + ((n, "e"),))

        def rows(i, result=result):
            return result.at[pl.ds(pl.multiple_of(i * Q, Q), Q)]

        add_scatter(
            plan, g, n, "z", "x", tok, (n, "t"), got, parts, one, two, make, rows, old, final
        )

    def owner_sums(r):
        def work():
            @pl.loop(0, NSEQ)
            def _(o):
                for slot in range(2):
                    p = 2 * o + slot
                    before = chain[2, p]
                    for kind in range(2):
                        for h in range(HEADS):
                            rows = slice(h * HALF, (h + 1) * HALF)
                            value = slot_in[h, r, o, slot, kind].astype(F32)
                            reads[kind, p, rows, :] = value + reads[kind, before, rows, :]

            for n in range(NSEQ):
                latest = chain[3, n]
                for kind in range(2):
                    for h in range(HEADS):
                        rows = slice(h * HALF, (h + 1) * HALF)
                        cols = slice(h * HEAD_DIM, (h + 1) * HEAD_DIM)
                        place = slice((n % per) * HALF, (n % per + 1) * HALF)
                        gkv[n // per, kind, place, cols] = reads[kind, latest, rows, :].astype(BF16)
            for k in range(SIDE):
                for kind in range(2):
                    gkv_t[r, k, kind] = gkv[k, kind].astype(F32).T.astype(BF16)

        return work

    def enc_part(r):
        def make(t):
            depth = pl.ds(pl.multiple_of(t * W, W), W)
            total = None
            for kind, w in ((0, wk), (1, wv)):
                for k in range(SIDE):
                    term = jnp.dot(
                        w[k, depth, :], gkv_got[r, k, kind], preferred_element_type=F32
                    )
                    total = term if total is None else total + term
            return total

        return make

    for r in range(2):
        came = tuple(("S", h, r, "a", k) for h in range(HEADS) for k in range(1, NSEQ))
        plan.step(("W", r), owner_sums(r), came + (("B", 0), ("B", 1)))

        def rows(i, r=r):
            return ge_ref.at[pl.ds(i * per, per), pl.ds(r * HALF, HALF)]

        add_scatter(
            plan, g, ("Y", r), "x", "z", gkv_t.at[r], ("W", r), gkv_got.at[r], parts_enc.at[r],
            one_enc.at[r], two_enc.at[r], enc_part(r), rows, (), final_enc.at[r],
        )


def kernel(*refs):
    *refs, send, recv, local = refs
    g = Grid()
    plan = Plan(send, recv, local)
    register(plan, g, *refs)
    names = list(plan.actions)
    assert sorted(ORDER) == list(range(len(names)))
    g.barrier()
    for number in ORDER:
        plan.run(names[number])
    plan.finish()


def scratch():
    def vmem(*dims, dtype=BF16):
        return pltpu.VMEM(dims, dtype)

    weight = vmem(SIDE, NT * W, W)
    quarters = vmem(SIDE, Q, W)
    return [
        vmem(SIDE, SIDE, EQ, W), vmem(SIDE, SIDE, Q, W), vmem(SIDE, SIDE, Q, W),
        weight, weight, weight, vmem(SIDE, W, NT * W),
        vmem(2, SIDE, EQ // RLEN, RLEN, W), quarters, quarters,
        vmem(NSEQ, RLEN, W), vmem(NSEQ, RLEN, W),
        vmem(NSEQ, 2, RLEN, W), vmem(NSEQ, 2, RLEN, W), vmem(NSEQ, 2, RLEN, W), vmem(NSEQ, 2, RLEN, W),
        vmem(ROWS + SPAN, W), vmem(ROWS + SPAN, W), vmem(ROWS, W), vmem(ROWS, W),
        vmem(HEADS, SPANS, SPAN, NEIGH * RLEN, dtype=F32),
        vmem(ROWS + SPAN, W), vmem(ROWS + SPAN, W),
        quarters, vmem(SIDE, W, Q), quarters, vmem(SIDE, W, Q),
        vmem(2, NONE + 1, RLEN, HEAD_DIM, dtype=F32),
        vmem(HEADS, 2, NSEQ, 2, 2, HALF, HEAD_DIM), vmem(HEADS, 2, NSEQ, 2, 2, HALF, HEAD_DIM),
        vmem(SIDE, 2, Q, W), vmem(2, SIDE, 2, W, Q), vmem(2, SIDE, 2, W, Q),
        vmem(SIDE, SIDE, W, Q), vmem(2, SIDE, SIDE, W, Q),
        vmem(2, 2, Q, W), vmem(2, SIDE, Q, W), vmem(2, 2, W, Q), vmem(2, SIDE, W, Q),
        vmem(2, 2, 2, W, Q), vmem(2, 2, SIDE, W, Q),
        quarters, vmem(2, SIDE, 2, HALF, W), pltpu.SMEM((4, NONE), jnp.int32),
    ]


def shape(*dims, dtype=BF16):
    return jax.ShapeDtypeStruct(dims, dtype)


def per_device(hidden, encoded, w_query, w_key, w_value, w_out, send_rows, read_slot, grad_out):
    dma = pltpu.SemaphoreType.DMA
    out, gh, ge = pl.pallas_call(
        kernel,
        name="cross_attention",
        out_shape=(shape(ROWS, W), shape(ROWS, W), shape(NSEQ, RLEN, W)),
        in_specs=[ANY] * 7 + [SM, SM],
        out_specs=(VM, VM, VM),
        scratch_shapes=scratch() + [dma((MESSAGES,)), dma((MESSAGES,)), dma((7,))],
        compiler_params=pltpu.CompilerParams(
            collective_id=0, has_side_effects=True, vmem_limit_bytes=63 * 1024 * 1024
        ),
    )(
        encoded.reshape(2 * ROWS, W), hidden, grad_out, w_query, w_key, w_value, w_out, send_rows, read_slot,
    )
    return out, gh, ge


def solution(mesh):
    placed = (
        P("seq", "tensor"),
        P("seq", None, "tensor"),
        P(None, "tensor"),
        P(None, "tensor"),
        P(None, "tensor"),
        P("tensor", None),
        P("seq", None),
        P("seq", None),
        P("seq", "tensor"),
    )
    return jax.shard_map(
        per_device,
        mesh=mesh,
        in_specs=placed,
        out_specs=(P("seq", "tensor"), P("seq", "tensor"), P("seq", None, "tensor")),
        check_vma=False,
    )
```

```python
import functools

import jax
import jax.numpy as jnp
from jax import lax
from jax.experimental import pallas as pl
from jax.experimental.pallas import tpu as pltpu
from jax.sharding import PartitionSpec as P

SPAN = 64
NEIGH = 2
RLEN = 128
HEAD_DIM = 128
NSEQ = 8
SIDE = 4
NT = SIDE * SIDE
W = 256
ROWS = 512
Q = ROWS // SIDE
EQ = 2 * ROWS // SIDE
MESH = pl.DeviceIdType.MESH
ANY = pl.BlockSpec(memory_space=pl.ANY)
VM = pl.BlockSpec(memory_space=pltpu.VMEM)
SM = pl.BlockSpec(memory_space=pltpu.SMEM)
F32 = jnp.float32
BF16 = jnp.bfloat16
NT_DIMS = (((1,), (1,)), ((), ()))
TN_DIMS = (((0,), (0,)), ((), ()))
SPANS = ROWS // SPAN
SLOTS = 2 * NSEQ
HEADS = W // HEAD_DIM
HALF = RLEN // 2
NONE = SPANS * NEIGH
OFFSETS = (0, 3, 1, 2)
SHARES = {"K": (256,), "V": (256,), "Q": (), "O": (256,)}
ALONE = 512
UNROLL = 2


ORDER = (
    0, 32, 64, 93, 125, 157, 189, 218, 250, 266, 282, 2, 253, 1, 26, 268, 19, 94, 251, 34, 252, 112, 95, 118,
    33, 244, 25, 50, 66, 119, 243, 111, 283, 254, 394, 267, 98, 99, 87, 3, 5, 6, 275, 7, 8, 101, 100, 36, 39,
    40, 35, 38, 18, 37, 65, 104, 4, 42, 41, 116, 255, 57, 58, 261, 248, 70, 123, 68, 23, 21, 259, 51, 258, 28,
    114, 286, 288, 271, 151, 12, 11, 27, 105, 52, 126, 272, 256, 262, 260, 44, 10, 144, 9, 257, 54, 30, 43,
    91, 115, 122, 46, 108, 67, 72, 69, 29, 247, 45, 15, 13, 20, 158, 22, 47, 14, 49, 97, 109, 80, 48, 127, 17,
    287, 16, 294, 143, 31, 274, 130, 128, 270, 131, 71, 205, 264, 265, 60, 62, 183, 73, 136, 96, 86, 263, 113,
    79, 53, 55, 120, 74, 163, 160, 150, 153, 273, 155, 76, 162, 61, 59, 182, 24, 159, 146, 148, 129, 132, 133,
    176, 140, 168, 103, 219, 102, 137, 82, 84, 246, 280, 278, 175, 172, 107, 106, 141, 117, 236, 134, 289,
    135, 110, 207, 237, 209, 245, 63, 56, 197, 138, 139, 279, 220, 161, 165, 164, 145, 147, 75, 269, 77, 223,
    224, 314, 316, 318, 313, 317, 315, 319, 301, 187, 295, 81, 298, 167, 229, 186, 152, 169, 185, 303, 249,
    180, 178, 331, 343, 90, 89, 221, 121, 299, 226, 225, 149, 88, 284, 285, 328, 78, 179, 304, 83, 198, 302,
    184, 222, 241, 204, 300, 276, 166, 171, 211, 191, 177, 277, 332, 212, 173, 230, 344, 320, 324, 322, 326,
    321, 170, 327, 325, 323, 346, 85, 156, 190, 201, 345, 142, 238, 199, 347, 234, 233, 333, 124, 227, 228,
    239, 334, 281, 174, 92, 240, 291, 290, 293, 292, 154, 305, 310, 307, 309, 311, 308, 312, 181, 188, 306,
    329, 232, 330, 231, 361, 348, 358, 242, 206, 376, 297, 208, 200, 296, 363, 364, 195, 193, 216, 192, 194,
    362, 349, 335, 340, 337, 341, 342, 336, 339, 338, 215, 359, 360, 214, 235, 213, 202, 377, 370, 368, 379,
    367, 369, 372, 373, 378, 203, 388, 210, 371, 386, 387, 365, 350, 354, 196, 217, 380, 385, 355, 352, 351,
    390, 391, 353, 356, 357, 389, 366, 374, 395, 381, 382, 392, 375, 397, 403, 402, 400, 383, 398, 401, 404,
    409, 393, 399, 407, 411, 406, 405, 410, 408, 384, 396, 412, 422, 424, 425, 427, 420, 451, 413, 421, 415,
    426, 428, 429, 423, 431, 418, 476, 480, 481, 478, 479, 505, 510, 509, 507, 508, 452, 455, 453, 454, 456,
    417, 414, 430, 416, 419, 432, 506, 511, 513, 514, 512, 435, 460, 477, 484, 482, 485, 434, 483, 457, 462,
    436, 433, 437, 438, 458, 465, 445, 459, 515, 520, 519, 518, 517, 527, 516, 523, 441, 469, 461, 486, 522,
    491, 490, 526, 488, 498, 521, 524, 489, 487, 494, 439, 442, 464, 468, 440, 444, 463, 466, 493, 497, 492,
    495, 528, 443, 525, 529, 532, 531, 533, 530, 470, 446, 448, 447, 467, 471, 474, 472, 475, 499, 496, 500,
    502, 503, 504, 501, 473, 450, 449,
)
MESSAGES = 427


def wrap(value, count):
    return lax.rem(value + count, count)


class Grid:
    def __init__(self):
        self.seq = lax.axis_index("seq")
        tensor = lax.axis_index("tensor")
        self.z = lax.div(tensor, SIDE)
        self.x = lax.rem(tensor, SIDE)
        self.y = lax.div(self.seq, 2)
        self.core = lax.rem(self.seq, 2)

    def at(self, axis):
        return self.z if axis == "z" else self.x

    def along(self, axis, step):
        if axis == "z":
            return {"tensor": wrap(self.z + step, SIDE) * SIDE + self.x}
        if axis == "x":
            return {"tensor": self.z * SIDE + wrap(self.x + step, SIDE)}
        if axis == "y":
            return {"seq": wrap(self.y + step, SIDE) * 2 + self.core}
        if axis == "core":
            return {"seq": self.y * 2 + (1 - self.core)}
        return {"seq": wrap(self.seq + step, NSEQ)}

    def barrier(self):
        sem = pltpu.get_barrier_semaphore()
        peers = [self.along(axis, k) for axis in "zx" for k in range(1, SIDE)]
        peers += [self.along("seq", k) for k in range(1, NSEQ)]
        for peer in peers:
            pl.semaphore_signal(sem, inc=1, device_id=peer, device_id_type=MESH)
        pl.semaphore_wait(sem, len(peers))


class Plan:
    def __init__(self, send, recv, local):
        self.send, self.recv, self.local = send, recv, local
        self.actions, self.copies, self.landed, self.left = {}, {}, set(), set()
        self.messages = self.locals = 0

    def message(self, name, src, dst, peer, land, after=()):
        self.actions[name] = ("message", (src, dst, peer, land, self.messages), after, ())
        self.messages += 1

    def step(self, name, work, after=(), sent=()):
        self.actions[name] = ("step", work, after, sent)

    def load(self, name, src, dst):
        self.actions[name] = ("load", (src, dst, self.locals), (), ())
        self.locals += 1

    def need(self, name):
        if name in self.landed:
            return
        kind, data, _, _ = self.actions[name]
        assert name in self.copies, name
        if kind == "message":
            land = data[3]
            pltpu.make_async_copy(land, land, self.recv.at[data[4]]).wait()
        else:
            self.copies[name].wait()
        self.landed.add(name)

    def leave(self, name):
        if name not in self.left:
            self.copies[name].wait_send()
            self.left.add(name)

    def run(self, name):
        kind, data, after, sent = self.actions[name]
        for other in after:
            self.need(other)
        for other in sent:
            self.leave(other)
        if kind == "message":
            src, dst, peer, _, number = data
            copy = pltpu.make_async_remote_copy(
                src_ref=src,
                dst_ref=dst,
                send_sem=self.send.at[number],
                recv_sem=self.recv.at[number],
                device_id=peer,
                device_id_type=MESH,
            )
            copy.start()
            self.copies[name] = copy
        elif kind == "load":
            src, dst, number = data
            copy = pltpu.make_async_copy(src, dst, self.local.at[number])
            copy.start()
            self.copies[name] = copy
        else:
            data()
            self.landed.add(name)

    def finish(self):
        for name, (kind, _, _, _) in self.actions.items():
            if kind != "step":
                self.need(name)
            if kind == "message":
                self.leave(name)


def signs():
    return (("+", 1), ("-", -1))


def add_gather(plan, g, n, cut, ring, own, buf):
    rows = buf.shape[2]
    i, j = g.at(cut), g.at(ring)

    def slot(dj, di):
        return buf.at[wrap(j + dj, SIDE), wrap(i + di, SIDE)]

    def quarter(di):
        return own.at[pl.ds(pl.multiple_of(wrap(i + di, SIDE) * rows, rows), rows)]

    plan.load((n, "l"), quarter(0), slot(0, 0))
    for k in (1, 3, 2):
        plan.message((n, "x", k), quarter(k), slot(0, 0), g.along(cut, k), slot(0, SIDE - k))
    for d in OFFSETS:
        src, after = (slot(0, d), ((n, "x", SIDE - d),)) if d else (quarter(0), ())
        for sign, step in signs():
            plan.message(
                (n, "s", d, sign), src, slot(0, d), g.along(ring, step), slot(-step + SIDE, d), after
            )
    for d in OFFSETS:
        sign, step = ("+", 1) if d in (0, 1) else ("-", -1)
        block = slot(SIDE - step, d)
        plan.message((n, "f", d), block, block, g.along(ring, step), slot(2, d), ((n, "s", d, sign),))
    names = [(n, "l")] + [(n, "x", k) for k in (1, 2, 3)] + [(n, "f", d) for d in OFFSETS]
    return names + [(n, "s", d, sign) for d in OFFSETS for sign in "+-"]


def add_weight(plan, g, n, h, cut, own, full, wide):
    i = g.at(cut)
    needs = {e: [] for e in OFFSETS}
    mine = pl.ds(h * HEAD_DIM, HEAD_DIM)

    def cutout(ref, start, size):
        rows = pl.ds(pl.multiple_of(start, 128), size)
        return ref.at[mine, rows] if wide else ref.at[rows, mine]

    plan.load((n, h, "l"), cutout(own, 0, NT * W), cutout(full.at[i], 0, NT * W))
    needs[0].append((n, h, "l"))

    def add_piece(p, begin, size, shared):
        half = SIDE * size if shared else size
        other = begin + (1 - g.core) * half
        region = begin + g.core * half

        def chunk(dy):
            return region + wrap(g.y + dy, SIDE) * size if shared else region

        def at(e, start, length=size):
            return cutout(full.at[wrap(i + e, SIDE)], start, length)

        def ends(sign):
            return 0 if sign == "+" else size // 2

        here = chunk(0)
        for sign, step in signs():
            plan.message(
                (p, "n", sign), cutout(own, here, size), at(0, here), g.along(cut, step),
                at(SIDE - step, here),
            )
        for sign, step in signs():
            part = at(SIDE - step, here + ends(sign), size // 2)
            plan.message(
                (p, "h", sign), part, part, g.along(cut, step), at(2, here + ends(sign), size // 2),
                ((p, "n", sign),),
            )
        have = {3: [(p, "n", "+")], 1: [(p, "n", "-")], 2: [(p, "h", "+"), (p, "h", "-")]}
        if shared:
            for e in (3, 1, 2):
                for sign, step in signs():
                    plan.message(
                        (p, "y", e, sign), at(e, here), at(e, here), g.along("y", step),
                        at(e, chunk(SIDE - step)), tuple(have[e]),
                    )
            for e, sign, step, length in ((3, "+", 1, size), (1, "-", -1, size), (2, "+", 1, size // 2), (2, "-", -1, size // 2)):
                off = ends(sign) if e == 2 else 0
                part = at(e, chunk(SIDE - step) + off, length)
                plan.message(
                    (p, "z", e, sign), part, part, g.along("y", step), at(e, chunk(2) + off, length),
                    ((p, "y", e, sign),),
                )
            for e, last in ((3, "+"), (1, "-"), (2, "+-")):
                have[e] += [(p, "y", e, "+"), (p, "y", e, "-")] + [(p, "z", e, sign) for sign in last]
        for e in (3, 1, 2):
            block = at(e, region, half)
            plan.message(
                (p, "c", e), block, block, g.along("core", 1), at(e, other, half), tuple(have[e])
            )
            needs[e] += have[e] + [(p, "c", e)]

    begin = 0
    for count, size in enumerate(SHARES[n]):
        add_piece((n, h, count), begin, size, True)
        begin += 2 * SIDE * size
    while begin < NT * W:
        add_piece((n, h, begin // (2 * ALONE) + 8), begin, ALONE, False)
        begin += 2 * ALONE
    return needs


def lanes(blocks):
    return jnp.concatenate(blocks, 1)


def add_project(plan, g, n, h, cut, ring, buf, have, full, needs, wide, dst, sender):
    i = g.at(cut)
    mine = slice(h * HEAD_DIM, (h + 1) * HEAD_DIM)

    def columns(e):
        at = wrap(i + e, SIDE)
        total = None
        for m in range(SIDE):
            if ring == "z":
                left = lanes([buf[m, k] for k in range(SIDE)])
            else:
                left = lanes([buf[k, m] for k in range(SIDE)])
            depth = pl.ds(m * SIDE * W, SIDE * W)
            if wide:
                term = lax.dot_general(left, full[at, mine, depth], NT_DIMS, preferred_element_type=F32)
            else:
                term = jnp.dot(left, full[at, depth, mine], preferred_element_type=F32)
            total = term if total is None else total + term
        return total.astype(BF16)

    def make(e):
        def work():
            if e:
                sender[e] = columns(e).reshape(sender.shape[1:])
            else:
                dst(i)[...] = columns(e).reshape(sender.shape[1:])

        return work

    for e in OFFSETS:
        plan.step((n, h, "p", e), make(e), tuple(have + needs[e]))
        if e:
            plan.message(
                (n, h, "o", e), sender.at[e], dst(i), g.along(cut, e), dst(wrap(i - e, SIDE)),
                ((n, h, "p", e),),
            )
    return [(n, h, "p", 0)] + [(n, h, "o", e) for e in (1, 2, 3)]


def add_scatter(plan, g, n, cut, ring, swaps, parts, one, two, make, out, old=(), final=None):
    i, j = g.at(cut), g.at(ring)
    swapped = ()
    for count, (own, own_step, got) in enumerate(swaps):
        def keep(own=own, got=got):
            got[i] = own[i]

        plan.step((n, "k", count), keep, (own_step,))
        for k in (1, 3, 2):
            peer = wrap(i + k, SIDE)
            plan.message(
                (n, "x", count, k), own.at[peer], got.at[i], g.along(cut, k), got.at[wrap(i - k, SIDE)],
                (own_step,),
            )
        swapped += ((n, "k", count),) + tuple((n, "x", count, k) for k in (1, 2, 3))

    def part(dj, where=None):
        block = parts.at[wrap(j + dj, SIDE)]
        return block if where is None else block.at[pl.ds(2 * where, 2)]

    def fill(dj):
        def work():
            row = wrap(j + dj, SIDE)

            @pl.loop(0, SIDE)
            def _(k):
                t = row * SIDE + k if ring == "z" else k * SIDE + row
                parts[row, k] = make(t).astype(BF16)

        return work

    def add(ref, *others):
        total = ref[...].astype(F32)
        for other in others:
            total = total + other[...].astype(F32)
        ref[...] = total.astype(BF16)

    for dj in (2, 1, 3, 0):
        plan.step((n, "f", dj), fill(dj), swapped, old)
    plan.message((n, "n", 0), part(2, 0), one.at[0], g.along(ring, -1), one.at[0], ((n, "f", 2),))
    plan.message((n, "n", 1), part(2, 1), one.at[1], g.along(ring, 1), one.at[1], ((n, "f", 2),))
    plan.step((n, "r", 0), lambda: add(part(3, 0), one.at[0]), ((n, "f", 3), (n, "n", 0)))
    plan.step((n, "r", 1), lambda: add(part(1, 1), one.at[1]), ((n, "f", 1), (n, "n", 1)))
    for where in range(2):
        half = pl.ds(2 * where, 2)
        up, down = two.at[0, half], two.at[1, half]
        plan.message(
            (n, "u", where), part(1, where), up, g.along(ring, 1), up, ((n, "r", 1) if where else (n, "f", 1),)
        )
        plan.message(
            (n, "d", where), part(3, where), down, g.along(ring, -1), down, ((n, "f", 3) if where else (n, "r", 0),)
        )
        plan.step(
            (n, "t", where),
            functools.partial(add, part(0, where), up, down),
            ((n, "f", 0), (n, "u", where), (n, "d", where)),
        )
    totals = ((n, "t", 0), (n, "t", 1))
    ready = parts.at[j]
    if final is not None:
        ready = final

        def turn():
            for k in range(SIDE):
                final[k] = parts[j, k].astype(F32).T.astype(BF16).reshape(final.shape[1:])

        plan.step((n, "v"), turn, totals)
        totals = ((n, "v"),)
    for k in (1, 3, 2):
        plan.message(
            (n, "b", k), ready.at[wrap(i + k, SIDE)], out(i), g.along(cut, k),
            out(wrap(i - k, SIDE)), totals,
        )

    def own_rows():
        out(i)[...] = ready[i]

    plan.step((n, "b", 0), own_rows, totals)


def register(
    plan, g,
    enc_ref, hid_ref, gout_ref, wq_ref, wk_ref, wv_ref, wo_ref, rows_ref, slot_ref,
    out_ref, gh_ref, ge_ref,
    enc_all, hid_all, gout_all, wq, wk, wv, wo, kv_send, q_send, ga_send, own_k0, own_k1, own_v0, own_v1,
    stage_k, stage_v, k_in0, k_in1, v_in0, v_in1, q_ext, ga_ext, q_span, ga_span, probs, att, gq, tok_a, tok_c, got_a, got_c, reads,
    slot_out, slot_in, gkv_t, gkv_got, parts_c, parts_enc, one_a, two_a, one_c, two_c, one_enc, two_enc,
    final_c, final_enc, chain,
):
    scale = HEAD_DIM ** (-0.5)
    k_in, v_in = (k_in0, k_in1), (v_in0, v_in1)
    all_weights = {}
    for h in range(HEADS):
        for n, cut, own, full in (
            ("K", "x", wk_ref, wk), ("V", "x", wv_ref, wv), ("Q", "z", wq_ref, wq), ("O", "z", wo_ref, wo)
        ):
            all_weights[n, h] = add_weight(plan, g, n, h, cut, own, full, n == "O")
    enc = add_gather(plan, g, "E", "x", "z", enc_ref, enc_all)
    hid = add_gather(plan, g, "H", "z", "x", hid_ref, hid_all)
    gout = add_gather(plan, g, "G", "z", "x", gout_ref, gout_all)

    per = EQ // RLEN
    for h in range(HEADS):
        for n, full, own, stage, sender, land in (
            ("K", wk, (own_k0, own_k1)[h], stage_k.at[h], kv_send.at[0, h], k_in[h]),
            ("V", wv, (own_v0, own_v1)[h], stage_v.at[h], kv_send.at[1, h], v_in[h]),
        ):
            def rows(i, own=own):
                return own.at[pl.ds(i * per, per)]

            made = add_project(
                plan, g, n, h, "x", "z", enc_all, enc, full, all_weights[n, h], False, rows, sender
            )

            def pick(own=own, stage=stage, land=land):
                @pl.loop(0, NSEQ)
                def _(r):
                    for s in range(2):
                        stage[r, s] = own[jnp.maximum(rows_ref[0, 2 * r + s], 0)]

                land[g.seq] = stage[g.seq]

            plan.step((n, h, "x"), pick, tuple(made))
            for k in range(1, NSEQ):
                plan.message(
                    (n, h, "a", k), stage.at[wrap(g.seq + k, NSEQ)], land.at[g.seq], g.along("seq", k),
                    land.at[wrap(g.seq - k, NSEQ)], ((n, h, "x"),),
                )

    head, tail = pl.ds(0, SPAN), pl.ds(ROWS, SPAN)
    def shift_rows(by, limit=None):
        row = lax.broadcasted_iota(jnp.int32, (Q, Q + SPAN), 0)
        col = lax.broadcasted_iota(jnp.int32, (Q, Q + SPAN), 1)
        picked = col == row + by
        if limit is not None:
            picked = jnp.logical_and(picked, col < limit)
        return picked.astype(BF16)

    for h in range(HEADS):
        for n, buf, have, full, ext, span, sender in (
            ("Q", hid_all, hid, wq, q_ext.at[h], q_span.at[h], q_send.at[h]),
            ("O", gout_all, gout, wo, ga_ext.at[h], ga_span.at[h], ga_send.at[h]),
        ):
            def rows(i, ext=ext):
                return ext.at[pl.ds(pl.multiple_of(i * Q, Q), Q)]

            made = add_project(
                plan, g, n, h, "z", "x", buf, have, full, all_weights[n, h], n == "O", rows, sender
            )
            plan.message(
                (n, h, "e"), ext.at[head], ext.at[tail], g.along("seq", NSEQ - 1), ext.at[tail], tuple(made)
            )

            def align(ext=ext, span=span):
                for m in range(SIDE):
                    limit = None
                    if m == SIDE - 1:
                        limit = jnp.where(g.seq == NSEQ - 1, Q, Q + SPAN)
                    moved = jnp.dot(
                        shift_rows(SPAN - 1, limit), ext[m * Q : (m + 1) * Q + SPAN, :],
                        preferred_element_type=F32,
                    )
                    span[m * Q : (m + 1) * Q, :] = moved.astype(BF16)

            plan.step((n, h, "t"), align, tuple(made) + ((n, h, "e"),))

    def tables():
        for kind in range(2):
            reads[kind, NONE] = jnp.zeros((RLEN, HEAD_DIM), F32)
        ids = [slot_ref[p % NEIGH, p // NEIGH] for p in range(NONE)]
        targets = [rows_ref[0, j] for j in range(NONE)]
        for line, values in ((0, ids), (2, targets)):
            for p in range(NONE):
                before, latest = jnp.int32(NONE), jnp.int32(NONE)
                for q in range(NONE):
                    if q < p:
                        before = jnp.where(values[q] == values[p], q, before)
                    latest = jnp.where(values[q] == p, q, latest)
                chain[line, p] = before
                chain[line + 1, p] = latest

    plan.step(("T", "t"), tables)

    def read(ref, u):
        picked = []
        for j in range(NEIGH):
            s = slot_ref[j, u]
            picked.append(ref[lax.div(s, 2), lax.rem(s, 2)])
        return jnp.concatenate(picked, 0)

    def forward(h):
        cols = slice(h * HEAD_DIM, (h + 1) * HEAD_DIM)

        def work():
            @pl.loop(0, SPANS, unroll=UNROLL)
            def _(u):
                here = pl.ds(pl.multiple_of(u * SPAN, SPAN), SPAN)
                k, v = read(k_in[h], u), read(v_in[h], u)
                scores = lax.dot_general(
                    q_span[h, here, :], k, NT_DIMS, preferred_element_type=F32
                ) * scale
                peak = jnp.max(scores, axis=-1, keepdims=True)
                weights = jnp.exp(scores - peak)
                prob = weights / jnp.sum(weights, axis=-1, keepdims=True)
                probs[h, u] = prob
                context = jnp.dot(prob.astype(BF16), v, preferred_element_type=F32)
                att[pl.ds(pl.multiple_of(u * SPAN, SPAN) + SPAN, SPAN), cols] = context.astype(BF16)

        return work

    def backward(h):
        cols = slice(h * HEAD_DIM, (h + 1) * HEAD_DIM)

        def work():
            @pl.loop(0, SPANS, unroll=UNROLL)
            def _(u):
                here = pl.ds(pl.multiple_of(u * SPAN, SPAN), SPAN)
                k, v = read(k_in[h], u), read(v_in[h], u)
                prob = probs[h, u]
                q, gr = q_span[h, here, :], ga_span[h, here, :]
                grad_probs = lax.dot_general(gr, v, NT_DIMS, preferred_element_type=F32)
                dot_sum = jnp.sum(grad_probs * prob, axis=-1, keepdims=True)
                grad_scores = (prob * (grad_probs - dot_sum) * scale).astype(BF16)
                grad_q = jnp.dot(grad_scores, k, preferred_element_type=F32)
                gq[pl.ds(pl.multiple_of(u * SPAN, SPAN) + SPAN, SPAN), cols] = grad_q.astype(BF16)
                grad_k = lax.dot_general(grad_scores, q, TN_DIMS, preferred_element_type=F32)
                grad_v = lax.dot_general(
                    prob.astype(BF16), gr, TN_DIMS, preferred_element_type=F32
                )
                for j in range(NEIGH):
                    part = slice(j * RLEN, (j + 1) * RLEN)
                    p = NEIGH * u + j
                    before = chain[0, p]
                    reads[0, p] = grad_k[part] + reads[0, before]
                    reads[1, p] = grad_v[part] + reads[1, before]

            @pl.loop(0, SLOTS)
            def _(s):
                latest = chain[1, s]
                for r in range(2):
                    for kind in range(2):
                        slot_out[h, r, lax.div(s, 2), lax.rem(s, 2), kind] = reads[
                            kind, latest, r * HALF : (r + 1) * HALF, :
                        ].astype(BF16)

            for r in range(2):
                slot_in[h, r, g.seq] = slot_out[h, r, g.seq]

        return work

    for h in range(HEADS):
        landed = tuple((n, h, "a", k) for n in "KV" for k in range(1, NSEQ))
        landed += tuple((n, h, "x") for n in "KV")
        plan.step(("F", h), forward(h), landed + (("Q", h, "t"),))
    for h in range(HEADS):
        plan.step(("B", h), backward(h), (("F", h), ("O", h, "t"), ("T", "t")))
        for r in range(2):
            for k in range(1, NSEQ):
                plan.message(
                    ("S", h, r, "a", k), slot_out.at[h, r, wrap(g.seq + k, NSEQ)], slot_in.at[h, r, g.seq],
                    g.along("seq", k), slot_in.at[h, r, wrap(g.seq - k, NSEQ)], (("B", h),),
                )

    last = pl.ds(ROWS, SPAN)

    def out_part(t):
        depth = pl.ds(pl.multiple_of(t * W, W), W)
        return sum(
            jnp.dot(got_a[k], wo[k, :, depth], preferred_element_type=F32) for k in range(SIDE)
        )

    def hidden_part(t):
        depth = pl.ds(pl.multiple_of(t * W, W), W)
        return sum(
            jnp.dot(wq[k, depth, :], got_c[k], preferred_element_type=F32)
            for k in range(SIDE)
        )

    gone = [("H", "f", d) for d in OFFSETS]
    gone += [("H", "s", d, sign) for d in (1, 2, 3) for sign in "+-"]
    for n, src, made, make, tok, got, parts, one, two, result, old, final in (
        ("A", att, (("F", 0), ("F", 1)), out_part, tok_a, got_a, hid_all, one_a, two_a, out_ref, tuple(gone), None),
        ("C", gq, (("B", 0), ("B", 1)), hidden_part, tok_c, got_c, parts_c, one_c, two_c, gh_ref, (), final_c),
    ):
        plan.message((n, "e"), src.at[last], src.at[head], g.along("seq", 1), src.at[head], made)

        def align(src=src, tok=tok, final=final):
            @pl.when(g.seq == 0)
            def _():
                src[head, :] = jnp.zeros((SPAN, W), BF16)

            for m in range(SIDE):
                moved = jnp.dot(
                    shift_rows(1), src[m * Q : (m + 1) * Q + SPAN, :], preferred_element_type=F32
                )
                tok[m] = (moved if final is None else moved.T).astype(BF16)

        plan.step((n, "t"), align, made + ((n, "e"),))

        def rows(i, result=result):
            return result.at[pl.ds(pl.multiple_of(i * Q, Q), Q)]

        add_scatter(
            plan, g, n, "z", "x", ((tok, (n, "t"), got),), parts, one, two, make, rows, old, final
        )

    def owner_sums(r, h):
        def work():
            rows = slice(h * HALF, (h + 1) * HALF)

            @pl.loop(0, NSEQ)
            def _(o):
                for slot in range(2):
                    p = 2 * o + slot
                    before = chain[2, p]
                    for kind in range(2):
                        value = slot_in[h, r, o, slot, kind].astype(F32)
                        reads[kind, p, rows, :] = value + reads[kind, before, rows, :]

            for k in range(SIDE):
                for kind in range(2):
                    owned = [reads[kind, chain[3, k * per + m], rows, :] for m in range(per)]
                    total = jnp.concatenate(owned, 0).astype(BF16).astype(F32)
                    gkv_t[r, h, k, kind] = total.T.astype(BF16)

        return work

    def enc_part(r):
        def make(t):
            depth = pl.ds(pl.multiple_of(t * W, W), W)
            total = None
            for kind, w in ((0, wk), (1, wv)):
                for k in range(SIDE):
                    right = jnp.concatenate([gkv_got[r, h, k, kind] for h in range(HEADS)], 0)
                    term = jnp.dot(w[k, depth, :], right, preferred_element_type=F32)
                    total = term if total is None else total + term
            return total

        return make

    for r in range(2):
        for h in range(HEADS):
            came = tuple(("S", h, r, "a", k) for k in range(1, NSEQ))
            plan.step(("W", h, r), owner_sums(r, h), came + (("B", h),))

        def rows(i, r=r):
            return ge_ref.at[pl.ds(i * per, per), pl.ds(r * HALF, HALF)]

        add_scatter(
            plan, g, ("Y", r), "x", "z",
            [(gkv_t.at[r, h], ("W", h, r), gkv_got.at[r, h]) for h in range(HEADS)], parts_enc.at[r],
            one_enc.at[r], two_enc.at[r], enc_part(r), rows, (), final_enc.at[r],
        )


def kernel(*refs):
    *refs, send, recv, local = refs
    g = Grid()
    plan = Plan(send, recv, local)
    register(plan, g, *refs)
    names = list(plan.actions)
    assert sorted(ORDER) == list(range(len(names)))
    g.barrier()
    for number in ORDER:
        plan.run(names[number])
    plan.finish()


def scratch():
    def vmem(*dims, dtype=BF16):
        return pltpu.VMEM(dims, dtype)

    weight = vmem(SIDE, NT * W, W)
    quarters = vmem(SIDE, Q, W)
    by_head = vmem(HEADS, SIDE, Q, HEAD_DIM)
    owned, came = vmem(NSEQ, RLEN, HEAD_DIM), vmem(NSEQ, 2, RLEN, HEAD_DIM)
    tokens = vmem(HEADS, ROWS + SPAN, HEAD_DIM)
    return [
        vmem(SIDE, SIDE, EQ, W), vmem(SIDE, SIDE, Q, W), vmem(SIDE, SIDE, Q, W),
        weight, weight, weight, vmem(SIDE, W, NT * W),
        vmem(2, HEADS, SIDE, EQ // RLEN, RLEN, HEAD_DIM), by_head, by_head,
        owned, owned, owned, owned,
        vmem(HEADS, NSEQ, 2, RLEN, HEAD_DIM), vmem(HEADS, NSEQ, 2, RLEN, HEAD_DIM), came, came, came, came,
        tokens, tokens, vmem(HEADS, ROWS, HEAD_DIM), vmem(HEADS, ROWS, HEAD_DIM),
        vmem(HEADS, SPANS, SPAN, NEIGH * RLEN, dtype=F32),
        vmem(ROWS + SPAN, W), vmem(ROWS + SPAN, W),
        quarters, vmem(SIDE, W, Q), quarters, vmem(SIDE, W, Q),
        vmem(2, NONE + 1, RLEN, HEAD_DIM, dtype=F32),
        vmem(HEADS, 2, NSEQ, 2, 2, HALF, HEAD_DIM), vmem(HEADS, 2, NSEQ, 2, 2, HALF, HEAD_DIM),
        vmem(2, HEADS, SIDE, 2, HEAD_DIM, Q), vmem(2, HEADS, SIDE, 2, HEAD_DIM, Q),
        vmem(SIDE, SIDE, W, Q), vmem(2, SIDE, SIDE, W, Q),
        vmem(2, 2, Q, W), vmem(2, SIDE, Q, W), vmem(2, 2, W, Q), vmem(2, SIDE, W, Q),
        vmem(2, 2, 2, W, Q), vmem(2, 2, SIDE, W, Q),
        quarters, vmem(2, SIDE, 2, HALF, W), pltpu.SMEM((4, NONE), jnp.int32),
    ]


def shape(*dims, dtype=BF16):
    return jax.ShapeDtypeStruct(dims, dtype)


def hand_over(*refs):
    *pairs, sem = refs
    copies = [
        pltpu.make_async_copy(src, dst, sem.at[k]) for k, (src, dst) in enumerate(zip(pairs[:3], pairs[3:]))
    ]
    for copy in copies:
        copy.start()
    for copy in copies:
        copy.wait()


def per_device(hidden, encoded, w_query, w_key, w_value, w_out, send_rows, read_slot, grad_out):
    dma = pltpu.SemaphoreType.DMA
    shapes = (shape(ROWS, W), shape(ROWS, W), shape(NSEQ, RLEN, W))
    results = pl.pallas_call(
        kernel,
        name="cross_attention",
        out_shape=shapes,
        in_specs=[ANY] * 7 + [SM, SM],
        out_specs=(VM, VM, VM),
        scratch_shapes=scratch() + [dma((MESSAGES,)), dma((MESSAGES,)), dma((11,))],
        compiler_params=pltpu.CompilerParams(
            collective_id=0, has_side_effects=True, vmem_limit_bytes=63 * 1024 * 1024
        ),
    )(
        encoded.reshape(2 * ROWS, W), hidden, grad_out, w_query, w_key, w_value, w_out, send_rows, read_slot.T,
    )
    return pl.pallas_call(
        hand_over,
        name="hand_over",
        out_shape=shapes,
        in_specs=[ANY] * 3,
        out_specs=(ANY,) * 3,
        scratch_shapes=[dma((3,))],
    )(*results)


def solution(mesh):
    placed = (
        P("seq", "tensor"),
        P("seq", None, "tensor"),
        P(None, "tensor"),
        P(None, "tensor"),
        P(None, "tensor"),
        P("tensor", None),
        P("seq", None),
        P("seq", None),
        P("seq", "tensor"),
    )
    return jax.shard_map(
        per_device,
        mesh=mesh,
        in_specs=placed,
        out_specs=(P("seq", "tensor"), P("seq", "tensor"), P("seq", None, "tensor")),
        check_vma=False,
    )
```

```python
import functools

import jax
import jax.numpy as jnp
from jax import lax
from jax.experimental import pallas as pl
from jax.experimental.pallas import tpu as pltpu
from jax.sharding import PartitionSpec as P

SPAN = 64
NEIGH = 2
RLEN = 128
HEAD_DIM = 128
NSEQ = 8
SIDE = 4
NT = SIDE * SIDE
W = 256
ROWS = 512
Q = ROWS // SIDE
EQ = 2 * ROWS // SIDE
MESH = pl.DeviceIdType.MESH
ANY = pl.BlockSpec(memory_space=pl.ANY)
VM = pl.BlockSpec(memory_space=pltpu.VMEM)
SM = pl.BlockSpec(memory_space=pltpu.SMEM)
F32 = jnp.float32
BF16 = jnp.bfloat16
NT_DIMS = (((1,), (1,)), ((), ()))
TN_DIMS = (((0,), (0,)), ((), ()))
SPANS = ROWS // SPAN
SLOTS = 2 * NSEQ
HEADS = W // HEAD_DIM
HALF = RLEN // 2
NONE = SPANS * NEIGH
OFFSETS = (0, 3, 1, 2)
SHARES = {"K": (256, 256), "V": (256,), "Q": (256,), "O": ()}
ALONE = 256
UNROLL = 2


ORDER = (
    0, 35, 81, 127, 184, 200, 216, 2, 185, 1, 19, 113, 18, 114, 188, 136, 280, 129, 106, 186, 4, 7, 8, 25,
    117, 115, 205, 21, 24, 116, 196, 53, 5, 191, 3, 187, 192, 110, 133, 131, 193, 6, 140, 75, 118, 190, 119,
    22, 54, 12, 60, 29, 164, 57, 55, 9, 82, 11, 23, 74, 198, 197, 221, 195, 194, 79, 77, 37, 28, 64, 58, 62,
    204, 20, 56, 16, 166, 10, 68, 67, 163, 78, 33, 86, 87, 13, 120, 189, 108, 199, 138, 14, 15, 36, 61, 26,
    212, 27, 39, 42, 70, 72, 168, 32, 69, 43, 76, 92, 177, 201, 100, 217, 17, 165, 218, 220, 235, 233, 232,
    124, 47, 71, 167, 107, 63, 236, 38, 40, 234, 31, 41, 224, 228, 65, 83, 202, 59, 207, 80, 84, 30, 225, 247,
    169, 156, 96, 142, 223, 128, 46, 66, 181, 34, 102, 44, 206, 45, 109, 150, 230, 208, 209, 88, 85, 89, 213,
    222, 111, 237, 238, 51, 229, 121, 99, 49, 144, 146, 50, 250, 135, 93, 251, 90, 91, 48, 143, 214, 132, 160,
    73, 248, 249, 152, 154, 130, 104, 112, 239, 245, 241, 242, 101, 219, 103, 123, 240, 125, 94, 246, 52, 137,
    95, 203, 122, 145, 178, 139, 134, 147, 252, 253, 157, 149, 226, 227, 105, 97, 244, 243, 170, 211, 210, 98,
    158, 171, 231, 254, 256, 260, 255, 126, 180, 215, 259, 141, 151, 179, 271, 257, 153, 182, 159, 261, 161,
    267, 268, 262, 263, 264, 265, 266, 173, 174, 175, 155, 172, 258, 183, 272, 273, 274, 275, 162, 148, 269,
    176, 276, 277, 270, 281, 278, 282, 313, 279, 298, 303, 302, 299, 301, 304, 314, 317, 309, 318, 300, 283,
    337, 289, 306, 284, 291, 315, 316, 311, 338, 340, 342, 288, 341, 287, 290, 339, 285, 308, 286, 319, 323,
    322, 324, 305, 320, 327, 321, 331, 343, 346, 345, 294, 355, 344, 310, 325, 328, 307, 296, 362, 326, 366,
    330, 293, 295, 363, 292, 312, 364, 297, 365, 329, 386, 387, 347, 389, 388, 332, 334, 333, 336, 367, 371,
    372, 335, 390, 368, 369, 379, 370, 348, 375, 351, 374, 373, 391, 395, 396, 378, 376, 393, 403, 392, 399,
    394, 350, 354, 349, 352, 397, 400, 398, 402, 380, 377, 381, 384, 385, 383, 382, 356, 353, 357, 361, 358,
    360, 359, 401, 404, 405, 408, 407, 409, 406,
)
MESSAGES = 331


def wrap(value, count):
    return lax.rem(value + count, count)


class Grid:
    def __init__(self):
        self.seq = lax.axis_index("seq")
        tensor = lax.axis_index("tensor")
        self.z = lax.div(tensor, SIDE)
        self.x = lax.rem(tensor, SIDE)
        self.y = lax.div(self.seq, 2)
        self.core = lax.rem(self.seq, 2)

    def at(self, axis):
        return self.z if axis == "z" else self.x

    def along(self, axis, step):
        if axis == "z":
            return {"tensor": wrap(self.z + step, SIDE) * SIDE + self.x}
        if axis == "x":
            return {"tensor": self.z * SIDE + wrap(self.x + step, SIDE)}
        if axis == "y":
            return {"seq": wrap(self.y + step, SIDE) * 2 + self.core}
        if axis == "core":
            return {"seq": self.y * 2 + (1 - self.core)}
        return {"seq": wrap(self.seq + step, NSEQ)}

    def barrier(self):
        sem = pltpu.get_barrier_semaphore()
        peers = [self.along(axis, k) for axis in "zx" for k in range(1, SIDE)]
        peers += [self.along("seq", k) for k in range(1, NSEQ)]
        for peer in peers:
            pl.semaphore_signal(sem, inc=1, device_id=peer, device_id_type=MESH)
        pl.semaphore_wait(sem, len(peers))


class Plan:
    def __init__(self, send, recv, local):
        self.send, self.recv, self.local = send, recv, local
        self.actions, self.copies, self.landed, self.left = {}, {}, set(), set()
        self.messages = self.locals = 0

    def message(self, name, src, dst, peer, land, after=()):
        self.actions[name] = ("message", (src, dst, peer, land, self.messages), after, ())
        self.messages += 1

    def step(self, name, work, after=(), sent=()):
        self.actions[name] = ("step", work, after, sent)

    def load(self, name, src, dst):
        self.actions[name] = ("load", (src, dst, self.locals), (), ())
        self.locals += 1

    def need(self, name):
        if name in self.landed:
            return
        kind, data, _, _ = self.actions[name]
        assert name in self.copies, name
        if kind == "message":
            land = data[3]
            pltpu.make_async_copy(land, land, self.recv.at[data[4]]).wait()
        else:
            self.copies[name].wait()
        self.landed.add(name)

    def leave(self, name):
        if name not in self.left:
            self.copies[name].wait_send()
            self.left.add(name)

    def run(self, name):
        kind, data, after, sent = self.actions[name]
        for other in after:
            self.need(other)
        for other in sent:
            self.leave(other)
        if kind == "message":
            src, dst, peer, _, number = data
            copy = pltpu.make_async_remote_copy(
                src_ref=src,
                dst_ref=dst,
                send_sem=self.send.at[number],
                recv_sem=self.recv.at[number],
                device_id=peer,
                device_id_type=MESH,
            )
            copy.start()
            self.copies[name] = copy
        elif kind == "load":
            src, dst, number = data
            copy = pltpu.make_async_copy(src, dst, self.local.at[number])
            copy.start()
            self.copies[name] = copy
        else:
            data()
            self.landed.add(name)

    def finish(self):
        for name, (kind, _, _, _) in self.actions.items():
            if kind != "step":
                self.need(name)
            if kind == "message":
                self.leave(name)


def signs():
    return (("+", 1), ("-", -1))


def add_gather(plan, g, n, cut, ring, own, buf):
    rows = buf.shape[2]
    i, j = g.at(cut), g.at(ring)

    def slot(dj, di):
        return buf.at[wrap(j + dj, SIDE), wrap(i + di, SIDE)]

    def quarter(di):
        return own.at[pl.ds(pl.multiple_of(wrap(i + di, SIDE) * rows, rows), rows)]

    plan.load((n, "l"), quarter(0), slot(0, 0))
    for k in (1, 3, 2):
        plan.message((n, "x", k), quarter(k), slot(0, 0), g.along(cut, k), slot(0, SIDE - k))
    for d in OFFSETS:
        src, after = (slot(0, d), ((n, "x", SIDE - d),)) if d else (quarter(0), ())
        for sign, step in signs():
            plan.message(
                (n, "s", d, sign), src, slot(0, d), g.along(ring, step), slot(-step + SIDE, d), after
            )
    for d in OFFSETS:
        sign, step = ("+", 1) if d in (0, 1) else ("-", -1)
        block = slot(SIDE - step, d)
        plan.message((n, "f", d), block, block, g.along(ring, step), slot(2, d), ((n, "s", d, sign),))
    names = [(n, "l")] + [(n, "x", k) for k in (1, 2, 3)] + [(n, "f", d) for d in OFFSETS]
    return names + [(n, "s", d, sign) for d in OFFSETS for sign in "+-"]


def add_weight(plan, g, n, cut, own, full, wide):
    i = g.at(cut)
    needs = {e: [] for e in OFFSETS}
    plan.load((n, "l"), own, full.at[i])
    needs[0].append((n, "l"))

    def cutout(ref, start, size):
        rows = pl.ds(pl.multiple_of(start, 128), size)
        return ref.at[:, rows] if wide else ref.at[rows]

    def add_piece(p, begin, size, shared):
        half = SIDE * size if shared else size
        other = begin + (1 - g.core) * half
        region = begin + g.core * half

        def chunk(dy):
            return region + wrap(g.y + dy, SIDE) * size if shared else region

        def at(e, start, length=size):
            return cutout(full.at[wrap(i + e, SIDE)], start, length)

        def ends(sign):
            return 0 if sign == "+" else size // 2

        here = chunk(0)
        for sign, step in signs():
            plan.message(
                (p, "n", sign), cutout(own, here, size), at(0, here), g.along(cut, step),
                at(SIDE - step, here),
            )
        for sign, step in signs():
            part = at(SIDE - step, here + ends(sign), size // 2)
            plan.message(
                (p, "h", sign), part, part, g.along(cut, step), at(2, here + ends(sign), size // 2),
                ((p, "n", sign),),
            )
        have = {3: [(p, "n", "+")], 1: [(p, "n", "-")], 2: [(p, "h", "+"), (p, "h", "-")]}
        if shared:
            for e in (3, 1, 2):
                for sign, step in signs():
                    plan.message(
                        (p, "y", e, sign), at(e, here), at(e, here), g.along("y", step),
                        at(e, chunk(SIDE - step)), tuple(have[e]),
                    )
            for e, sign, step, length in ((3, "+", 1, size), (1, "-", -1, size), (2, "+", 1, size // 2), (2, "-", -1, size // 2)):
                off = ends(sign) if e == 2 else 0
                part = at(e, chunk(SIDE - step) + off, length)
                plan.message(
                    (p, "z", e, sign), part, part, g.along("y", step), at(e, chunk(2) + off, length),
                    ((p, "y", e, sign),),
                )
            for e, last in ((3, "+"), (1, "-"), (2, "+-")):
                have[e] += [(p, "y", e, "+"), (p, "y", e, "-")] + [(p, "z", e, sign) for sign in last]
        for e in (3, 1, 2):
            block = at(e, region, half)
            plan.message(
                (p, "c", e), block, block, g.along("core", 1), at(e, other, half), tuple(have[e])
            )
            needs[e] += have[e] + [(p, "c", e)]

    begin = 0
    for count, size in enumerate(SHARES[n]):
        add_piece((n, count), begin, size, True)
        begin += 2 * SIDE * size
    while begin < NT * W:
        add_piece((n, begin // (2 * ALONE) + 8), begin, ALONE, False)
        begin += 2 * ALONE
    return needs


def lanes(blocks):
    return jnp.concatenate(blocks, 1)


def add_project(plan, g, n, cut, ring, buf, have, full, needs, wide, dst, sender):
    i = g.at(cut)

    def columns(e):
        at = wrap(i + e, SIDE)
        total = None
        for m in range(SIDE):
            if ring == "z":
                left = lanes([buf[m, k] for k in range(SIDE)])
            else:
                left = lanes([buf[k, m] for k in range(SIDE)])
            depth = pl.ds(m * SIDE * W, SIDE * W)
            if wide:
                term = lax.dot_general(left, full[at, :, depth], NT_DIMS, preferred_element_type=F32)
            else:
                term = jnp.dot(left, full[at, depth, :], preferred_element_type=F32)
            total = term if total is None else total + term
        return total.astype(BF16)

    def make(e):
        def work():
            if e:
                sender[e] = columns(e).reshape(sender.shape[1:])
            else:
                dst(i)[...] = columns(e).reshape(sender.shape[1:])

        return work

    for e in OFFSETS:
        plan.step((n, "p", e), make(e), tuple(have + needs[e]))
        if e:
            plan.message(
                (n, "o", e), sender.at[e], dst(i), g.along(cut, e), dst(wrap(i - e, SIDE)),
                ((n, "p", e),),
            )
    return [(n, "p", 0)] + [(n, "o", e) for e in (1, 2, 3)]


def add_scatter(plan, g, n, cut, ring, own, own_step, got, parts, one, two, make, out, old=(), final=None):
    i, j = g.at(cut), g.at(ring)

    def keep():
        got[i] = own[i]

    plan.step((n, "k"), keep, (own_step,))
    for k in (1, 3, 2):
        peer = wrap(i + k, SIDE)
        plan.message(
            (n, "x", k), own.at[peer], got.at[i], g.along(cut, k), got.at[wrap(i - k, SIDE)],
            (own_step,),
        )
    swapped = ((n, "k"), (n, "x", 1), (n, "x", 2), (n, "x", 3))

    def part(dj, where=None):
        block = parts.at[wrap(j + dj, SIDE)]
        return block if where is None else block.at[pl.ds(2 * where, 2)]

    def fill(dj):
        def work():
            row = wrap(j + dj, SIDE)

            @pl.loop(0, SIDE)
            def _(k):
                t = row * SIDE + k if ring == "z" else k * SIDE + row
                parts[row, k] = make(t).astype(BF16)

        return work

    def add(ref, *others):
        total = ref[...].astype(F32)
        for other in others:
            total = total + other[...].astype(F32)
        ref[...] = total.astype(BF16)

    for dj in (2, 1, 3, 0):
        plan.step((n, "f", dj), fill(dj), swapped, old)
    plan.message((n, "n", 0), part(2, 0), one.at[0], g.along(ring, -1), one.at[0], ((n, "f", 2),))
    plan.message((n, "n", 1), part(2, 1), one.at[1], g.along(ring, 1), one.at[1], ((n, "f", 2),))
    plan.step((n, "r", 0), lambda: add(part(3, 0), one.at[0]), ((n, "f", 3), (n, "n", 0)))
    plan.step((n, "r", 1), lambda: add(part(1, 1), one.at[1]), ((n, "f", 1), (n, "n", 1)))
    for where in range(2):
        half = pl.ds(2 * where, 2)
        up, down = two.at[0, half], two.at[1, half]
        plan.message(
            (n, "u", where), part(1, where), up, g.along(ring, 1), up, ((n, "r", 1) if where else (n, "f", 1),)
        )
        plan.message(
            (n, "d", where), part(3, where), down, g.along(ring, -1), down, ((n, "f", 3) if where else (n, "r", 0),)
        )
        plan.step(
            (n, "t", where),
            functools.partial(add, part(0, where), up, down),
            ((n, "f", 0), (n, "u", where), (n, "d", where)),
        )
    totals = ((n, "t", 0), (n, "t", 1))
    ready = parts.at[j]
    if final is not None:
        ready = final

        def turn():
            for k in range(SIDE):
                final[k] = parts[j, k].astype(F32).T.astype(BF16).reshape(final.shape[1:])

        plan.step((n, "v"), turn, totals)
        totals = ((n, "v"),)
    for k in (1, 3, 2):
        plan.message(
            (n, "b", k), ready.at[wrap(i + k, SIDE)], out(i), g.along(cut, k),
            out(wrap(i - k, SIDE)), totals,
        )

    def own_rows():
        out(i)[...] = ready[i]

    plan.step((n, "b", 0), own_rows, totals)


def register(
    plan, g,
    enc_ref, hid_ref, gout_ref, wq_ref, wk_ref, wv_ref, wo_ref, rows_ref, slot_ref,
    out_ref, gh_ref, ge_ref,
    enc_all, hid_all, gout_all, wq, wk, wv, wo, kv_send, q_send, ga_send, own_k, own_v, stage_k, stage_v,
    k_in, v_in, q_ext, ga_ext, q_span, ga_span, probs, att, gq, tok_a, tok_c, got_a, got_c, reads,
    slot_out, slot_in, gkv, gkv_t, gkv_got, parts_c, parts_enc, one_a, two_a, one_c, two_c, one_enc, two_enc,
    final_c, final_enc, chain,
):
    scale = HEAD_DIM ** (-0.5)
    all_weights = {}
    for n, cut, own, full in (("K", "x", wk_ref, wk), ("V", "x", wv_ref, wv), ("Q", "z", wq_ref, wq), ("O", "z", wo_ref, wo)):
        all_weights[n] = add_weight(plan, g, n, cut, own, full, n == "O")
    enc = add_gather(plan, g, "E", "x", "z", enc_ref, enc_all)
    hid = add_gather(plan, g, "H", "z", "x", hid_ref, hid_all)
    gout = add_gather(plan, g, "G", "z", "x", gout_ref, gout_all)

    per = EQ // RLEN
    for n, full, own, stage, sender, land in (
        ("K", wk, own_k, stage_k, kv_send.at[0], k_in), ("V", wv, own_v, stage_v, kv_send.at[1], v_in)
    ):
        def rows(i, own=own):
            return own.at[pl.ds(i * per, per)]

        made = add_project(
            plan, g, n, "x", "z", enc_all, enc, full, all_weights[n], False, rows, sender
        )

        def pick(own=own, stage=stage, land=land):
            @pl.loop(0, NSEQ)
            def _(r):
                for s in range(2):
                    stage[r, s] = own[jnp.maximum(rows_ref[0, 2 * r + s], 0)]

            land[g.seq] = stage[g.seq]

        plan.step((n, "x"), pick, tuple(made))
        for k in range(1, NSEQ):
            plan.message(
                (n, "a", k), stage.at[wrap(g.seq + k, NSEQ)], land.at[g.seq], g.along("seq", k),
                land.at[wrap(g.seq - k, NSEQ)], ((n, "x"),),
            )

    head, tail = pl.ds(0, SPAN), pl.ds(ROWS, SPAN)
    row = col = None

    def shift_rows(by, limit=None):
        row = lax.broadcasted_iota(jnp.int32, (Q, Q + SPAN), 0)
        col = lax.broadcasted_iota(jnp.int32, (Q, Q + SPAN), 1)
        picked = col == row + by
        if limit is not None:
            picked = jnp.logical_and(picked, col < limit)
        return picked.astype(BF16)

    for n, buf, have, full, ext, span, sender in (
        ("Q", hid_all, hid, wq, q_ext, q_span, q_send), ("O", gout_all, gout, wo, ga_ext, ga_span, ga_send)
    ):
        def rows(i, ext=ext):
            return ext.at[pl.ds(pl.multiple_of(i * Q, Q), Q)]

        made = add_project(
            plan, g, n, "z", "x", buf, have, full, all_weights[n], n == "O", rows, sender
        )
        plan.message(
            (n, "e"), ext.at[head], ext.at[tail], g.along("seq", NSEQ - 1), ext.at[tail], tuple(made)
        )

        def align(ext=ext, span=span):
            for m in range(SIDE):
                limit = None
                if m == SIDE - 1:
                    limit = jnp.where(g.seq == NSEQ - 1, Q, Q + SPAN)
                moved = jnp.dot(
                    shift_rows(SPAN - 1, limit), ext[m * Q : (m + 1) * Q + SPAN, :],
                    preferred_element_type=F32,
                )
                span[m * Q : (m + 1) * Q, :] = moved.astype(BF16)

        plan.step((n, "t"), align, tuple(made) + ((n, "e"),))

    def tables():
        for kind in range(2):
            reads[kind, NONE] = jnp.zeros((RLEN, HEAD_DIM), F32)
        ids = [slot_ref[p % NEIGH, p // NEIGH] for p in range(NONE)]
        targets = [rows_ref[0, j] for j in range(NONE)]
        for line, values in ((0, ids), (2, targets)):
            for p in range(NONE):
                before, latest = jnp.int32(NONE), jnp.int32(NONE)
                for q in range(NONE):
                    if q < p:
                        before = jnp.where(values[q] == values[p], q, before)
                    latest = jnp.where(values[q] == p, q, latest)
                chain[line, p] = before
                chain[line + 1, p] = latest

    plan.step(("T", "t"), tables)

    def read(ref, u, cols):
        picked = []
        for j in range(NEIGH):
            s = slot_ref[j, u]
            picked.append(ref[lax.div(s, 2), lax.rem(s, 2), :, cols])
        return jnp.concatenate(picked, 0)

    def forward(h):
        cols = slice(h * HEAD_DIM, (h + 1) * HEAD_DIM)

        def work():
            @pl.loop(0, SPANS, unroll=UNROLL)
            def _(u):
                here = pl.ds(pl.multiple_of(u * SPAN, SPAN), SPAN)
                k, v = read(k_in, u, cols), read(v_in, u, cols)
                scores = lax.dot_general(
                    q_span[here, cols], k, NT_DIMS, preferred_element_type=F32
                ) * scale
                peak = jnp.max(scores, axis=-1, keepdims=True)
                weights = jnp.exp(scores - peak)
                prob = weights / jnp.sum(weights, axis=-1, keepdims=True)
                probs[h, u] = prob
                context = jnp.dot(prob.astype(BF16), v, preferred_element_type=F32)
                att[pl.ds(pl.multiple_of(u * SPAN, SPAN) + SPAN, SPAN), cols] = context.astype(BF16)

        return work

    def backward(h):
        cols = slice(h * HEAD_DIM, (h + 1) * HEAD_DIM)

        def work():
            @pl.loop(0, SPANS, unroll=UNROLL)
            def _(u):
                here = pl.ds(pl.multiple_of(u * SPAN, SPAN), SPAN)
                k, v = read(k_in, u, cols), read(v_in, u, cols)
                prob = probs[h, u]
                q, gr = q_span[here, cols], ga_span[here, cols]
                grad_probs = lax.dot_general(gr, v, NT_DIMS, preferred_element_type=F32)
                dot_sum = jnp.sum(grad_probs * prob, axis=-1, keepdims=True)
                grad_scores = (prob * (grad_probs - dot_sum) * scale).astype(BF16)
                grad_q = jnp.dot(grad_scores, k, preferred_element_type=F32)
                gq[pl.ds(pl.multiple_of(u * SPAN, SPAN) + SPAN, SPAN), cols] = grad_q.astype(BF16)
                grad_k = lax.dot_general(grad_scores, q, TN_DIMS, preferred_element_type=F32)
                grad_v = lax.dot_general(
                    prob.astype(BF16), gr, TN_DIMS, preferred_element_type=F32
                )
                for j in range(NEIGH):
                    part = slice(j * RLEN, (j + 1) * RLEN)
                    p = NEIGH * u + j
                    before = chain[0, p]
                    reads[0, p] = grad_k[part] + reads[0, before]
                    reads[1, p] = grad_v[part] + reads[1, before]

            @pl.loop(0, SLOTS)
            def _(s):
                latest = chain[1, s]
                for r in range(2):
                    for kind in range(2):
                        slot_out[h, r, lax.div(s, 2), lax.rem(s, 2), kind] = reads[
                            kind, latest, r * HALF : (r + 1) * HALF, :
                        ].astype(BF16)

            for r in range(2):
                slot_in[h, r, g.seq] = slot_out[h, r, g.seq]

        return work

    landed = tuple((n, "a", k) for n in "KV" for k in range(1, NSEQ)) + (("K", "x"), ("V", "x"))
    for h in range(HEADS):
        plan.step(("F", h), forward(h), landed + (("Q", "t"),))
    for h in range(HEADS):
        plan.step(("B", h), backward(h), (("F", h), ("O", "t"), ("T", "t")))
        for r in range(2):
            for k in range(1, NSEQ):
                plan.message(
                    ("S", h, r, "a", k), slot_out.at[h, r, wrap(g.seq + k, NSEQ)], slot_in.at[h, r, g.seq],
                    g.along("seq", k), slot_in.at[h, r, wrap(g.seq - k, NSEQ)], (("B", h),),
                )

    last = pl.ds(ROWS, SPAN)

    def out_part(t):
        depth = pl.ds(pl.multiple_of(t * W, W), W)
        return sum(
            jnp.dot(got_a[k], wo[k, :, depth], preferred_element_type=F32) for k in range(SIDE)
        )

    def hidden_part(t):
        depth = pl.ds(pl.multiple_of(t * W, W), W)
        return sum(
            jnp.dot(wq[k, depth, :], got_c[k], preferred_element_type=F32)
            for k in range(SIDE)
        )

    gone = [("H", "f", d) for d in OFFSETS]
    gone += [("H", "s", d, sign) for d in (1, 2, 3) for sign in "+-"]
    for n, src, made, make, tok, got, parts, one, two, result, old, final in (
        ("A", att, (("F", 0), ("F", 1)), out_part, tok_a, got_a, hid_all, one_a, two_a, out_ref, tuple(gone), None),
        ("C", gq, (("B", 0), ("B", 1)), hidden_part, tok_c, got_c, parts_c, one_c, two_c, gh_ref, (), final_c),
    ):
        plan.message((n, "e"), src.at[last], src.at[head], g.along("seq", 1), src.at[head], made)

        def align(src=src, tok=tok, final=final):
            @pl.when(g.seq == 0)
            def _():
                src[head, :] = jnp.zeros((SPAN, W), BF16)

            for m in range(SIDE):
                moved = jnp.dot(
                    shift_rows(1), src[m * Q : (m + 1) * Q + SPAN, :], preferred_element_type=F32
                )
                tok[m] = (moved if final is None else moved.T).astype(BF16)

        plan.step((n, "t"), align, made + ((n, "e"),))

        def rows(i, result=result):
            return result.at[pl.ds(pl.multiple_of(i * Q, Q), Q)]

        add_scatter(
            plan, g, n, "z", "x", tok, (n, "t"), got, parts, one, two, make, rows, old, final
        )

    def owner_sums(r):
        def work():
            @pl.loop(0, NSEQ)
            def _(o):
                for slot in range(2):
                    p = 2 * o + slot
                    before = chain[2, p]
                    for kind in range(2):
                        for h in range(HEADS):
                            rows = slice(h * HALF, (h + 1) * HALF)
                            value = slot_in[h, r, o, slot, kind].astype(F32)
                            reads[kind, p, rows, :] = value + reads[kind, before, rows, :]

            for n in range(NSEQ):
                latest = chain[3, n]
                for kind in range(2):
                    for h in range(HEADS):
                        rows = slice(h * HALF, (h + 1) * HALF)
                        cols = slice(h * HEAD_DIM, (h + 1) * HEAD_DIM)
                        place = slice((n % per) * HALF, (n % per + 1) * HALF)
                        gkv[n // per, kind, place, cols] = reads[kind, latest, rows, :].astype(BF16)
            for k in range(SIDE):
                for kind in range(2):
                    gkv_t[r, k, kind] = gkv[k, kind].astype(F32).T.astype(BF16)

        return work

    def enc_part(r):
        def make(t):
            depth = pl.ds(pl.multiple_of(t * W, W), W)
            total = None
            for kind, w in ((0, wk), (1, wv)):
                for k in range(SIDE):
                    term = jnp.dot(
                        w[k, depth, :], gkv_got[r, k, kind], preferred_element_type=F32
                    )
                    total = term if total is None else total + term
            return total

        return make

    for r in range(2):
        came = tuple(("S", h, r, "a", k) for h in range(HEADS) for k in range(1, NSEQ))
        plan.step(("W", r), owner_sums(r), came + (("B", 0), ("B", 1)))

        def rows(i, r=r):
            return ge_ref.at[pl.ds(i * per, per), pl.ds(r * HALF, HALF)]

        add_scatter(
            plan, g, ("Y", r), "x", "z", gkv_t.at[r], ("W", r), gkv_got.at[r], parts_enc.at[r],
            one_enc.at[r], two_enc.at[r], enc_part(r), rows, (), final_enc.at[r],
        )


def kernel(*refs):
    *refs, send, recv, local = refs
    g = Grid()
    plan = Plan(send, recv, local)
    register(plan, g, *refs)
    names = list(plan.actions)
    assert sorted(ORDER) == list(range(len(names)))
    g.barrier()
    for number in ORDER:
        plan.run(names[number])
    plan.finish()


def scratch():
    def vmem(*dims, dtype=BF16):
        return pltpu.VMEM(dims, dtype)

    weight = vmem(SIDE, NT * W, W)
    quarters = vmem(SIDE, Q, W)
    return [
        vmem(SIDE, SIDE, EQ, W), vmem(SIDE, SIDE, Q, W), vmem(SIDE, SIDE, Q, W),
        weight, weight, weight, vmem(SIDE, W, NT * W),
        vmem(2, SIDE, EQ // RLEN, RLEN, W), quarters, quarters,
        vmem(NSEQ, RLEN, W), vmem(NSEQ, RLEN, W),
        vmem(NSEQ, 2, RLEN, W), vmem(NSEQ, 2, RLEN, W), vmem(NSEQ, 2, RLEN, W), vmem(NSEQ, 2, RLEN, W),
        vmem(ROWS + SPAN, W), vmem(ROWS + SPAN, W), vmem(ROWS, W), vmem(ROWS, W),
        vmem(HEADS, SPANS, SPAN, NEIGH * RLEN, dtype=F32),
        vmem(ROWS + SPAN, W), vmem(ROWS + SPAN, W),
        quarters, vmem(SIDE, W, Q), quarters, vmem(SIDE, W, Q),
        vmem(2, NONE + 1, RLEN, HEAD_DIM, dtype=F32),
        vmem(HEADS, 2, NSEQ, 2, 2, HALF, HEAD_DIM), vmem(HEADS, 2, NSEQ, 2, 2, HALF, HEAD_DIM),
        vmem(SIDE, 2, Q, W), vmem(2, SIDE, 2, W, Q), vmem(2, SIDE, 2, W, Q),
        vmem(SIDE, SIDE, W, Q), vmem(2, SIDE, SIDE, W, Q),
        vmem(2, 2, Q, W), vmem(2, SIDE, Q, W), vmem(2, 2, W, Q), vmem(2, SIDE, W, Q),
        vmem(2, 2, 2, W, Q), vmem(2, 2, SIDE, W, Q),
        quarters, vmem(2, SIDE, 2, HALF, W), pltpu.SMEM((4, NONE), jnp.int32),
    ]


def shape(*dims, dtype=BF16):
    return jax.ShapeDtypeStruct(dims, dtype)


def hand_over(*refs):
    for src, dst in zip(refs[:3], refs[3:]):
        dst[...] = src[...]


def per_device(hidden, encoded, w_query, w_key, w_value, w_out, send_rows, read_slot, grad_out):
    dma = pltpu.SemaphoreType.DMA
    shapes = (shape(ROWS, W), shape(ROWS, W), shape(NSEQ, RLEN, W))
    results = pl.pallas_call(
        kernel,
        name="cross_attention",
        out_shape=shapes,
        in_specs=[ANY] * 7 + [SM, SM],
        out_specs=(VM, VM, VM),
        scratch_shapes=scratch() + [dma((MESSAGES,)), dma((MESSAGES,)), dma((7,))],
        compiler_params=pltpu.CompilerParams(
            collective_id=0, has_side_effects=True, vmem_limit_bytes=63 * 1024 * 1024
        ),
    )(
        encoded.reshape(2 * ROWS, W), hidden, grad_out, w_query, w_key, w_value, w_out, send_rows, read_slot.T,
    )
    return pl.pallas_call(
        hand_over,
        name="hand_over",
        out_shape=shapes,
        in_specs=[VM] * 3,
        out_specs=(VM,) * 3,
    )(*results)


def solution(mesh):
    placed = (
        P("seq", "tensor"),
        P("seq", None, "tensor"),
        P(None, "tensor"),
        P(None, "tensor"),
        P(None, "tensor"),
        P("tensor", None),
        P("seq", None),
        P("seq", None),
        P("seq", "tensor"),
    )
    return jax.shard_map(
        per_device,
        mesh=mesh,
        in_specs=placed,
        out_specs=(P("seq", "tensor"), P("seq", "tensor"), P("seq", None, "tensor")),
        check_vma=False,
    )
```

```python
import functools

import jax
import jax.numpy as jnp
from jax import lax
from jax.experimental import pallas as pl
from jax.experimental.pallas import tpu as pltpu
from jax.sharding import PartitionSpec as P

SPAN = 64
NEIGH = 2
RLEN = 128
HEAD_DIM = 128
NSEQ = 8
SIDE = 4
NT = SIDE * SIDE
W = 256
ROWS = 512
Q = ROWS // SIDE
EQ = 2 * ROWS // SIDE
MESH = pl.DeviceIdType.MESH
ANY = pl.BlockSpec(memory_space=pl.ANY)
VM = pl.BlockSpec(memory_space=pltpu.VMEM)
SM = pl.BlockSpec(memory_space=pltpu.SMEM)
F32 = jnp.float32
BF16 = jnp.bfloat16
NT_DIMS = (((1,), (1,)), ((), ()))
TN_DIMS = (((0,), (0,)), ((), ()))
SPANS = ROWS // SPAN
SLOTS = 2 * NSEQ
HEADS = W // HEAD_DIM
HALF = RLEN // 2
NONE = SPANS * NEIGH
OFFSETS = (0, 3, 1, 2)
SHARES = {"K": (256, 256), "V": (256,), "Q": (256,), "O": ()}
ALONE = 256
UNROLL = 2


ORDER = (
    0, 35, 81, 127, 184, 200, 216, 219, 99, 18, 106, 218, 1, 164, 107, 2, 280, 187, 19, 82, 171, 4, 7, 8, 20,
    22, 23, 113, 3, 110, 108, 60, 103, 5, 6, 185, 168, 109, 166, 100, 111, 227, 21, 54, 120, 186, 195, 175,
    188, 53, 86, 12, 112, 115, 28, 117, 87, 202, 11, 25, 37, 62, 64, 74, 190, 124, 102, 104, 191, 56, 199,
    201, 55, 196, 67, 75, 57, 58, 16, 92, 27, 39, 114, 205, 9, 32, 10, 61, 24, 29, 192, 36, 101, 206, 59, 78,
    15, 197, 69, 163, 76, 189, 31, 26, 96, 207, 77, 68, 194, 116, 226, 63, 79, 118, 13, 198, 65, 14, 43, 42,
    220, 204, 33, 208, 38, 41, 224, 83, 165, 30, 40, 193, 213, 173, 209, 80, 167, 119, 225, 122, 142, 17, 70,
    221, 228, 47, 84, 212, 170, 169, 34, 214, 157, 45, 44, 230, 231, 46, 89, 85, 88, 235, 236, 66, 237, 232,
    73, 121, 72, 238, 51, 247, 144, 217, 91, 150, 159, 149, 233, 172, 234, 174, 161, 250, 251, 49, 146, 48,
    93, 105, 71, 90, 50, 123, 129, 128, 222, 223, 239, 241, 95, 243, 176, 125, 52, 248, 249, 203, 143, 151,
    229, 156, 94, 154, 97, 246, 252, 253, 245, 130, 131, 152, 133, 132, 153, 136, 271, 211, 210, 135, 244,
    240, 126, 98, 242, 145, 177, 254, 215, 158, 256, 134, 147, 160, 260, 178, 261, 155, 255, 265, 263, 267,
    264, 137, 268, 139, 259, 148, 138, 140, 262, 257, 266, 162, 179, 181, 180, 182, 272, 258, 274, 275, 273,
    141, 269, 183, 276, 277, 270, 281, 278, 282, 313, 279, 298, 302, 305, 314, 316, 318, 317, 315, 303, 300,
    299, 312, 301, 283, 290, 285, 321, 331, 288, 320, 289, 319, 324, 287, 286, 322, 323, 327, 304, 284, 306,
    293, 291, 337, 292, 338, 339, 341, 297, 340, 307, 342, 296, 325, 328, 326, 330, 311, 310, 308, 362, 366,
    364, 365, 294, 363, 344, 295, 329, 345, 351, 332, 333, 336, 334, 335, 355, 309, 343, 346, 347, 386, 389,
    367, 388, 371, 372, 390, 369, 379, 387, 368, 375, 370, 374, 378, 373, 376, 349, 352, 348, 391, 396, 395,
    393, 403, 392, 399, 350, 354, 394, 398, 397, 400, 402, 377, 380, 353, 381, 384, 382, 385, 383, 356, 357,
    358, 361, 360, 359, 401, 404, 405, 408, 407, 406, 409,
)
MESSAGES = 331


def wrap(value, count):
    return lax.rem(value + count, count)


class Grid:
    def __init__(self):
        self.seq = lax.axis_index("seq")
        tensor = lax.axis_index("tensor")
        self.z = lax.div(tensor, SIDE)
        self.x = lax.rem(tensor, SIDE)
        self.y = lax.div(self.seq, 2)
        self.core = lax.rem(self.seq, 2)

    def at(self, axis):
        return self.z if axis == "z" else self.x

    def along(self, axis, step):
        if axis == "z":
            return {"tensor": wrap(self.z + step, SIDE) * SIDE + self.x}
        if axis == "x":
            return {"tensor": self.z * SIDE + wrap(self.x + step, SIDE)}
        if axis == "y":
            return {"seq": wrap(self.y + step, SIDE) * 2 + self.core}
        if axis == "core":
            return {"seq": self.y * 2 + (1 - self.core)}
        return {"seq": wrap(self.seq + step, NSEQ)}

    def barrier(self):
        sem = pltpu.get_barrier_semaphore()
        peers = [self.along(axis, k) for axis in "zx" for k in range(1, SIDE)]
        peers += [self.along("seq", k) for k in range(1, NSEQ)]
        for peer in peers:
            pl.semaphore_signal(sem, inc=1, device_id=peer, device_id_type=MESH)
        pl.semaphore_wait(sem, len(peers))


class Plan:
    def __init__(self, send, recv, local):
        self.send, self.recv, self.local = send, recv, local
        self.actions, self.copies, self.landed, self.left = {}, {}, set(), set()
        self.messages = self.locals = 0

    def message(self, name, src, dst, peer, land, after=()):
        self.actions[name] = ("message", (src, dst, peer, land, self.messages), after, ())
        self.messages += 1

    def step(self, name, work, after=(), sent=()):
        self.actions[name] = ("step", work, after, sent)

    def load(self, name, src, dst):
        self.actions[name] = ("load", (src, dst, self.locals), (), ())
        self.locals += 1

    def need(self, name):
        if name in self.landed:
            return
        kind, data, _, _ = self.actions[name]
        assert name in self.copies, name
        if kind == "message":
            land = data[3]
            pltpu.make_async_copy(land, land, self.recv.at[data[4]]).wait()
        else:
            self.copies[name].wait()
        self.landed.add(name)

    def leave(self, name):
        if name not in self.left:
            self.copies[name].wait_send()
            self.left.add(name)

    def run(self, name):
        kind, data, after, sent = self.actions[name]
        for other in after:
            self.need(other)
        for other in sent:
            self.leave(other)
        if kind == "message":
            src, dst, peer, _, number = data
            copy = pltpu.make_async_remote_copy(
                src_ref=src,
                dst_ref=dst,
                send_sem=self.send.at[number],
                recv_sem=self.recv.at[number],
                device_id=peer,
                device_id_type=MESH,
            )
            copy.start()
            self.copies[name] = copy
        elif kind == "load":
            src, dst, number = data
            copy = pltpu.make_async_copy(src, dst, self.local.at[number])
            copy.start()
            self.copies[name] = copy
        else:
            data()
            self.landed.add(name)

    def finish(self):
        for name, (kind, _, _, _) in self.actions.items():
            if kind != "step":
                self.need(name)
            if kind == "message":
                self.leave(name)


def signs():
    return (("+", 1), ("-", -1))


def add_gather(plan, g, n, cut, ring, own, buf):
    rows = buf.shape[2]
    i, j = g.at(cut), g.at(ring)

    def slot(dj, di):
        return buf.at[wrap(j + dj, SIDE), wrap(i + di, SIDE)]

    def quarter(di):
        return own.at[pl.ds(pl.multiple_of(wrap(i + di, SIDE) * rows, rows), rows)]

    plan.load((n, "l"), quarter(0), slot(0, 0))
    for k in (1, 3, 2):
        plan.message((n, "x", k), quarter(k), slot(0, 0), g.along(cut, k), slot(0, SIDE - k))
    for d in OFFSETS:
        src, after = (slot(0, d), ((n, "x", SIDE - d),)) if d else (quarter(0), ())
        for sign, step in signs():
            plan.message(
                (n, "s", d, sign), src, slot(0, d), g.along(ring, step), slot(-step + SIDE, d), after
            )
    for d in OFFSETS:
        sign, step = ("+", 1) if d in (0, 1) else ("-", -1)
        block = slot(SIDE - step, d)
        plan.message((n, "f", d), block, block, g.along(ring, step), slot(2, d), ((n, "s", d, sign),))
    names = [(n, "l")] + [(n, "x", k) for k in (1, 2, 3)] + [(n, "f", d) for d in OFFSETS]
    return names + [(n, "s", d, sign) for d in OFFSETS for sign in "+-"]


def add_weight(plan, g, n, cut, own, full, wide):
    i = g.at(cut)
    needs = {e: [] for e in OFFSETS}
    plan.load((n, "l"), own, full.at[i])
    needs[0].append((n, "l"))

    def cutout(ref, start, size):
        rows = pl.ds(pl.multiple_of(start, 128), size)
        return ref.at[:, rows] if wide else ref.at[rows]

    def add_piece(p, begin, size, shared):
        half = SIDE * size if shared else size
        other = begin + (1 - g.core) * half
        region = begin + g.core * half

        def chunk(dy):
            return region + wrap(g.y + dy, SIDE) * size if shared else region

        def at(e, start, length=size):
            return cutout(full.at[wrap(i + e, SIDE)], start, length)

        def ends(sign):
            return 0 if sign == "+" else size // 2

        here = chunk(0)
        for sign, step in signs():
            plan.message(
                (p, "n", sign), cutout(own, here, size), at(0, here), g.along(cut, step),
                at(SIDE - step, here),
            )
        for sign, step in signs():
            part = at(SIDE - step, here + ends(sign), size // 2)
            plan.message(
                (p, "h", sign), part, part, g.along(cut, step), at(2, here + ends(sign), size // 2),
                ((p, "n", sign),),
            )
        have = {3: [(p, "n", "+")], 1: [(p, "n", "-")], 2: [(p, "h", "+"), (p, "h", "-")]}
        if shared:
            for e in (3, 1, 2):
                for sign, step in signs():
                    plan.message(
                        (p, "y", e, sign), at(e, here), at(e, here), g.along("y", step),
                        at(e, chunk(SIDE - step)), tuple(have[e]),
                    )
            for e, sign, step, length in ((3, "+", 1, size), (1, "-", -1, size), (2, "+", 1, size // 2), (2, "-", -1, size // 2)):
                off = ends(sign) if e == 2 else 0
                part = at(e, chunk(SIDE - step) + off, length)
                plan.message(
                    (p, "z", e, sign), part, part, g.along("y", step), at(e, chunk(2) + off, length),
                    ((p, "y", e, sign),),
                )
            for e, last in ((3, "+"), (1, "-"), (2, "+-")):
                have[e] += [(p, "y", e, "+"), (p, "y", e, "-")] + [(p, "z", e, sign) for sign in last]
        for e in (3, 1, 2):
            block = at(e, region, half)
            plan.message(
                (p, "c", e), block, block, g.along("core", 1), at(e, other, half), tuple(have[e])
            )
            needs[e] += have[e] + [(p, "c", e)]

    begin = 0
    for count, size in enumerate(SHARES[n]):
        add_piece((n, count), begin, size, True)
        begin += 2 * SIDE * size
    while begin < NT * W:
        add_piece((n, begin // (2 * ALONE) + 8), begin, ALONE, False)
        begin += 2 * ALONE
    return needs


def lanes(blocks):
    return jnp.concatenate(blocks, 1)


def add_project(plan, g, n, cut, ring, buf, have, full, needs, wide, dst, sender):
    i = g.at(cut)

    def columns(e):
        at = wrap(i + e, SIDE)
        total = None
        for m in range(SIDE):
            if ring == "z":
                left = lanes([buf[m, k] for k in range(SIDE)])
            else:
                left = lanes([buf[k, m] for k in range(SIDE)])
            depth = pl.ds(m * SIDE * W, SIDE * W)
            if wide:
                term = lax.dot_general(left, full[at, :, depth], NT_DIMS, preferred_element_type=F32)
            else:
                term = jnp.dot(left, full[at, depth, :], preferred_element_type=F32)
            total = term if total is None else total + term
        return total.astype(BF16)

    def make(e):
        def work():
            if e:
                sender[e] = columns(e).reshape(sender.shape[1:])
            else:
                dst(i)[...] = columns(e).reshape(sender.shape[1:])

        return work

    for e in OFFSETS:
        plan.step((n, "p", e), make(e), tuple(have + needs[e]))
        if e:
            plan.message(
                (n, "o", e), sender.at[e], dst(i), g.along(cut, e), dst(wrap(i - e, SIDE)),
                ((n, "p", e),),
            )
    return [(n, "p", 0)] + [(n, "o", e) for e in (1, 2, 3)]


def add_scatter(plan, g, n, cut, ring, own, own_step, got, parts, one, two, make, out, old=(), final=None):
    i, j = g.at(cut), g.at(ring)

    def keep():
        got[i] = own[i]

    plan.step((n, "k"), keep, (own_step,))
    for k in (1, 3, 2):
        peer = wrap(i + k, SIDE)
        plan.message(
            (n, "x", k), own.at[peer], got.at[i], g.along(cut, k), got.at[wrap(i - k, SIDE)],
            (own_step,),
        )
    swapped = ((n, "k"), (n, "x", 1), (n, "x", 2), (n, "x", 3))

    def part(dj, where=None):
        block = parts.at[wrap(j + dj, SIDE)]
        return block if where is None else block.at[pl.ds(2 * where, 2)]

    def fill(dj):
        def work():
            row = wrap(j + dj, SIDE)

            @pl.loop(0, SIDE)
            def _(k):
                t = row * SIDE + k if ring == "z" else k * SIDE + row
                parts[row, k] = make(t).astype(BF16)

        return work

    def add(ref, *others):
        total = ref[...].astype(F32)
        for other in others:
            total = total + other[...].astype(F32)
        ref[...] = total.astype(BF16)

    for dj in (2, 1, 3, 0):
        plan.step((n, "f", dj), fill(dj), swapped, old)
    plan.message((n, "n", 0), part(2, 0), one.at[0], g.along(ring, -1), one.at[0], ((n, "f", 2),))
    plan.message((n, "n", 1), part(2, 1), one.at[1], g.along(ring, 1), one.at[1], ((n, "f", 2),))
    plan.step((n, "r", 0), lambda: add(part(3, 0), one.at[0]), ((n, "f", 3), (n, "n", 0)))
    plan.step((n, "r", 1), lambda: add(part(1, 1), one.at[1]), ((n, "f", 1), (n, "n", 1)))
    for where in range(2):
        half = pl.ds(2 * where, 2)
        up, down = two.at[0, half], two.at[1, half]
        plan.message(
            (n, "u", where), part(1, where), up, g.along(ring, 1), up, ((n, "r", 1) if where else (n, "f", 1),)
        )
        plan.message(
            (n, "d", where), part(3, where), down, g.along(ring, -1), down, ((n, "f", 3) if where else (n, "r", 0),)
        )
        plan.step(
            (n, "t", where),
            functools.partial(add, part(0, where), up, down),
            ((n, "f", 0), (n, "u", where), (n, "d", where)),
        )
    totals = ((n, "t", 0), (n, "t", 1))
    ready = parts.at[j]
    if final is not None:
        ready = final

        def turn():
            for k in range(SIDE):
                final[k] = parts[j, k].astype(F32).T.astype(BF16).reshape(final.shape[1:])

        plan.step((n, "v"), turn, totals)
        totals = ((n, "v"),)
    for k in (1, 3, 2):
        plan.message(
            (n, "b", k), ready.at[wrap(i + k, SIDE)], out(i), g.along(cut, k),
            out(wrap(i - k, SIDE)), totals,
        )

    def own_rows():
        out(i)[...] = ready[i]

    plan.step((n, "b", 0), own_rows, totals)


def register(
    plan, g,
    enc_ref, hid_ref, gout_ref, wq_ref, wk_ref, wv_ref, wo_ref, rows_ref, slot_ref,
    out_ref, gh_ref, ge_ref,
    enc_all, hid_all, gout_all, wq, wk, wv, wo, kv_send, q_send, ga_send, own_k, own_v, stage_k, stage_v,
    k_in, v_in, q_ext, ga_ext, q_span, ga_span, probs, att, gq, tok_a, tok_c, got_a, got_c, reads,
    slot_out, slot_in, gkv, gkv_t, gkv_got, parts_c, parts_enc, one_a, two_a, one_c, two_c, one_enc, two_enc,
    final_c, final_enc, chain,
):
    scale = HEAD_DIM ** (-0.5)
    all_weights = {}
    for n, cut, own, full in (("K", "x", wk_ref, wk), ("V", "x", wv_ref, wv), ("Q", "z", wq_ref, wq), ("O", "z", wo_ref, wo)):
        all_weights[n] = add_weight(plan, g, n, cut, own, full, n == "O")
    enc = add_gather(plan, g, "E", "x", "z", enc_ref, enc_all)
    hid = add_gather(plan, g, "H", "z", "x", hid_ref, hid_all)
    gout = add_gather(plan, g, "G", "z", "x", gout_ref, gout_all)

    per = EQ // RLEN
    for n, full, own, stage, sender, land in (
        ("K", wk, own_k, stage_k, kv_send.at[0], k_in), ("V", wv, own_v, stage_v, kv_send.at[1], v_in)
    ):
        def rows(i, own=own):
            return own.at[pl.ds(i * per, per)]

        made = add_project(
            plan, g, n, "x", "z", enc_all, enc, full, all_weights[n], False, rows, sender
        )

        def pick(own=own, stage=stage, land=land):
            @pl.loop(0, NSEQ)
            def _(r):
                for s in range(2):
                    stage[r, s] = own[jnp.maximum(rows_ref[0, 2 * r + s], 0)]

            land[g.seq] = stage[g.seq]

        plan.step((n, "x"), pick, tuple(made))
        for k in range(1, NSEQ):
            plan.message(
                (n, "a", k), stage.at[wrap(g.seq + k, NSEQ)], land.at[g.seq], g.along("seq", k),
                land.at[wrap(g.seq - k, NSEQ)], ((n, "x"),),
            )

    head, tail = pl.ds(0, SPAN), pl.ds(ROWS, SPAN)
    row = col = None

    def shift_rows(by, limit=None):
        row = lax.broadcasted_iota(jnp.int32, (Q, Q + SPAN), 0)
        col = lax.broadcasted_iota(jnp.int32, (Q, Q + SPAN), 1)
        picked = col == row + by
        if limit is not None:
            picked = jnp.logical_and(picked, col < limit)
        return picked.astype(BF16)

    for n, buf, have, full, ext, span, sender in (
        ("Q", hid_all, hid, wq, q_ext, q_span, q_send), ("O", gout_all, gout, wo, ga_ext, ga_span, ga_send)
    ):
        def rows(i, ext=ext):
            return ext.at[pl.ds(pl.multiple_of(i * Q, Q), Q)]

        made = add_project(
            plan, g, n, "z", "x", buf, have, full, all_weights[n], n == "O", rows, sender
        )
        plan.message(
            (n, "e"), ext.at[head], ext.at[tail], g.along("seq", NSEQ - 1), ext.at[tail], tuple(made)
        )

        def align(ext=ext, span=span):
            for m in range(SIDE):
                limit = None
                if m == SIDE - 1:
                    limit = jnp.where(g.seq == NSEQ - 1, Q, Q + SPAN)
                moved = jnp.dot(
                    shift_rows(SPAN - 1, limit), ext[m * Q : (m + 1) * Q + SPAN, :],
                    preferred_element_type=F32,
                )
                span[m * Q : (m + 1) * Q, :] = moved.astype(BF16)

        plan.step((n, "t"), align, tuple(made) + ((n, "e"),))

    def tables():
        for kind in range(2):
            reads[kind, NONE] = jnp.zeros((RLEN, HEAD_DIM), F32)
        ids = [slot_ref[p % NEIGH, p // NEIGH] for p in range(NONE)]
        targets = [rows_ref[0, j] for j in range(NONE)]
        for line, values in ((0, ids), (2, targets)):
            for p in range(NONE):
                before, latest = jnp.int32(NONE), jnp.int32(NONE)
                for q in range(NONE):
                    if q < p:
                        before = jnp.where(values[q] == values[p], q, before)
                    latest = jnp.where(values[q] == p, q, latest)
                chain[line, p] = before
                chain[line + 1, p] = latest

    plan.step(("T", "t"), tables)

    def read(ref, u, cols):
        picked = []
        for j in range(NEIGH):
            s = slot_ref[j, u]
            picked.append(ref[lax.div(s, 2), lax.rem(s, 2), :, cols])
        return jnp.concatenate(picked, 0)

    def forward(h):
        cols = slice(h * HEAD_DIM, (h + 1) * HEAD_DIM)

        def work():
            @pl.loop(0, SPANS, unroll=UNROLL)
            def _(u):
                here = pl.ds(pl.multiple_of(u * SPAN, SPAN), SPAN)
                k, v = read(k_in, u, cols), read(v_in, u, cols)
                scores = lax.dot_general(
                    q_span[here, cols], k, NT_DIMS, preferred_element_type=F32
                ) * scale
                peak = jnp.max(scores, axis=-1, keepdims=True)
                weights = jnp.exp(scores - peak)
                prob = weights / jnp.sum(weights, axis=-1, keepdims=True)
                probs[h, u] = prob
                context = jnp.dot(prob.astype(BF16), v, preferred_element_type=F32)
                att[pl.ds(pl.multiple_of(u * SPAN, SPAN) + SPAN, SPAN), cols] = context.astype(BF16)

        return work

    def backward(h):
        cols = slice(h * HEAD_DIM, (h + 1) * HEAD_DIM)

        def work():
            @pl.loop(0, SPANS, unroll=UNROLL)
            def _(u):
                here = pl.ds(pl.multiple_of(u * SPAN, SPAN), SPAN)
                k, v = read(k_in, u, cols), read(v_in, u, cols)
                prob = probs[h, u]
                q, gr = q_span[here, cols], ga_span[here, cols]
                grad_probs = lax.dot_general(gr, v, NT_DIMS, preferred_element_type=F32)
                dot_sum = jnp.sum(grad_probs * prob, axis=-1, keepdims=True)
                grad_scores = (prob * (grad_probs - dot_sum) * scale).astype(BF16)
                grad_q = jnp.dot(grad_scores, k, preferred_element_type=F32)
                gq[pl.ds(pl.multiple_of(u * SPAN, SPAN) + SPAN, SPAN), cols] = grad_q.astype(BF16)
                grad_k = lax.dot_general(grad_scores, q, TN_DIMS, preferred_element_type=F32)
                grad_v = lax.dot_general(
                    prob.astype(BF16), gr, TN_DIMS, preferred_element_type=F32
                )
                for j in range(NEIGH):
                    part = slice(j * RLEN, (j + 1) * RLEN)
                    p = NEIGH * u + j
                    before = chain[0, p]
                    reads[0, p] = grad_k[part] + reads[0, before]
                    reads[1, p] = grad_v[part] + reads[1, before]

            @pl.loop(0, SLOTS)
            def _(s):
                latest = chain[1, s]
                for r in range(2):
                    for kind in range(2):
                        slot_out[h, r, lax.div(s, 2), lax.rem(s, 2), kind] = reads[
                            kind, latest, r * HALF : (r + 1) * HALF, :
                        ].astype(BF16)

            for r in range(2):
                slot_in[h, r, g.seq] = slot_out[h, r, g.seq]

        return work

    landed = tuple((n, "a", k) for n in "KV" for k in range(1, NSEQ)) + (("K", "x"), ("V", "x"))
    for h in range(HEADS):
        plan.step(("F", h), forward(h), landed + (("Q", "t"),))
    for h in range(HEADS):
        plan.step(("B", h), backward(h), (("F", h), ("O", "t"), ("T", "t")))
        for r in range(2):
            for k in range(1, NSEQ):
                plan.message(
                    ("S", h, r, "a", k), slot_out.at[h, r, wrap(g.seq + k, NSEQ)], slot_in.at[h, r, g.seq],
                    g.along("seq", k), slot_in.at[h, r, wrap(g.seq - k, NSEQ)], (("B", h),),
                )

    last = pl.ds(ROWS, SPAN)

    def out_part(t):
        depth = pl.ds(pl.multiple_of(t * W, W), W)
        return sum(
            jnp.dot(got_a[k], wo[k, :, depth], preferred_element_type=F32) for k in range(SIDE)
        )

    def hidden_part(t):
        depth = pl.ds(pl.multiple_of(t * W, W), W)
        return sum(
            jnp.dot(wq[k, depth, :], got_c[k], preferred_element_type=F32)
            for k in range(SIDE)
        )

    gone = [("H", "f", d) for d in OFFSETS]
    gone += [("H", "s", d, sign) for d in (1, 2, 3) for sign in "+-"]
    for n, src, made, make, tok, got, parts, one, two, result, old, final in (
        ("A", att, (("F", 0), ("F", 1)), out_part, tok_a, got_a, hid_all, one_a, two_a, out_ref, tuple(gone), None),
        ("C", gq, (("B", 0), ("B", 1)), hidden_part, tok_c, got_c, parts_c, one_c, two_c, gh_ref, (), final_c),
    ):
        plan.message((n, "e"), src.at[last], src.at[head], g.along("seq", 1), src.at[head], made)

        def align(src=src, tok=tok, final=final):
            @pl.when(g.seq == 0)
            def _():
                src[head, :] = jnp.zeros((SPAN, W), BF16)

            for m in range(SIDE):
                moved = jnp.dot(
                    shift_rows(1), src[m * Q : (m + 1) * Q + SPAN, :], preferred_element_type=F32
                )
                tok[m] = (moved if final is None else moved.T).astype(BF16)

        plan.step((n, "t"), align, made + ((n, "e"),))

        def rows(i, result=result):
            return result.at[pl.ds(pl.multiple_of(i * Q, Q), Q)]

        add_scatter(
            plan, g, n, "z", "x", tok, (n, "t"), got, parts, one, two, make, rows, old, final
        )

    def owner_sums(r):
        def work():
            @pl.loop(0, NSEQ)
            def _(o):
                for slot in range(2):
                    p = 2 * o + slot
                    before = chain[2, p]
                    for kind in range(2):
                        for h in range(HEADS):
                            rows = slice(h * HALF, (h + 1) * HALF)
                            value = slot_in[h, r, o, slot, kind].astype(F32)
                            reads[kind, p, rows, :] = value + reads[kind, before, rows, :]

            for n in range(NSEQ):
                latest = chain[3, n]
                for kind in range(2):
                    for h in range(HEADS):
                        rows = slice(h * HALF, (h + 1) * HALF)
                        cols = slice(h * HEAD_DIM, (h + 1) * HEAD_DIM)
                        place = slice((n % per) * HALF, (n % per + 1) * HALF)
                        gkv[n // per, kind, place, cols] = reads[kind, latest, rows, :].astype(BF16)
            for k in range(SIDE):
                for kind in range(2):
                    gkv_t[r, k, kind] = gkv[k, kind].astype(F32).T.astype(BF16)

        return work

    def enc_part(r):
        def make(t):
            depth = pl.ds(pl.multiple_of(t * W, W), W)
            total = None
            for kind, w in ((0, wk), (1, wv)):
                for k in range(SIDE):
                    term = jnp.dot(
                        w[k, depth, :], gkv_got[r, k, kind], preferred_element_type=F32
                    )
                    total = term if total is None else total + term
            return total

        return make

    for r in range(2):
        came = tuple(("S", h, r, "a", k) for h in range(HEADS) for k in range(1, NSEQ))
        plan.step(("W", r), owner_sums(r), came + (("B", 0), ("B", 1)))

        def rows(i, r=r):
            return ge_ref.at[pl.ds(i * per, per), pl.ds(r * HALF, HALF)]

        add_scatter(
            plan, g, ("Y", r), "x", "z", gkv_t.at[r], ("W", r), gkv_got.at[r], parts_enc.at[r],
            one_enc.at[r], two_enc.at[r], enc_part(r), rows, (), final_enc.at[r],
        )


def kernel(*refs):
    *refs, send, recv, local = refs
    g = Grid()
    plan = Plan(send, recv, local)
    register(plan, g, *refs)
    names = list(plan.actions)
    assert sorted(ORDER) == list(range(len(names)))
    g.barrier()
    for number in ORDER:
        plan.run(names[number])
    plan.finish()


def scratch():
    def vmem(*dims, dtype=BF16):
        return pltpu.VMEM(dims, dtype)

    weight = vmem(SIDE, NT * W, W)
    quarters = vmem(SIDE, Q, W)
    return [
        vmem(SIDE, SIDE, EQ, W), vmem(SIDE, SIDE, Q, W), vmem(SIDE, SIDE, Q, W),
        weight, weight, weight, vmem(SIDE, W, NT * W),
        vmem(2, SIDE, EQ // RLEN, RLEN, W), quarters, quarters,
        vmem(NSEQ, RLEN, W), vmem(NSEQ, RLEN, W),
        vmem(NSEQ, 2, RLEN, W), vmem(NSEQ, 2, RLEN, W), vmem(NSEQ, 2, RLEN, W), vmem(NSEQ, 2, RLEN, W),
        vmem(ROWS + SPAN, W), vmem(ROWS + SPAN, W), vmem(ROWS, W), vmem(ROWS, W),
        vmem(HEADS, SPANS, SPAN, NEIGH * RLEN, dtype=F32),
        vmem(ROWS + SPAN, W), vmem(ROWS + SPAN, W),
        quarters, vmem(SIDE, W, Q), quarters, vmem(SIDE, W, Q),
        vmem(2, NONE + 1, RLEN, HEAD_DIM, dtype=F32),
        vmem(HEADS, 2, NSEQ, 2, 2, HALF, HEAD_DIM), vmem(HEADS, 2, NSEQ, 2, 2, HALF, HEAD_DIM),
        vmem(SIDE, 2, Q, W), vmem(2, SIDE, 2, W, Q), vmem(2, SIDE, 2, W, Q),
        vmem(SIDE, SIDE, W, Q), vmem(2, SIDE, SIDE, W, Q),
        vmem(2, 2, Q, W), vmem(2, SIDE, Q, W), vmem(2, 2, W, Q), vmem(2, SIDE, W, Q),
        vmem(2, 2, 2, W, Q), vmem(2, 2, SIDE, W, Q),
        quarters, vmem(2, SIDE, 2, HALF, W), pltpu.SMEM((4, NONE), jnp.int32),
    ]


def shape(*dims, dtype=BF16):
    return jax.ShapeDtypeStruct(dims, dtype)


def hand_over(*refs):
    for src, dst in zip(refs[:3], refs[3:]):
        dst[...] = src[...]


def per_device(hidden, encoded, w_query, w_key, w_value, w_out, send_rows, read_slot, grad_out):
    dma = pltpu.SemaphoreType.DMA
    shapes = (shape(ROWS, W), shape(ROWS, W), shape(NSEQ, RLEN, W))
    results = pl.pallas_call(
        kernel,
        name="cross_attention",
        out_shape=shapes,
        in_specs=[ANY] * 7 + [SM, SM],
        out_specs=(VM, VM, VM),
        scratch_shapes=scratch() + [dma((MESSAGES,)), dma((MESSAGES,)), dma((7,))],
        compiler_params=pltpu.CompilerParams(
            collective_id=0, has_side_effects=True, vmem_limit_bytes=63 * 1024 * 1024
        ),
    )(
        encoded.reshape(2 * ROWS, W), hidden, grad_out, w_query, w_key, w_value, w_out, send_rows, read_slot.T,
    )
    return pl.pallas_call(
        hand_over,
        name="hand_over",
        out_shape=shapes,
        in_specs=[VM] * 3,
        out_specs=(VM,) * 3,
    )(*results)


def solution(mesh):
    placed = (
        P("seq", "tensor"),
        P("seq", None, "tensor"),
        P(None, "tensor"),
        P(None, "tensor"),
        P(None, "tensor"),
        P("tensor", None),
        P("seq", None),
        P("seq", None),
        P("seq", "tensor"),
    )
    return jax.shard_map(
        per_device,
        mesh=mesh,
        in_specs=placed,
        out_specs=(P("seq", "tensor"), P("seq", "tensor"), P("seq", None, "tensor")),
        check_vma=False,
    )
```

```python
import functools

import jax
import jax.numpy as jnp
from jax import lax
from jax.experimental import pallas as pl
from jax.experimental.pallas import tpu as pltpu
from jax.sharding import PartitionSpec as P

SPAN = 64
NEIGH = 2
RLEN = 128
HEAD_DIM = 128
NSEQ = 8
SIDE = 4
NT = SIDE * SIDE
W = 256
ROWS = 512
Q = ROWS // SIDE
EQ = 2 * ROWS // SIDE
MESH = pl.DeviceIdType.MESH
ANY = pl.BlockSpec(memory_space=pl.ANY)
VM = pl.BlockSpec(memory_space=pltpu.VMEM)
SM = pl.BlockSpec(memory_space=pltpu.SMEM)
F32 = jnp.float32
BF16 = jnp.bfloat16
NT_DIMS = (((1,), (1,)), ((), ()))
TN_DIMS = (((0,), (0,)), ((), ()))
SPANS = ROWS // SPAN
SLOTS = 2 * NSEQ
HEADS = W // HEAD_DIM
HALF = RLEN // 2
NONE = SPANS * NEIGH
OFFSETS = (0, 3, 1, 2)
SHARES = {"K": (256, 256), "V": (256,), "Q": (256,), "O": ()}
ALONE = 256
UNROLL = 4


ORDER = (
    0, 35, 81, 127, 184, 200, 216, 188, 219, 187, 106, 2, 19, 67, 218, 18, 280, 114, 189, 202, 217, 196, 74,
    110, 108, 113, 75, 69, 21, 8, 22, 4, 25, 195, 208, 71, 1, 116, 100, 186, 24, 118, 23, 7, 194, 82, 76, 60,
    107, 37, 28, 78, 115, 117, 77, 79, 12, 199, 185, 29, 102, 54, 104, 6, 5, 53, 192, 80, 119, 99, 68, 32, 86,
    163, 109, 39, 42, 150, 20, 11, 164, 64, 111, 87, 16, 3, 36, 56, 205, 43, 191, 112, 58, 33, 61, 55, 27,
    214, 198, 92, 70, 190, 103, 72, 165, 57, 10, 62, 209, 152, 9, 221, 26, 15, 166, 193, 47, 224, 197, 222,
    38, 59, 168, 204, 154, 220, 120, 223, 84, 40, 31, 96, 63, 149, 225, 227, 83, 14, 41, 229, 73, 169, 65,
    230, 13, 30, 135, 167, 226, 121, 51, 44, 45, 212, 228, 232, 235, 236, 233, 234, 124, 151, 17, 85, 247,
    122, 46, 203, 89, 137, 250, 123, 101, 49, 34, 129, 251, 231, 48, 88, 128, 157, 91, 237, 238, 125, 271, 50,
    90, 136, 93, 210, 201, 177, 211, 105, 126, 248, 95, 52, 249, 239, 246, 242, 215, 131, 94, 130, 159, 142,
    241, 245, 171, 240, 66, 97, 207, 206, 138, 252, 253, 161, 140, 133, 179, 170, 243, 213, 143, 98, 244, 144,
    156, 178, 141, 134, 146, 254, 258, 173, 267, 260, 255, 263, 175, 262, 265, 139, 257, 132, 155, 266, 145,
    264, 261, 172, 147, 174, 158, 268, 256, 160, 180, 182, 181, 153, 274, 275, 259, 148, 272, 273, 176, 162,
    269, 183, 276, 277, 270, 282, 278, 281, 313, 279, 298, 302, 301, 305, 314, 318, 317, 316, 303, 300, 304,
    299, 315, 283, 286, 290, 321, 287, 320, 285, 327, 319, 324, 323, 288, 293, 289, 284, 297, 306, 337, 291,
    322, 331, 338, 340, 342, 339, 296, 341, 307, 311, 292, 325, 328, 308, 326, 330, 312, 362, 366, 364, 363,
    295, 309, 365, 345, 329, 294, 355, 310, 346, 343, 332, 333, 334, 336, 335, 348, 344, 347, 386, 388, 387,
    367, 372, 390, 371, 368, 375, 389, 369, 379, 370, 373, 376, 374, 378, 350, 351, 354, 349, 352, 391, 396,
    395, 392, 399, 393, 403, 394, 397, 398, 400, 402, 377, 380, 381, 385, 382, 383, 384, 353, 356, 357, 358,
    360, 361, 359, 404, 401, 405, 409, 408, 407, 406,
)
MESSAGES = 331


def wrap(value, count):
    return lax.rem(value + count, count)


class Grid:
    def __init__(self):
        self.seq = lax.axis_index("seq")
        tensor = lax.axis_index("tensor")
        self.z = lax.div(tensor, SIDE)
        self.x = lax.rem(tensor, SIDE)
        self.y = lax.div(self.seq, 2)
        self.core = lax.rem(self.seq, 2)

    def at(self, axis):
        return self.z if axis == "z" else self.x

    def along(self, axis, step):
        if axis == "z":
            return {"tensor": wrap(self.z + step, SIDE) * SIDE + self.x}
        if axis == "x":
            return {"tensor": self.z * SIDE + wrap(self.x + step, SIDE)}
        if axis == "y":
            return {"seq": wrap(self.y + step, SIDE) * 2 + self.core}
        if axis == "core":
            return {"seq": self.y * 2 + (1 - self.core)}
        return {"seq": wrap(self.seq + step, NSEQ)}

    def barrier(self):
        sem = pltpu.get_barrier_semaphore()
        peers = [self.along(axis, k) for axis in "zx" for k in range(1, SIDE)]
        peers += [self.along("seq", k) for k in range(1, NSEQ)]
        for peer in peers:
            pl.semaphore_signal(sem, inc=1, device_id=peer, device_id_type=MESH)
        pl.semaphore_wait(sem, len(peers))


class Plan:
    def __init__(self, send, recv, local):
        self.send, self.recv, self.local = send, recv, local
        self.actions, self.copies, self.landed, self.left = {}, {}, set(), set()
        self.messages = self.locals = 0

    def message(self, name, src, dst, peer, land, after=()):
        self.actions[name] = ("message", (src, dst, peer, land, self.messages), after, ())
        self.messages += 1

    def step(self, name, work, after=(), sent=()):
        self.actions[name] = ("step", work, after, sent)

    def load(self, name, src, dst):
        self.actions[name] = ("load", (src, dst, self.locals), (), ())
        self.locals += 1

    def need(self, name):
        if name in self.landed:
            return
        kind, data, _, _ = self.actions[name]
        assert name in self.copies, name
        if kind == "message":
            land = data[3]
            pltpu.make_async_copy(land, land, self.recv.at[data[4]]).wait()
        else:
            self.copies[name].wait()
        self.landed.add(name)

    def leave(self, name):
        if name not in self.left:
            self.copies[name].wait_send()
            self.left.add(name)

    def run(self, name):
        kind, data, after, sent = self.actions[name]
        for other in after:
            self.need(other)
        for other in sent:
            self.leave(other)
        if kind == "message":
            src, dst, peer, _, number = data
            copy = pltpu.make_async_remote_copy(
                src_ref=src,
                dst_ref=dst,
                send_sem=self.send.at[number],
                recv_sem=self.recv.at[number],
                device_id=peer,
                device_id_type=MESH,
            )
            copy.start()
            self.copies[name] = copy
        elif kind == "load":
            src, dst, number = data
            copy = pltpu.make_async_copy(src, dst, self.local.at[number])
            copy.start()
            self.copies[name] = copy
        else:
            data()
            self.landed.add(name)

    def finish(self):
        for name, (kind, _, _, _) in self.actions.items():
            if kind != "step":
                self.need(name)
            if kind == "message":
                self.leave(name)


def signs():
    return (("+", 1), ("-", -1))


def add_gather(plan, g, n, cut, ring, own, buf):
    rows = buf.shape[2]
    i, j = g.at(cut), g.at(ring)

    def slot(dj, di):
        return buf.at[wrap(j + dj, SIDE), wrap(i + di, SIDE)]

    def quarter(di):
        return own.at[pl.ds(pl.multiple_of(wrap(i + di, SIDE) * rows, rows), rows)]

    plan.load((n, "l"), quarter(0), slot(0, 0))
    for k in (1, 3, 2):
        plan.message((n, "x", k), quarter(k), slot(0, 0), g.along(cut, k), slot(0, SIDE - k))
    for d in OFFSETS:
        src, after = (slot(0, d), ((n, "x", SIDE - d),)) if d else (quarter(0), ())
        for sign, step in signs():
            plan.message(
                (n, "s", d, sign), src, slot(0, d), g.along(ring, step), slot(-step + SIDE, d), after
            )
    for d in OFFSETS:
        sign, step = ("+", 1) if d in (0, 1) else ("-", -1)
        block = slot(SIDE - step, d)
        plan.message((n, "f", d), block, block, g.along(ring, step), slot(2, d), ((n, "s", d, sign),))
    names = [(n, "l")] + [(n, "x", k) for k in (1, 2, 3)] + [(n, "f", d) for d in OFFSETS]
    return names + [(n, "s", d, sign) for d in OFFSETS for sign in "+-"]


def add_weight(plan, g, n, cut, own, full, wide):
    i = g.at(cut)
    needs = {e: [] for e in OFFSETS}
    plan.load((n, "l"), own, full.at[i])
    needs[0].append((n, "l"))

    def cutout(ref, start, size):
        rows = pl.ds(pl.multiple_of(start, 128), size)
        return ref.at[:, rows] if wide else ref.at[rows]

    def add_piece(p, begin, size, shared):
        half = SIDE * size if shared else size
        other = begin + (1 - g.core) * half
        region = begin + g.core * half

        def chunk(dy):
            return region + wrap(g.y + dy, SIDE) * size if shared else region

        def at(e, start, length=size):
            return cutout(full.at[wrap(i + e, SIDE)], start, length)

        def ends(sign):
            return 0 if sign == "+" else size // 2

        here = chunk(0)
        for sign, step in signs():
            plan.message(
                (p, "n", sign), cutout(own, here, size), at(0, here), g.along(cut, step),
                at(SIDE - step, here),
            )
        for sign, step in signs():
            part = at(SIDE - step, here + ends(sign), size // 2)
            plan.message(
                (p, "h", sign), part, part, g.along(cut, step), at(2, here + ends(sign), size // 2),
                ((p, "n", sign),),
            )
        have = {3: [(p, "n", "+")], 1: [(p, "n", "-")], 2: [(p, "h", "+"), (p, "h", "-")]}
        if shared:
            for e in (3, 1, 2):
                for sign, step in signs():
                    plan.message(
                        (p, "y", e, sign), at(e, here), at(e, here), g.along("y", step),
                        at(e, chunk(SIDE - step)), tuple(have[e]),
                    )
            for e, sign, step, length in ((3, "+", 1, size), (1, "-", -1, size), (2, "+", 1, size // 2), (2, "-", -1, size // 2)):
                off = ends(sign) if e == 2 else 0
                part = at(e, chunk(SIDE - step) + off, length)
                plan.message(
                    (p, "z", e, sign), part, part, g.along("y", step), at(e, chunk(2) + off, length),
                    ((p, "y", e, sign),),
                )
            for e, last in ((3, "+"), (1, "-"), (2, "+-")):
                have[e] += [(p, "y", e, "+"), (p, "y", e, "-")] + [(p, "z", e, sign) for sign in last]
        for e in (3, 1, 2):
            block = at(e, region, half)
            plan.message(
                (p, "c", e), block, block, g.along("core", 1), at(e, other, half), tuple(have[e])
            )
            needs[e] += have[e] + [(p, "c", e)]

    begin = 0
    for count, size in enumerate(SHARES[n]):
        add_piece((n, count), begin, size, True)
        begin += 2 * SIDE * size
    while begin < NT * W:
        add_piece((n, begin // (2 * ALONE) + 8), begin, ALONE, False)
        begin += 2 * ALONE
    return needs


def lanes(blocks):
    return jnp.concatenate(blocks, 1)


def add_project(plan, g, n, cut, ring, buf, have, full, needs, wide, dst, sender):
    i = g.at(cut)

    def columns(e):
        at = wrap(i + e, SIDE)
        total = None
        for m in range(SIDE):
            if ring == "z":
                left = lanes([buf[m, k] for k in range(SIDE)])
            else:
                left = lanes([buf[k, m] for k in range(SIDE)])
            depth = pl.ds(m * SIDE * W, SIDE * W)
            if wide:
                term = lax.dot_general(left, full[at, :, depth], NT_DIMS, preferred_element_type=F32)
            else:
                term = jnp.dot(left, full[at, depth, :], preferred_element_type=F32)
            total = term if total is None else total + term
        return total.astype(BF16)

    def make(e):
        def work():
            if e:
                sender[e] = columns(e).reshape(sender.shape[1:])
            else:
                dst(i)[...] = columns(e).reshape(sender.shape[1:])

        return work

    for e in OFFSETS:
        plan.step((n, "p", e), make(e), tuple(have + needs[e]))
        if e:
            plan.message(
                (n, "o", e), sender.at[e], dst(i), g.along(cut, e), dst(wrap(i - e, SIDE)),
                ((n, "p", e),),
            )
    return [(n, "p", 0)] + [(n, "o", e) for e in (1, 2, 3)]


def add_scatter(plan, g, n, cut, ring, own, own_step, got, parts, one, two, make, out, old=(), final=None):
    i, j = g.at(cut), g.at(ring)

    def keep():
        got[i] = own[i]

    plan.step((n, "k"), keep, (own_step,))
    for k in (1, 3, 2):
        peer = wrap(i + k, SIDE)
        plan.message(
            (n, "x", k), own.at[peer], got.at[i], g.along(cut, k), got.at[wrap(i - k, SIDE)],
            (own_step,),
        )
    swapped = ((n, "k"), (n, "x", 1), (n, "x", 2), (n, "x", 3))

    def part(dj, where=None):
        block = parts.at[wrap(j + dj, SIDE)]
        return block if where is None else block.at[pl.ds(2 * where, 2)]

    def fill(dj):
        def work():
            row = wrap(j + dj, SIDE)

            @pl.loop(0, SIDE)
            def _(k):
                t = row * SIDE + k if ring == "z" else k * SIDE + row
                parts[row, k] = make(t).astype(BF16)

        return work

    def add(ref, *others):
        total = ref[...].astype(F32)
        for other in others:
            total = total + other[...].astype(F32)
        ref[...] = total.astype(BF16)

    for dj in (2, 1, 3, 0):
        plan.step((n, "f", dj), fill(dj), swapped, old)
    plan.message((n, "n", 0), part(2, 0), one.at[0], g.along(ring, -1), one.at[0], ((n, "f", 2),))
    plan.message((n, "n", 1), part(2, 1), one.at[1], g.along(ring, 1), one.at[1], ((n, "f", 2),))
    plan.step((n, "r", 0), lambda: add(part(3, 0), one.at[0]), ((n, "f", 3), (n, "n", 0)))
    plan.step((n, "r", 1), lambda: add(part(1, 1), one.at[1]), ((n, "f", 1), (n, "n", 1)))
    for where in range(2):
        half = pl.ds(2 * where, 2)
        up, down = two.at[0, half], two.at[1, half]
        plan.message(
            (n, "u", where), part(1, where), up, g.along(ring, 1), up, ((n, "r", 1) if where else (n, "f", 1),)
        )
        plan.message(
            (n, "d", where), part(3, where), down, g.along(ring, -1), down, ((n, "f", 3) if where else (n, "r", 0),)
        )
        plan.step(
            (n, "t", where),
            functools.partial(add, part(0, where), up, down),
            ((n, "f", 0), (n, "u", where), (n, "d", where)),
        )
    totals = ((n, "t", 0), (n, "t", 1))
    ready = parts.at[j]
    if final is not None:
        ready = final

        def turn():
            for k in range(SIDE):
                final[k] = parts[j, k].astype(F32).T.astype(BF16).reshape(final.shape[1:])

        plan.step((n, "v"), turn, totals)
        totals = ((n, "v"),)
    for k in (1, 3, 2):
        plan.message(
            (n, "b", k), ready.at[wrap(i + k, SIDE)], out(i), g.along(cut, k),
            out(wrap(i - k, SIDE)), totals,
        )

    def own_rows():
        out(i)[...] = ready[i]

    plan.step((n, "b", 0), own_rows, totals)


def register(
    plan, g,
    enc_ref, hid_ref, gout_ref, wq_ref, wk_ref, wv_ref, wo_ref, rows_ref, slot_ref,
    out_ref, gh_ref, ge_ref,
    enc_all, hid_all, gout_all, wq, wk, wv, wo, kv_send, q_send, ga_send, own_k, own_v, stage_k, stage_v,
    k_in, v_in, q_ext, ga_ext, q_span, ga_span, probs, att, gq, tok_a, tok_c, got_a, got_c, reads,
    slot_out, slot_in, gkv, gkv_t, gkv_got, parts_c, parts_enc, one_a, two_a, one_c, two_c, one_enc, two_enc,
    final_c, final_enc, chain,
):
    scale = HEAD_DIM ** (-0.5)
    all_weights = {}
    for n, cut, own, full in (("K", "x", wk_ref, wk), ("V", "x", wv_ref, wv), ("Q", "z", wq_ref, wq), ("O", "z", wo_ref, wo)):
        all_weights[n] = add_weight(plan, g, n, cut, own, full, n == "O")
    enc = add_gather(plan, g, "E", "x", "z", enc_ref, enc_all)
    hid = add_gather(plan, g, "H", "z", "x", hid_ref, hid_all)
    gout = add_gather(plan, g, "G", "z", "x", gout_ref, gout_all)

    per = EQ // RLEN
    for n, full, own, stage, sender, land in (
        ("K", wk, own_k, stage_k, kv_send.at[0], k_in), ("V", wv, own_v, stage_v, kv_send.at[1], v_in)
    ):
        def rows(i, own=own):
            return own.at[pl.ds(i * per, per)]

        made = add_project(
            plan, g, n, "x", "z", enc_all, enc, full, all_weights[n], False, rows, sender
        )

        def pick(own=own, stage=stage, land=land):
            @pl.loop(0, NSEQ)
            def _(r):
                for s in range(2):
                    stage[r, s] = own[jnp.maximum(rows_ref[0, 2 * r + s], 0)]

            land[g.seq] = stage[g.seq]

        plan.step((n, "x"), pick, tuple(made))
        for k in range(1, NSEQ):
            plan.message(
                (n, "a", k), stage.at[wrap(g.seq + k, NSEQ)], land.at[g.seq], g.along("seq", k),
                land.at[wrap(g.seq - k, NSEQ)], ((n, "x"),),
            )

    head, tail = pl.ds(0, SPAN), pl.ds(ROWS, SPAN)
    row = col = None

    def shift_rows(by, limit=None):
        row = lax.broadcasted_iota(jnp.int32, (Q, Q + SPAN), 0)
        col = lax.broadcasted_iota(jnp.int32, (Q, Q + SPAN), 1)
        picked = col == row + by
        if limit is not None:
            picked = jnp.logical_and(picked, col < limit)
        return picked.astype(BF16)

    for n, buf, have, full, ext, span, sender in (
        ("Q", hid_all, hid, wq, q_ext, q_span, q_send), ("O", gout_all, gout, wo, ga_ext, ga_span, ga_send)
    ):
        def rows(i, ext=ext):
            return ext.at[pl.ds(pl.multiple_of(i * Q, Q), Q)]

        made = add_project(
            plan, g, n, "z", "x", buf, have, full, all_weights[n], n == "O", rows, sender
        )
        plan.message(
            (n, "e"), ext.at[head], ext.at[tail], g.along("seq", NSEQ - 1), ext.at[tail], tuple(made)
        )

        def align(ext=ext, span=span):
            for m in range(SIDE):
                limit = None
                if m == SIDE - 1:
                    limit = jnp.where(g.seq == NSEQ - 1, Q, Q + SPAN)
                moved = jnp.dot(
                    shift_rows(SPAN - 1, limit), ext[m * Q : (m + 1) * Q + SPAN, :],
                    preferred_element_type=F32,
                )
                span[m * Q : (m + 1) * Q, :] = moved.astype(BF16)

        plan.step((n, "t"), align, tuple(made) + ((n, "e"),))

    def tables():
        for kind in range(2):
            reads[kind, NONE] = jnp.zeros((RLEN, HEAD_DIM), F32)
        ids = [slot_ref[p % NEIGH, p // NEIGH] for p in range(NONE)]
        targets = [rows_ref[0, j] for j in range(NONE)]
        for line, values in ((0, ids), (2, targets)):
            for p in range(NONE):
                before, latest = jnp.int32(NONE), jnp.int32(NONE)
                for q in range(NONE):
                    if q < p:
                        before = jnp.where(values[q] == values[p], q, before)
                    latest = jnp.where(values[q] == p, q, latest)
                chain[line, p] = before
                chain[line + 1, p] = latest

    plan.step(("T", "t"), tables)

    def read(ref, u, cols):
        picked = []
        for j in range(NEIGH):
            s = slot_ref[j, u]
            picked.append(ref[lax.div(s, 2), lax.rem(s, 2), :, cols])
        return jnp.concatenate(picked, 0)

    def forward(h):
        cols = slice(h * HEAD_DIM, (h + 1) * HEAD_DIM)

        def work():
            @pl.loop(0, SPANS, unroll=UNROLL)
            def _(u):
                here = pl.ds(pl.multiple_of(u * SPAN, SPAN), SPAN)
                k, v = read(k_in, u, cols), read(v_in, u, cols)
                scores = lax.dot_general(
                    q_span[here, cols], k, NT_DIMS, preferred_element_type=F32
                ) * scale
                peak = jnp.max(scores, axis=-1, keepdims=True)
                weights = jnp.exp(scores - peak)
                prob = weights / jnp.sum(weights, axis=-1, keepdims=True)
                probs[h, u] = prob
                context = jnp.dot(prob.astype(BF16), v, preferred_element_type=F32)
                att[pl.ds(pl.multiple_of(u * SPAN, SPAN) + SPAN, SPAN), cols] = context.astype(BF16)

        return work

    def backward(h):
        cols = slice(h * HEAD_DIM, (h + 1) * HEAD_DIM)

        def work():
            @pl.loop(0, SPANS, unroll=UNROLL)
            def _(u):
                here = pl.ds(pl.multiple_of(u * SPAN, SPAN), SPAN)
                k, v = read(k_in, u, cols), read(v_in, u, cols)
                prob = probs[h, u]
                q, gr = q_span[here, cols], ga_span[here, cols]
                grad_probs = lax.dot_general(gr, v, NT_DIMS, preferred_element_type=F32)
                dot_sum = jnp.sum(grad_probs * prob, axis=-1, keepdims=True)
                grad_scores = (prob * (grad_probs - dot_sum) * scale).astype(BF16)
                grad_q = jnp.dot(grad_scores, k, preferred_element_type=F32)
                gq[pl.ds(pl.multiple_of(u * SPAN, SPAN) + SPAN, SPAN), cols] = grad_q.astype(BF16)
                grad_k = lax.dot_general(grad_scores, q, TN_DIMS, preferred_element_type=F32)
                grad_v = lax.dot_general(
                    prob.astype(BF16), gr, TN_DIMS, preferred_element_type=F32
                )
                for j in range(NEIGH):
                    part = slice(j * RLEN, (j + 1) * RLEN)
                    p = NEIGH * u + j
                    before = chain[0, p]
                    reads[0, p] = grad_k[part] + reads[0, before]
                    reads[1, p] = grad_v[part] + reads[1, before]

            @pl.loop(0, SLOTS)
            def _(s):
                latest = chain[1, s]
                for r in range(2):
                    for kind in range(2):
                        slot_out[h, r, lax.div(s, 2), lax.rem(s, 2), kind] = reads[
                            kind, latest, r * HALF : (r + 1) * HALF, :
                        ].astype(BF16)

            for r in range(2):
                slot_in[h, r, g.seq] = slot_out[h, r, g.seq]

        return work

    landed = tuple((n, "a", k) for n in "KV" for k in range(1, NSEQ)) + (("K", "x"), ("V", "x"))
    for h in range(HEADS):
        plan.step(("F", h), forward(h), landed + (("Q", "t"),))
    for h in range(HEADS):
        plan.step(("B", h), backward(h), (("F", h), ("O", "t"), ("T", "t")))
        for r in range(2):
            for k in range(1, NSEQ):
                plan.message(
                    ("S", h, r, "a", k), slot_out.at[h, r, wrap(g.seq + k, NSEQ)], slot_in.at[h, r, g.seq],
                    g.along("seq", k), slot_in.at[h, r, wrap(g.seq - k, NSEQ)], (("B", h),),
                )

    last = pl.ds(ROWS, SPAN)

    def out_part(t):
        depth = pl.ds(pl.multiple_of(t * W, W), W)
        return sum(
            jnp.dot(got_a[k], wo[k, :, depth], preferred_element_type=F32) for k in range(SIDE)
        )

    def hidden_part(t):
        depth = pl.ds(pl.multiple_of(t * W, W), W)
        return sum(
            jnp.dot(wq[k, depth, :], got_c[k], preferred_element_type=F32)
            for k in range(SIDE)
        )

    gone = [("H", "f", d) for d in OFFSETS]
    gone += [("H", "s", d, sign) for d in (1, 2, 3) for sign in "+-"]
    for n, src, made, make, tok, got, parts, one, two, result, old, final in (
        ("A", att, (("F", 0), ("F", 1)), out_part, tok_a, got_a, hid_all, one_a, two_a, out_ref, tuple(gone), None),
        ("C", gq, (("B", 0), ("B", 1)), hidden_part, tok_c, got_c, parts_c, one_c, two_c, gh_ref, (), final_c),
    ):
        plan.message((n, "e"), src.at[last], src.at[head], g.along("seq", 1), src.at[head], made)

        def align(src=src, tok=tok, final=final):
            @pl.when(g.seq == 0)
            def _():
                src[head, :] = jnp.zeros((SPAN, W), BF16)

            for m in range(SIDE):
                moved = jnp.dot(
                    shift_rows(1), src[m * Q : (m + 1) * Q + SPAN, :], preferred_element_type=F32
                )
                tok[m] = (moved if final is None else moved.T).astype(BF16)

        plan.step((n, "t"), align, made + ((n, "e"),))

        def rows(i, result=result):
            return result.at[pl.ds(pl.multiple_of(i * Q, Q), Q)]

        add_scatter(
            plan, g, n, "z", "x", tok, (n, "t"), got, parts, one, two, make, rows, old, final
        )

    def owner_sums(r):
        def work():
            @pl.loop(0, NSEQ)
            def _(o):
                for slot in range(2):
                    p = 2 * o + slot
                    before = chain[2, p]
                    for kind in range(2):
                        for h in range(HEADS):
                            rows = slice(h * HALF, (h + 1) * HALF)
                            value = slot_in[h, r, o, slot, kind].astype(F32)
                            reads[kind, p, rows, :] = value + reads[kind, before, rows, :]

            for n in range(NSEQ):
                latest = chain[3, n]
                for kind in range(2):
                    for h in range(HEADS):
                        rows = slice(h * HALF, (h + 1) * HALF)
                        cols = slice(h * HEAD_DIM, (h + 1) * HEAD_DIM)
                        place = slice((n % per) * HALF, (n % per + 1) * HALF)
                        gkv[n // per, kind, place, cols] = reads[kind, latest, rows, :].astype(BF16)
            for k in range(SIDE):
                for kind in range(2):
                    gkv_t[r, k, kind] = gkv[k, kind].astype(F32).T.astype(BF16)

        return work

    def enc_part(r):
        def make(t):
            depth = pl.ds(pl.multiple_of(t * W, W), W)
            total = None
            for kind, w in ((0, wk), (1, wv)):
                for k in range(SIDE):
                    term = jnp.dot(
                        w[k, depth, :], gkv_got[r, k, kind], preferred_element_type=F32
                    )
                    total = term if total is None else total + term
            return total

        return make

    for r in range(2):
        came = tuple(("S", h, r, "a", k) for h in range(HEADS) for k in range(1, NSEQ))
        plan.step(("W", r), owner_sums(r), came + (("B", 0), ("B", 1)))

        def rows(i, r=r):
            return ge_ref.at[pl.ds(i * per, per), pl.ds(r * HALF, HALF)]

        add_scatter(
            plan, g, ("Y", r), "x", "z", gkv_t.at[r], ("W", r), gkv_got.at[r], parts_enc.at[r],
            one_enc.at[r], two_enc.at[r], enc_part(r), rows, (), final_enc.at[r],
        )


def kernel(*refs):
    *refs, send, recv, local = refs
    g = Grid()
    plan = Plan(send, recv, local)
    register(plan, g, *refs)
    names = list(plan.actions)
    assert sorted(ORDER) == list(range(len(names)))
    g.barrier()
    for number in ORDER:
        plan.run(names[number])
    plan.finish()


def scratch():
    def vmem(*dims, dtype=BF16):
        return pltpu.VMEM(dims, dtype)

    weight = vmem(SIDE, NT * W, W)
    quarters = vmem(SIDE, Q, W)
    return [
        vmem(SIDE, SIDE, EQ, W), vmem(SIDE, SIDE, Q, W), vmem(SIDE, SIDE, Q, W),
        weight, weight, weight, vmem(SIDE, W, NT * W),
        vmem(2, SIDE, EQ // RLEN, RLEN, W), quarters, quarters,
        vmem(NSEQ, RLEN, W), vmem(NSEQ, RLEN, W),
        vmem(NSEQ, 2, RLEN, W), vmem(NSEQ, 2, RLEN, W), vmem(NSEQ, 2, RLEN, W), vmem(NSEQ, 2, RLEN, W),
        vmem(ROWS + SPAN, W), vmem(ROWS + SPAN, W), vmem(ROWS, W), vmem(ROWS, W),
        vmem(HEADS, SPANS, SPAN, NEIGH * RLEN, dtype=F32),
        vmem(ROWS + SPAN, W), vmem(ROWS + SPAN, W),
        quarters, vmem(SIDE, W, Q), quarters, vmem(SIDE, W, Q),
        vmem(2, NONE + 1, RLEN, HEAD_DIM, dtype=F32),
        vmem(HEADS, 2, NSEQ, 2, 2, HALF, HEAD_DIM), vmem(HEADS, 2, NSEQ, 2, 2, HALF, HEAD_DIM),
        vmem(SIDE, 2, Q, W), vmem(2, SIDE, 2, W, Q), vmem(2, SIDE, 2, W, Q),
        vmem(SIDE, SIDE, W, Q), vmem(2, SIDE, SIDE, W, Q),
        vmem(2, 2, Q, W), vmem(2, SIDE, Q, W), vmem(2, 2, W, Q), vmem(2, SIDE, W, Q),
        vmem(2, 2, 2, W, Q), vmem(2, 2, SIDE, W, Q),
        quarters, vmem(2, SIDE, 2, HALF, W), pltpu.SMEM((4, NONE), jnp.int32),
    ]


def shape(*dims, dtype=BF16):
    return jax.ShapeDtypeStruct(dims, dtype)


def hand_over(*refs):
    for src, dst in zip(refs[:3], refs[3:]):
        dst[...] = src[...]


def per_device(hidden, encoded, w_query, w_key, w_value, w_out, send_rows, read_slot, grad_out):
    dma = pltpu.SemaphoreType.DMA
    shapes = (shape(ROWS, W), shape(ROWS, W), shape(NSEQ, RLEN, W))
    results = pl.pallas_call(
        kernel,
        name="cross_attention",
        out_shape=shapes,
        in_specs=[ANY] * 7 + [SM, SM],
        out_specs=(VM, VM, VM),
        scratch_shapes=scratch() + [dma((MESSAGES,)), dma((MESSAGES,)), dma((7,))],
        compiler_params=pltpu.CompilerParams(
            collective_id=0, has_side_effects=True, vmem_limit_bytes=63 * 1024 * 1024
        ),
    )(
        encoded.reshape(2 * ROWS, W), hidden, grad_out, w_query, w_key, w_value, w_out, send_rows, read_slot.T,
    )
    return pl.pallas_call(
        hand_over,
        name="hand_over",
        out_shape=shapes,
        in_specs=[VM] * 3,
        out_specs=(VM,) * 3,
    )(*results)


def solution(mesh):
    placed = (
        P("seq", "tensor"),
        P("seq", None, "tensor"),
        P(None, "tensor"),
        P(None, "tensor"),
        P(None, "tensor"),
        P("tensor", None),
        P("seq", None),
        P("seq", None),
        P("seq", "tensor"),
    )
    return jax.shard_map(
        per_device,
        mesh=mesh,
        in_specs=placed,
        out_specs=(P("seq", "tensor"), P("seq", "tensor"), P("seq", None, "tensor")),
        check_vma=False,
    )
```
